128 devices in a mesh: rows: 8 (over y, core), cols: 16 (over x, z).
Axes of the slice: x: 4, y: 4, z: 4, core: 2. Of those that a mesh axis runs over, the one named last changes fastest.
Arguments:
- position: float32 [2048, 3, 256], P(('rows', 'cols')), may hold values from 0 to 1
- velocity: float32 [2048, 3, 256], P(('rows', 'cols')), may hold values from -1.8 to 1.8
- mass: float32 [2048, 256], P(('rows', 'cols')), may hold values from 0.00025 to 0.001
- smoothing: float32 [2048, 256], P(('rows', 'cols')), may hold values from 0.1 to 0.25
- energy: float32 [2048, 256], P(('rows', 'cols')), may hold values from 0.05 to 0.5
- counts: int32 [2048], P(('rows', 'cols')), may hold values from 96 to 256
- proxy_cell: int32 [16384], P(('rows', 'cols')), may hold values from 0 to 15
- proxy_dest: int32 [16384, 1], P(('rows', 'cols')), may hold values from 0 to 127; in each aligned block of 128 rows (0 to 127, 128 to 255, ...) at most 2 rows name the same one
- proxy_target: int32 [16384], P(('rows', 'cols')), may hold values from 0 to 15
- pair_first: int32 [2048], P(('rows', 'cols')), may hold values from 0 to 15
- pair_offset: int32 [2048], P(('rows', 'cols')), may hold values from 1 to 15
- mig_cell: int32 [2048], P(('rows', 'cols')), may hold values from 0 to 15
- mig_dest: int32 [2048, 1], P(('rows', 'cols')), may hold values from 0 to 15; in each aligned block of 16 rows (0 to 15, 16 to 31, ...) at most 2 rows name the same one
Outputs:
- density: float32 [2048, 256], P(('rows', 'cols'))
- accel: float32 [2048, 4, 256], P(('rows', 'cols'))
- arrived: float32 [4096, 9, 256], P(('rows', 'cols'))
The draws below stay inside these ranges and needn't reach their ends.
Inputs may be any that keep to these rules, and one draw needn't show every extreme that they name: `proxy_dest`: among the 128 entries of one domain no destination appears more than 2 times; in every draw some domain names some destination exactly 2 times. `mig_dest`: among the 16 entries of one domain no column appears more than 2 times; in every draw some domain names some column exactly 2 times.
All inputs are finite; a program needn't handle non-finite values.
Results may differ from the reference program's by a relative error of at most 0.0003.
Values sent between devices are 32-bit elements; how exact they have to be, the bound alone decides.
No kernel may reach another device: no remote copies, remote signals or barrier semaphores. Data moves between devices by JAX's collectives and lax.ppermute only.
A program may use at most 64 MiB of HBM per device.

```python
import math
import jax
import jax.numpy as jnp
import numpy as np
from jax import lax

P_SIZE = 256
CELLS_DEV = 16
LOCAL_PAIRS = 16
CAP = 2
CAPM = 2
SEND_DEV = 128
MIG_DEV = 16
TOTAL_CELLS = 2048
N_COLS = 16
DEVICES = 128


def touch_ends(drawn, own_key, smallest, high):
    longest = drawn.shape.index(max(drawn.shape))
    spots = []
    for shift in (0, 1):
        where = [jax.random.randint(jax.random.fold_in(own_key, axis), (), 0, length) for axis, length in enumerate(drawn.shape)]
        where[longest] = (where[longest] + shift) % drawn.shape[longest]
        spots.append(tuple(where))
    return drawn.at[spots[0]].set(smallest).at[spots[1]].set(high)


def block_scale(own_key, dims, split, smallest, high):
    factor_of, own = 1.0, jax.random.fold_in(own_key, 6)
    for dim, shards_of in split:
        steps = jnp.exp(jax.random.uniform(jax.random.fold_in(own, dim), (shards_of,), jnp.float32, smallest / len(split), high / len(split)))
        factor_of = factor_of * jnp.repeat(steps, dims[dim] // shards_of).reshape([-1 if axis == dim else 1 for axis in range(len(dims))])
    return factor_of


def assign_block(key, own, number, rows, amount, top, reach, skew):
    ranking = jax.random.permutation(key, amount)
    packed, common = portions_of(amount, rows * top, reach, skew, True), portions_of(amount, rows * top, reach, skew, False)
    places = jnp.arange(amount)

    def named(lengths, turn):
        used = int((lengths > 0).sum())
        fixed = max(1, used // 4)
        passed = fixed + (places - fixed + turn * (used - fixed)) % max(1, amount - fixed)
        return jnp.zeros((amount,), jnp.int32).at[ranking[jnp.where(places < fixed, places, passed)]].set(jnp.asarray(lengths, jnp.int32))

    lengths = jnp.where(number % 4 == 0, named(packed, number // 4), named(common, number - number // 4 - 1))
    mixed = jax.random.permutation(jax.random.fold_in(own, 3), amount)
    giver, taker = mixed[0:amount // 2 * 2:2], mixed[1:amount // 2 * 2:2]
    room = jnp.minimum(lengths[giver] - 1, reach - lengths[taker]) // 2
    room = jnp.where((giver == ranking[0]) | (taker == ranking[0]) | (lengths[taker] == 0), 0, jnp.maximum(room, 0))
    passed = jax.random.randint(jax.random.fold_in(own, 4), (amount // 2,), 0, 1 << 20) % (room + 1)
    lengths = lengths.at[giver].add(-passed).at[taker].add(passed)
    labels = jnp.searchsorted(jnp.cumsum(lengths), jnp.arange(rows * top), side="right").astype(jnp.int32)
    listing = labels.reshape(top, rows).T
    listing = listing[jax.random.permutation(jax.random.fold_in(own, 1), rows)]
    turn = jax.random.randint(jax.random.fold_in(own, 2), (rows, 1), 0, top)
    return jnp.take_along_axis(listing, (jnp.arange(top)[None, :] + turn) % top, axis=1)


def portions_of(count, total, limit, skew, full):
    weights = [(1 << 20) // math.isqrt(grade ** skew) + 1 for grade in range(1, count + 1)]
    largest = limit if full else min(limit, max(-(-total // count), total * weights[0] // sum(weights)))
    least = 1 if total - largest >= count - 1 else 0
    given, surplus = [largest] + [least] * (count - 1), total - largest - least * (count - 1)
    while surplus > 0:
        free = [i for i in range(1, count) if given[i] < largest] or [i for i in range(1, count) if given[i] < limit]
        pool, left = sum([weights[i] for i in free]), surplus
        for i in free:
            addition = min(limit - given[i], max(1, left * weights[i] // pool), surplus)
            given[i] = given[i] + addition
            surplus = surplus - addition
    return np.array(given)


def bell_draw(stream_key, shape, width, bound, shards=(), kind=jnp.bfloat16):
    factor_of = block_scale(stream_key, shape, shards, -0.22, 0.18) if shards else 1.0
    values = jax.random.normal(stream_key, shape, jnp.float32) * width * factor_of
    return jnp.minimum(jnp.maximum(values, -bound), bound).astype(kind)


def setup_inputs(seed: int = 0) -> dict:
    key_of = jax.random.split(jax.random.key(seed), 14)
    position = jnp.clip(1.0 * jax.random.uniform(key_of[0], (TOTAL_CELLS, 3, P_SIZE), jnp.float32) ** block_scale(key_of[0], (TOTAL_CELLS, 3, P_SIZE), ((0, 128),), -0.2, 0.2), 0.0, 1.0)
    velocity = bell_draw(key_of[1], (TOTAL_CELLS, 3, P_SIZE), 0.3, 1.8, ((0, 128),), jnp.float32)
    mass = jnp.clip(jnp.exp(math.log(0.001) - 1.3862944 * jax.random.uniform(key_of[2], (TOTAL_CELLS, P_SIZE), jnp.float32) ** block_scale(key_of[2], (TOTAL_CELLS, P_SIZE), ((0, 128),), -0.2, 0.2)), 0.00025, 0.001)
    smoothing = jnp.clip(jnp.exp(math.log(0.25) - 0.9162907 * jax.random.uniform(key_of[3], (TOTAL_CELLS, P_SIZE), jnp.float32) ** block_scale(key_of[3], (TOTAL_CELLS, P_SIZE), ((0, 128),), -0.2, 0.2)), 0.1, 0.25)
    energy = jnp.clip(jnp.exp(math.log(0.5) - 2.3025851 * jax.random.uniform(key_of[4], (TOTAL_CELLS, P_SIZE), jnp.float32) ** block_scale(key_of[4], (TOTAL_CELLS, P_SIZE), ((0, 128),), -0.2, 0.2)), 0.05, 0.5)
    counts = touch_ends(jax.random.randint(key_of[5], (TOTAL_CELLS,), 3 * P_SIZE // 8, P_SIZE + 1), jax.random.fold_in(key_of[5], 1), 3 * P_SIZE // 8, P_SIZE).astype(jnp.int32)
    proxy_cell = touch_ends(jax.random.randint(key_of[6], (DEVICES * SEND_DEV,), 0, CELLS_DEV), jax.random.fold_in(key_of[6], 1), 0, CELLS_DEV - 1).astype(jnp.int32)
    proxy_dest_keys = jax.random.split(jax.random.fold_in(key_of[7], 1), (DEVICES * SEND_DEV) // SEND_DEV)
    proxy_dest_turns = jax.random.permutation(jax.random.fold_in(key_of[7], 3), (DEVICES * SEND_DEV) // SEND_DEV)
    proxy_dest = jax.vmap(lambda own, number: assign_block(jax.random.fold_in(key_of[7], 2), own, number, SEND_DEV, DEVICES, 1, CAP, 2))(proxy_dest_keys, proxy_dest_turns).reshape((DEVICES * SEND_DEV, 1))
    proxy_target = touch_ends(jax.random.randint(key_of[8], (DEVICES * SEND_DEV,), 0, CELLS_DEV), jax.random.fold_in(key_of[8], 1), 0, CELLS_DEV - 1).astype(jnp.int32)
    pair_first = touch_ends(jax.random.randint(key_of[9], (DEVICES * LOCAL_PAIRS,), 0, CELLS_DEV), jax.random.fold_in(key_of[9], 1), 0, CELLS_DEV - 1).astype(jnp.int32)
    pair_offset = touch_ends(jax.random.randint(key_of[10], (DEVICES * LOCAL_PAIRS,), 1, CELLS_DEV), jax.random.fold_in(key_of[10], 1), 1, CELLS_DEV - 1).astype(jnp.int32)
    mig_cell = touch_ends(jax.random.randint(key_of[11], (DEVICES * MIG_DEV,), 0, CELLS_DEV), jax.random.fold_in(key_of[11], 1), 0, CELLS_DEV - 1).astype(jnp.int32)
    mig_dest_keys = jax.random.split(jax.random.fold_in(key_of[12], 1), (DEVICES * MIG_DEV) // MIG_DEV)
    mig_dest_turns = jax.random.permutation(jax.random.fold_in(key_of[12], 3), (DEVICES * MIG_DEV) // MIG_DEV)
    mig_dest = jax.vmap(lambda own, number: assign_block(jax.random.fold_in(key_of[12], 2), own, number, MIG_DEV, N_COLS, 1, CAPM, 1))(mig_dest_keys, mig_dest_turns).reshape((DEVICES * MIG_DEV, 1))
    return dict(position=position, velocity=velocity, mass=mass, smoothing=smoothing, energy=energy, counts=counts, proxy_cell=proxy_cell, proxy_dest=proxy_dest, proxy_target=proxy_target, pair_first=pair_first, pair_offset=pair_offset, mig_cell=mig_cell, mig_dest=mig_dest)


SIGMA = 0.3183098861837907
GAMMA = 5.0 / 3.0
ALPHA = 1.0
BETA = 2.0
STEP = 0.02
pair_block = 16

def spline(ratio):
    inner = 1.0 - 1.5 * ratio * ratio + 0.75 * ratio * ratio * ratio
    far = jnp.maximum(2.0 - ratio, 0.0)
    return jnp.where(ratio < 1.0, inner, 0.25 * far * far * far)

def slope(ratio):
    inner = -3.0 + 2.25 * ratio
    far = jnp.maximum(2.0 - ratio, 0.0)
    return jnp.where(ratio < 1.0, inner, -0.75 * far * far / jnp.maximum(ratio, 1.0))

def geometry(first, second):
    offsets = first[0:3, :, None] - second[0:3, None, :]
    dist_sq = lax.optimization_barrier(jnp.sum(offsets * offsets, axis=0))
    pair_h = 0.5 * (first[7][:, None] + second[7][None, :])
    ratio = jnp.sqrt(dist_sq) / pair_h
    return (offsets, dist_sq, pair_h, ratio)

def density_pair(first, second, rho_first, rho_second):
    offsets, dist_sq, pair_h, ratio = geometry(first, second)
    kernel_val = SIGMA * spline(ratio) / (pair_h * pair_h * pair_h)
    return (lax.optimization_barrier(jnp.sum(kernel_val * second[6][None, :], axis=1)), lax.optimization_barrier(jnp.sum(kernel_val * first[6][:, None], axis=0)))

def force_pair(first, second, rho_first, rho_second):
    offsets, dist_sq, pair_h, ratio = geometry(first, second)
    press_first = (GAMMA - 1.0) * first[8] / rho_first
    press_second = (GAMMA - 1.0) * second[8] / rho_second
    sound_first = jnp.sqrt(GAMMA * (GAMMA - 1.0) * first[8])
    sound_second = jnp.sqrt(GAMMA * (GAMMA - 1.0) * second[8])
    relative = first[3:6, :, None] - second[3:6, None, :]
    approach = lax.optimization_barrier(jnp.sum(relative * offsets, axis=0))
    converge = pair_h * approach / (dist_sq + 0.01 * pair_h * pair_h)
    mean_sound = 0.5 * (sound_first[:, None] + sound_second[None, :])
    mean_rho = 0.5 * (rho_first[:, None] + rho_second[None, :])
    viscous = jnp.where(approach < 0.0, (-ALPHA * mean_sound * converge + BETA * converge * converge) / mean_rho, 0.0)
    scaled = (press_first[:, None] + press_second[None, :] + viscous) * SIGMA * slope(ratio) / pair_h ** 5
    weight_first = scaled * second[6][None, :]
    weight_second = scaled * first[6][:, None]
    accel_first = -lax.optimization_barrier(jnp.sum(weight_first[None] * offsets, axis=2))
    accel_second = lax.optimization_barrier(jnp.sum(weight_second[None] * offsets, axis=1))
    heat_first = 0.5 * lax.optimization_barrier(jnp.sum(weight_first * approach, axis=1))
    heat_second = 0.5 * lax.optimization_barrier(jnp.sum(weight_second * approach, axis=0))
    return (jnp.concatenate([accel_first, heat_first[None]], axis=0), jnp.concatenate([accel_second, heat_second[None]], axis=0))

def run_pairs(kernel, cells, rho, first_idx, second_idx):

    def one_block(block):
        left_idx, right_idx = block
        return jax.vmap(kernel)(cells[left_idx], cells[right_idx], rho[left_idx], rho[right_idx])
    result = lax.map(one_block, (first_idx.reshape(-1, pair_block), second_idx.reshape(-1, pair_block)))
    return jax.tree.map(lambda stacked: stacked.reshape((-1,) + stacked.shape[2:]), result)

def reference(position, velocity, mass, smoothing, energy, counts, proxy_cell, proxy_dest, proxy_target, pair_first, pair_offset, mig_cell, mig_dest):
    occupied = jnp.arange(P_SIZE, dtype=jnp.int32)[None, :] < counts[:, None]
    live_mass = jnp.where(occupied, mass, 0.0)
    cells = jnp.concatenate([position, velocity, live_mass[:, None], smoothing[:, None], energy[:, None]], axis=1)
    owner = (jnp.arange(DEVICES * SEND_DEV, dtype=jnp.int32) // SEND_DEV).astype(jnp.int32)
    source = owner * CELLS_DEV + proxy_cell
    target = proxy_dest[:, 0] * CELLS_DEV + proxy_target
    home = (jnp.arange(DEVICES * LOCAL_PAIRS, dtype=jnp.int32) // LOCAL_PAIRS).astype(jnp.int32)
    local_first = home * CELLS_DEV + pair_first
    local_second = home * CELLS_DEV + (pair_first + pair_offset) % CELLS_DEV
    first_all = jnp.concatenate([local_first, source]).astype(jnp.int32)
    second_all = jnp.concatenate([local_second, target]).astype(jnp.int32)
    every_cell = jnp.arange(TOTAL_CELLS, dtype=jnp.int32)
    unit_rho = jnp.ones((TOTAL_CELLS, P_SIZE), jnp.float32)
    self_rho = run_pairs(density_pair, cells, unit_rho, every_cell, every_cell)[0]
    rho_first, rho_second = run_pairs(density_pair, cells, unit_rho, first_all, second_all)
    density_raw = self_rho.at[first_all].add(rho_first).at[second_all].add(rho_second)
    rho = jnp.where(occupied, density_raw, 1.0)
    self_force = run_pairs(force_pair, cells, rho, every_cell, every_cell)[0]
    force_first, force_second = run_pairs(force_pair, cells, rho, first_all, second_all)
    total_force = self_force.at[first_all].add(force_first).at[second_all].add(force_second)
    accel = jnp.where(occupied[:, None, :], total_force, 0.0)
    density = jnp.where(occupied, density_raw, 0.0)
    new_vel = velocity + STEP * accel[:, 0:3]
    new_pos = position + STEP * new_vel
    new_energy = energy + STEP * accel[:, 3]
    kicked = jnp.concatenate([new_pos, new_vel, live_mass[:, None], smoothing[:, None], new_energy[:, None]], axis=1)
    kicked = kicked * occupied[:, None, :].astype(jnp.float32)
    moving = mig_dest[:, 0].reshape(DEVICES, MIG_DEV)
    hits = (moving[:, :, None] == jnp.arange(N_COLS, dtype=jnp.int32)[None, None, :]).astype(jnp.int32)
    earlier = jnp.cumsum(hits, axis=1) - hits
    rank = lax.optimization_barrier(jnp.sum(earlier * hits, axis=2)).reshape(-1)
    sender = (jnp.arange(DEVICES * MIG_DEV, dtype=jnp.int32) // MIG_DEV).astype(jnp.int32)
    new_owner = sender // N_COLS * N_COLS + mig_dest[:, 0]
    inbox_slot = new_owner * (N_COLS * CAPM) + sender % N_COLS * CAPM + rank
    arrived = jnp.zeros((DEVICES * N_COLS * CAPM, 9, P_SIZE), jnp.float32).at[inbox_slot.astype(jnp.int32)].set(kicked[sender * CELLS_DEV + mig_cell])
    return (density, accel, arrived)
```

```python
import jax
import jax.numpy as jnp
from jax import lax
from jax.experimental import pallas as pl
from jax.experimental.pallas import tpu as pltpu
from jax.sharding import PartitionSpec as P

CAP = 2
CAPM = 2
CELLS = 16
SEND = 128
PAIRS = 16
PART = 256

GAMMA = 5.0 / 3.0
STEP = 0.02
PI = 3.141592653589793
W_SCALE = 2.0 / PI
K_SCALE = -24.0 / PI
TINY = 1e-12
CHUNK = 32

f32, bf16, i32 = jnp.float32, jnp.bfloat16, jnp.int32
VMEM = pl.BlockSpec(memory_space=pltpu.VMEM)
SMEM = pl.BlockSpec(memory_space=pltpu.SMEM)
LIMIT = 56 * 2**20


def shape(*dims, dtype=f32):
    return jax.ShapeDtypeStruct(dims, dtype)


def kernel_call(body, out_shape, in_specs, out_specs, scratch=(), flops=0, moved=0):
    return pl.pallas_call(
        body,
        out_shape=out_shape,
        in_specs=in_specs,
        out_specs=out_specs,
        scratch_shapes=list(scratch),
        compiler_params=pltpu.CompilerParams(vmem_limit_bytes=LIMIT),
        cost_estimate=pl.CostEstimate(flops=flops, bytes_accessed=moved, transcendentals=0),
    )


def sublane():
    return lax.broadcasted_iota(i32, (8, PART), 0)


def split3(x):
    a = x.astype(bf16).astype(f32)
    b = (x - a).astype(bf16).astype(f32)
    return a, b, x - a - b


def left_parts(x):
    a, b, c = split3(x)
    return [a, a, b, b, a, c]


def right_parts(x):
    a, b, c = split3(x)
    return [a, b, a, b, c, a]


def stack16(parts):
    return jnp.concatenate(parts, axis=0).astype(bf16)


def basis(rows):
    row = sublane()
    place = jnp.where(row < 3, 2.0 * rows - 1.0, rows)
    first = place[0:3]
    norm = jnp.sum(first * first, axis=0, keepdims=True)
    cross = jnp.sum(first * place[3:6], axis=0, keepdims=True)
    full = jnp.where(row < 6, place, jnp.where(row == 6, cross, 1.0))
    return full, norm, cross


def right_distance(full, norm):
    row = sublane()
    return jnp.where(
        row < 3, full, jnp.where(row == 3, norm, jnp.where(row == 4, 1.0, 0.0))
    )


def left_distance(full, norm):
    row = sublane()
    return jnp.where(
        row < 3, -2.0 * full, jnp.where(row == 3, 1.0, jnp.where(row == 4, norm, 0.0))
    )


def left_approach(full, cross):
    return 4.0 * jnp.concatenate(
        [-full[3:6], -full[0:3], jnp.ones((1, PART), f32), cross], axis=0
    )


def columns(parts):
    fill = 128 - 8 * len(parts)
    return jnp.concatenate(parts + [jnp.zeros((fill, PART), f32)], axis=0).T


def mass_rows(mass):
    a, b, c = split3(mass)
    return jnp.concatenate([a, b, c, jnp.zeros((13, PART), f32)], axis=0).astype(bf16)


def halves(w):
    hi = w.astype(bf16)
    return hi, (w - hi.astype(f32)).astype(bf16)


def request_kernel(pos, vel, mass, smooth, counts, dest, target, state, req, slot, used):
    lane = lax.broadcasted_iota(i32, (1, PART), 1)

    def cell(c, _):
        live = jnp.where(lane < counts[c], mass[pl.ds(c, 1), :], 0.0)
        state[c] = jnp.concatenate([pos[c], vel[c], smooth[pl.ds(c, 1), :], live], axis=0)
        return 0

    lax.fori_loop(0, CELLS, cell, 0)
    req[...] = jnp.full_like(req, -1)

    def clear(d, _):
        used[d] = 0
        return 0

    lax.fori_loop(0, req.shape[0], clear, 0)
    short = lax.broadcasted_iota(i32, (1, 128), 1)

    def entry(e, _):
        d = dest[e]
        k = used[d]
        used[d] = k + 1
        slot[e] = d * CAP + k
        req[d] = jnp.where(short == k, target[e], req[d])
        return 0

    lax.fori_loop(0, SEND, entry, 0)


def respond_kernel(state, goals, out):
    def one(s, _):
        goal = jnp.maximum(goals[s], 0)
        out[s] = state[goal]
        return 0

    lax.fori_loop(0, out.shape[0], one, 0, unroll=4)


def pipeline(count, load, combine, store, work):
    load(0)

    def body(p, _):
        sums = combine(jnp.maximum(p - 1, 0))
        work(p)
        load(jnp.minimum(p + 1, count - 1))
        store(jnp.maximum(p - 1, 0), sums, p > 0)
        return 0

    lax.fori_loop(0, count, body, 0)
    store(count - 1, combine(count - 1), True)


def own_lists(pair_first, pair_offset, pa, po, ps, dummy):
    def one(e, _):
        pa[e] = e
        po[e] = e
        ps[e] = dummy
        a = pair_first[e]
        b = lax.rem(a + pair_offset[e], CELLS)
        pa[CELLS + e] = a
        po[CELLS + e] = b
        ps[CELLS + e] = b
        return 0

    lax.fori_loop(0, CELLS, one, 0)


def nn(a, b):
    return jnp.dot(a, b, preferred_element_type=f32)


def nt(a, b):
    return lax.dot_general(a, b, (((1,), (1,)), ((), ())), preferred_element_type=f32)


def density_weights(r2, total_h):
    inv = pltpu.reciprocal(total_h, approx=True)
    inv2 = inv * inv
    q2 = jnp.maximum(r2, TINY) * inv2
    q = q2 * lax.rsqrt(q2)
    u = 2.0 - q
    t = jnp.maximum(u, 0.0)
    return jnp.minimum(t * t * t, 4.0 - 3.0 * (q2 * u)) * (inv2 * inv)


def density_pairs(count, pa, po, ps, bf, cj, hj, at, bh, dist, ws, acc1, acc2):
    def load(p):
        dist[...] = nn(at[pa[p]], bf[po[p]])

    def work(p):
        a = pa[p]
        h_j = hj[po[p]]
        for c in range(0, PART, CHUNK):
            h_i = bh[a, c : c + CHUNK, :]
            w = density_weights(
                dist[c : c + CHUNK, :], jnp.concatenate([h_i, h_i], axis=1) + h_j
            )
            hi, lo = halves(w)
            ws[c : c + CHUNK, :] = hi
            ws[PART + c : PART + c + CHUNK, :] = lo

    def combine(p):
        own = cj[pa[p]]
        second = nn(jnp.concatenate([own, own], axis=1), ws[...])
        first = nt(cj[po[p]], ws[...])
        return first[0:8, 0:PART] + first[0:8, PART:], second[0:8]

    def store(p, sums, valid):
        if valid is True:
            acc1[pa[p]] += sums[0]
            acc2[ps[p]] += sums[1]
        else:
            keep = jnp.where(valid, 1.0, 0.0)
            acc1[pa[p]] += sums[0] * keep
            acc2[ps[p]] += sums[1] * keep

    ws[...] = jnp.zeros_like(ws)
    pipeline(count, load, combine, store, work)


def density_prepare_own(c, state, bf, cj, hj, at, bh):
    rows = state[c]
    full, norm, _ = basis(rows)
    bf[c] = stack16(right_parts(right_distance(full, norm)))
    cj[c] = mass_rows(rows[7:8])
    hj[c] = rows[6:7]
    t = columns(
        left_parts(left_distance(full, norm)) + [jnp.broadcast_to(rows[6:7], (8, PART))]
    )
    at[c] = t[:, 0:48].astype(bf16)
    bh[c] = jnp.broadcast_to(t[:, 48:49], (PART, 128))


def density_prepare_other(o, rows, bf, cj, hj):
    full, norm, _ = basis(rows)
    bf[o] = stack16(right_parts(right_distance(full, norm)))
    cj[o] = mass_rows(rows[7:8])
    hj[o] = rows[6:7]


def own_density_kernel(
    state, pair_first, pair_offset, total, acc1, acc2, bf, cj, hj, at, bh, dist, ws, pa, po, ps
):
    lax.fori_loop(
        0, CELLS, lambda c, _: density_prepare_own(c, state, bf, cj, hj, at, bh) or 0, 0
    )
    own_lists(pair_first, pair_offset, pa, po, ps, CELLS)
    acc1[...] = jnp.zeros_like(acc1)
    acc2[...] = jnp.zeros_like(acc2)
    density_pairs(CELLS + PAIRS, pa, po, ps, bf, cj, hj, at, bh, dist, ws, acc1, acc2)
    total[...] = acc1[...] + acc2[0:CELLS]


def far_density_kernel(
    state, far, slot, proxy_cell, acc1, ret, acc2, bf, cj, hj, at, bh, dist, ws, pa, po, ps
):
    lax.fori_loop(
        0, CELLS, lambda c, _: density_prepare_own(c, state, bf, cj, hj, at, bh) or 0, 0
    )

    def other(e, _):
        density_prepare_other(CELLS + e, far[slot[e]], bf, cj, hj)
        pa[e] = proxy_cell[e]
        po[e] = CELLS + e
        ps[e] = e
        return 0

    lax.fori_loop(0, SEND, other, 0, unroll=4)
    acc1[...] = jnp.zeros_like(acc1)
    acc2[...] = jnp.zeros_like(acc2)
    density_pairs(SEND, pa, po, ps, bf, cj, hj, at, bh, dist, ws, acc1, acc2)

    def back(e, _):
        ret[slot[e]] = jnp.sum(acc2[e][0:3], axis=0, keepdims=True)
        return 0

    lax.fori_loop(0, SEND, back, 0, unroll=4)


def combine_density_kernel(
    back, goals, near, far, energy, counts, density, fluid, answer, sums
):
    sums[...] = jnp.zeros_like(sums)

    def one(s, _):
        goal = goals[s]
        sums[jnp.where(goal < 0, CELLS, goal)] += back[s]
        return 0

    lax.fori_loop(0, back.shape[0], one, 0, unroll=2)
    lane = lax.broadcasted_iota(i32, (1, PART), 1)

    def cell(c, _):
        both = near[c] + far[c]
        raw = W_SCALE * (jnp.sum(both[0:3], axis=0, keepdims=True) + sums[c])
        here = lane < counts[c]
        density[pl.ds(c, 1), :] = jnp.where(here, raw, 0.0)
        fluid[c] = jnp.concatenate(
            [jnp.where(here, raw, 1.0), energy[pl.ds(c, 1), :]], axis=0
        )
        return 0

    lax.fori_loop(0, CELLS, cell, 0)

    def send(s, _):
        answer[s] = fluid[jnp.maximum(goals[s], 0)]
        return 0

    lax.fori_loop(0, answer.shape[0], send, 0, unroll=4)


def force_weights(r2, s, total_h, total_c, total_p, total_r):
    inv = pltpu.reciprocal(total_h, approx=True)
    inv2 = inv * inv
    q2 = jnp.maximum(r2, TINY) * inv2
    rs = lax.rsqrt(q2)
    q = q2 * rs
    u = 2.0 - q
    t = jnp.maximum(u, 0.0)
    grad = jnp.where(q < 1.0, 3.0 * u - 2.0, t * t * rs)
    m = jnp.minimum(s, 0.0) * (inv * pltpu.reciprocal(q2 + 0.01, approx=True))
    visc = m * (m - total_c) * pltpu.reciprocal(total_r, approx=True)
    return (total_p + visc) * (grad * (inv2 * inv2 * inv))


def force_fluid(fluid):
    rho, u = fluid[0:1], fluid[1:2]
    pressure = (GAMMA - 1.0) * u / rho
    sound = jnp.sqrt(GAMMA * (GAMMA - 1.0) * u)
    return pressure, sound, 4.0 * rho


def force_pairs(count, pa, po, ps, refs, acc1, acc2):
    bd, bs, cf, ad, as_, row, col, dist, appr, ws = refs

    def load(p):
        a, o = pa[p], po[p]
        dist[...] = nn(ad[a], bd[o])
        appr[...] = nn(as_[a], bs[o])

    def work(p):
        a, o = pa[p], po[p]
        side = row[o]

        def total(k, c):
            v = col[a, k, c : c + CHUNK, :]
            return jnp.concatenate([v, v], axis=1) + side[k : k + 1]

        for c in range(0, PART, CHUNK):
            w = force_weights(
                dist[c : c + CHUNK, :],
                appr[c : c + CHUNK, :],
                total(0, c),
                total(1, c),
                total(2, c),
                total(3, c),
            )
            hi, lo = halves(w)
            ws[c : c + CHUNK, :] = hi
            ws[PART + c : PART + c + CHUNK, :] = lo

    def fold(x):
        return x[0:8] + x[8:16] + x[16:24]

    def combine(p):
        own = cf[pa[p]]
        second = fold(nn(jnp.concatenate([own, own], axis=1), ws[...]))
        first = fold(nt(cf[po[p]], ws[...]))
        return first[:, 0:PART] + first[:, PART:], second

    def store(p, sums, valid):
        if valid is True:
            acc1[pa[p]] += sums[0]
            acc2[ps[p]] += sums[1]
        else:
            keep = jnp.where(valid, 1.0, 0.0)
            acc1[pa[p]] += sums[0] * keep
            acc2[ps[p]] += sums[1] * keep

    ws[...] = jnp.zeros_like(ws)
    pipeline(count, load, combine, store, work)


def force_prepare_other(o, rows, fluid, bd, bs, cf, row):
    full, norm, cross = basis(rows)
    bd[o] = stack16(right_parts(right_distance(full, norm)))
    bs[o] = stack16(right_parts(full))
    cf[o] = stack16(list(split3(rows[7:8] * full)))
    pressure, sound, rho4 = force_fluid(fluid)
    row[o] = jnp.concatenate(
        [rows[6:7], sound, pressure, rho4, jnp.zeros((4, PART), f32)], axis=0
    )
    return full, norm, cross


def force_prepare_own(c, rows, fluid, bd, bs, cf, row, ad, as_, col):
    full, norm, cross = force_prepare_other(c, rows, fluid, bd, bs, cf, row)
    t = columns(left_parts(left_distance(full, norm)) + [row[c]])
    ad[c] = t[:, 0:48].astype(bf16)
    for k in range(4):
        col[c, k] = jnp.broadcast_to(t[:, 48 + k : 49 + k], (PART, 128))
    as_[c] = columns(left_parts(left_approach(full, cross)))[:, 0:48].astype(bf16)


def force_sums(rows, sums):
    full, _, cross = basis(rows)
    count = sums[7:8]
    accel = (-0.5 * K_SCALE) * (full[0:3] * count - sums[0:3])
    mixed = jnp.sum(full[3:6] * sums[0:3] + full[0:3] * sums[3:6], axis=0, keepdims=True)
    heat = (0.25 * K_SCALE) * (cross * count - mixed + sums[6:7])
    return jnp.concatenate([accel, heat], axis=0)


def own_force_kernel(
    state, fluid, pair_first, pair_offset, total, acc1, acc2,
    bd, bs, cf, ad, as_, row, col, dist, appr, ws, pa, po, ps,
):
    def mine(c, _):
        force_prepare_own(c, state[c], fluid[c], bd, bs, cf, row, ad, as_, col)
        return 0

    lax.fori_loop(0, CELLS, mine, 0)
    own_lists(pair_first, pair_offset, pa, po, ps, CELLS)
    acc1[...] = jnp.zeros_like(acc1)
    acc2[...] = jnp.zeros_like(acc2)
    refs = (bd, bs, cf, ad, as_, row, col, dist, appr, ws)
    force_pairs(CELLS + PAIRS, pa, po, ps, refs, acc1, acc2)
    total[...] = acc1[...] + acc2[0:CELLS]


def far_force_kernel(
    state, fluid, far, far_fluid, slot, proxy_cell, acc1, ret, acc2,
    bd, bs, cf, ad, as_, row, col, dist, appr, ws, pa, po, ps,
):
    def mine(c, _):
        force_prepare_own(c, state[c], fluid[c], bd, bs, cf, row, ad, as_, col)
        return 0

    lax.fori_loop(0, CELLS, mine, 0)

    def other(e, _):
        s = slot[e]
        force_prepare_other(CELLS + e, far[s], far_fluid[s], bd, bs, cf, row)
        pa[e] = proxy_cell[e]
        po[e] = CELLS + e
        ps[e] = e
        return 0

    lax.fori_loop(0, SEND, other, 0, unroll=2)
    acc1[...] = jnp.zeros_like(acc1)
    acc2[...] = jnp.zeros_like(acc2)
    refs = (bd, bs, cf, ad, as_, row, col, dist, appr, ws)
    force_pairs(SEND, pa, po, ps, refs, acc1, acc2)

    def back(e, _):
        s = slot[e]
        ret[s] = force_sums(far[s], acc2[e])
        return 0

    lax.fori_loop(0, SEND, back, 0, unroll=2)


def finish_kernel(
    back, goals, near, far, state, energy, counts, mig_cell, mig_dest, accel, leave, sums, moved, used
):
    sums[...] = jnp.zeros_like(sums)

    def one(s, _):
        goal = goals[s]
        sums[jnp.where(goal < 0, CELLS, goal)] += back[s]
        return 0

    lax.fori_loop(0, back.shape[0], one, 0, unroll=2)
    lane = lax.broadcasted_iota(i32, (1, PART), 1)

    def cell(c, _):
        rows = state[c]
        here = lane < counts[c]
        total = jnp.where(here, force_sums(rows, near[c] + far[c]) + sums[c], 0.0)
        accel[c] = total
        new_vel = rows[3:6] + STEP * total[0:3]
        new_pos = rows[0:3] + STEP * new_vel
        new_energy = energy[pl.ds(c, 1), :] + STEP * total[3:4]
        kicked = jnp.concatenate(
            [new_pos, new_vel, rows[7:8], rows[6:7], new_energy], axis=0
        )
        moved[c] = jnp.where(here, kicked, 0.0)
        return 0

    lax.fori_loop(0, CELLS, cell, 0)
    leave[...] = jnp.zeros_like(leave)

    def clear(d, _):
        used[d] = 0
        return 0

    lax.fori_loop(0, leave.shape[0] // CAPM, clear, 0)

    def entry(e, _):
        d = mig_dest[e]
        k = used[d]
        used[d] = k + 1
        leave[d * CAPM + k] = moved[mig_cell[e]]
        return 0

    lax.fori_loop(0, mig_cell.shape[0], entry, 0)


def density_scratch(others):
    return [
        pltpu.VMEM((others, 48, PART), bf16),
        pltpu.VMEM((others, 16, PART), bf16),
        pltpu.VMEM((others, 1, PART), f32),
        pltpu.VMEM((CELLS, PART, 48), bf16),
        pltpu.VMEM((CELLS, PART, 128), f32),
        pltpu.VMEM((PART, PART), f32),
        pltpu.VMEM((2 * PART, PART), bf16),
    ] + [pltpu.SMEM((SEND,), i32)] * 3


def force_scratch(others):
    return [
        pltpu.VMEM((others, 48, PART), bf16),
        pltpu.VMEM((others, 48, PART), bf16),
        pltpu.VMEM((others, 24, PART), bf16),
        pltpu.VMEM((CELLS, PART, 48), bf16),
        pltpu.VMEM((CELLS, PART, 48), bf16),
        pltpu.VMEM((others, 8, PART), f32),
        pltpu.VMEM((CELLS, 4, PART, 128), f32),
        pltpu.VMEM((PART, PART), f32),
        pltpu.VMEM((PART, PART), f32),
        pltpu.VMEM((2 * PART, PART), bf16),
    ] + [pltpu.SMEM((SEND,), i32)] * 3


def exchange(x, axes):
    return lax.all_to_all(x, axes, split_axis=0, concat_axis=0, tiled=True)


def local(
    position, velocity, mass, smoothing, energy, counts, proxy_cell, proxy_dest,
    proxy_target, pair_first, pair_offset, mig_cell, mig_dest,
):
    devices = lax.axis_size(("rows", "cols"))
    col_count = lax.axis_size("cols")
    slots = devices * CAP
    both = ("rows", "cols")
    state, req, slot = kernel_call(
        request_kernel,
        (shape(CELLS, 8, PART), shape(devices, 1, 128, dtype=i32), shape(SEND, dtype=i32)),
        [VMEM] * 4 + [SMEM] * 3,
        (VMEM, VMEM, SMEM),
        [pltpu.SMEM((devices,), i32)],
        moved=2**20,
    )(position, velocity, mass, smoothing, counts, proxy_dest[:, 0], proxy_target)
    goals = exchange(req, both)[:, 0, 0:CAP].reshape(slots)
    near = kernel_call(
        own_density_kernel,
        shape(CELLS, 8, PART),
        [VMEM] + [SMEM] * 2,
        VMEM,
        [pltpu.VMEM((CELLS, 8, PART), f32), pltpu.VMEM((CELLS + 1, 8, PART), f32)]
        + density_scratch(CELLS),
        flops=32 * PART * PART * 300,
        moved=2**20,
    )(state, pair_first, pair_offset)
    answer = kernel_call(
        respond_kernel, shape(slots, 8, PART), [VMEM, SMEM], VMEM, moved=4 * 2**20
    )(state, goals)
    far = exchange(answer, both)
    far_sums, ret = kernel_call(
        far_density_kernel,
        (shape(CELLS, 8, PART), shape(slots, 1, PART)),
        [VMEM] * 2 + [SMEM] * 2,
        (VMEM, VMEM),
        [pltpu.VMEM((SEND, 8, PART), f32)] + density_scratch(CELLS + SEND),
        flops=128 * PART * PART * 300,
        moved=2**20,
    )(state, far, slot, proxy_cell)
    back = exchange(ret, both)
    density, fluid, answer2 = kernel_call(
        combine_density_kernel,
        (shape(CELLS, PART), shape(CELLS, 2, PART), shape(slots, 2, PART)),
        [VMEM, SMEM] + [VMEM] * 3 + [SMEM],
        (VMEM, VMEM, VMEM),
        [pltpu.VMEM((CELLS + 1, 1, PART), f32)],
        moved=2**20,
    )(back, goals, near, far_sums, energy, counts)
    far_fluid = exchange(answer2, both)
    near_force = kernel_call(
        own_force_kernel,
        shape(CELLS, 8, PART),
        [VMEM] * 2 + [SMEM] * 2,
        VMEM,
        [pltpu.VMEM((CELLS, 8, PART), f32), pltpu.VMEM((CELLS + 1, 8, PART), f32)]
        + force_scratch(CELLS),
        flops=32 * PART * PART * 600,
        moved=2**20,
    )(state, fluid, pair_first, pair_offset)
    far_force, ret4 = kernel_call(
        far_force_kernel,
        (shape(CELLS, 8, PART), shape(slots, 4, PART)),
        [VMEM] * 4 + [SMEM] * 2,
        (VMEM, VMEM),
        [pltpu.VMEM((SEND, 8, PART), f32)] + force_scratch(CELLS + SEND),
        flops=128 * PART * PART * 600,
        moved=2**20,
    )(state, fluid, far, far_fluid, slot, proxy_cell)
    back4 = exchange(ret4, both)
    accel, leave = kernel_call(
        finish_kernel,
        (shape(CELLS, 4, PART), shape(col_count * CAPM, 9, PART)),
        [VMEM, SMEM] + [VMEM] * 4 + [SMEM] * 3,
        (VMEM, VMEM),
        [
            pltpu.VMEM((CELLS + 1, 4, PART), f32),
            pltpu.VMEM((CELLS, 9, PART), f32),
            pltpu.SMEM((col_count,), i32),
        ],
        moved=2**20,
    )(back4, goals, near_force, far_force, state, energy, counts, mig_cell, mig_dest[:, 0])
    arrived = exchange(leave, "cols")
    return (density, accel, arrived)


def solution(mesh):
    lead = ("rows", "cols")
    one, two, three = P(lead), P(lead, None), P(lead, None, None)
    return jax.shard_map(
        local,
        mesh=mesh,
        in_specs=(three, three, two, two, two, one, one, two, one, one, one, one, two),
        out_specs=(two, three, three),
        check_vma=False,
    )
```

```python
import jax
import jax.numpy as jnp
from jax import lax
from jax.experimental import pallas as pl
from jax.experimental.pallas import tpu as pltpu
from jax.sharding import PartitionSpec as P

CAP = 2
CAPM = 2
CELLS = 16
SEND = 128
PAIRS = 16
PART = 256

GAMMA = 5.0 / 3.0
STEP = 0.02
PI = 3.141592653589793
W_SCALE = 2.0 / PI
K_SCALE = -24.0 / PI
TINY = 1e-12
CHUNK = 32
ROWS = (128, 160, 192, 224, 256)
BLOCKS = SEND + CELLS

f32, bf16, i32 = jnp.float32, jnp.bfloat16, jnp.int32
VMEM = pl.BlockSpec(memory_space=pltpu.VMEM)
SMEM = pl.BlockSpec(memory_space=pltpu.SMEM)
LIMIT = 56 * 2**20


def shape(*dims, dtype=f32):
    return jax.ShapeDtypeStruct(dims, dtype)


def kernel_call(body, out_shape, in_specs, out_specs, scratch=(), flops=0, moved=0):
    return pl.pallas_call(
        body,
        out_shape=out_shape,
        in_specs=in_specs,
        out_specs=out_specs,
        scratch_shapes=list(scratch),
        compiler_params=pltpu.CompilerParams(vmem_limit_bytes=LIMIT),
        cost_estimate=pl.CostEstimate(flops=flops, bytes_accessed=moved, transcendentals=0),
    )


def sublane():
    return lax.broadcasted_iota(i32, (8, PART), 0)


def split3(x):
    a = x.astype(bf16).astype(f32)
    b = (x - a).astype(bf16).astype(f32)
    return a, b, x - a - b


def left_parts(x):
    a, b, c = split3(x)
    return [a, a, b, b, a, c]


def right_parts(x):
    a, b, c = split3(x)
    return [a, b, a, b, c, a]


def stack16(parts):
    return jnp.concatenate(parts, axis=0).astype(bf16)


def basis(rows):
    row = sublane()
    place = jnp.where(row < 3, 2.0 * rows - 1.0, rows)
    first = place[0:3]
    norm = jnp.sum(first * first, axis=0, keepdims=True)
    cross = jnp.sum(first * place[3:6], axis=0, keepdims=True)
    full = jnp.where(row < 6, place, jnp.where(row == 6, cross, 1.0))
    return full, norm, cross


def right_distance(full, norm):
    row = sublane()
    return jnp.where(
        row < 3, full, jnp.where(row == 3, norm, jnp.where(row == 4, 1.0, 0.0))
    )


def left_distance(full, norm):
    row = sublane()
    return jnp.where(
        row < 3, -2.0 * full, jnp.where(row == 3, 1.0, jnp.where(row == 4, norm, 0.0))
    )


def left_approach(full, cross):
    return 4.0 * jnp.concatenate(
        [-full[3:6], -full[0:3], jnp.ones((1, PART), f32), cross], axis=0
    )


def columns(parts):
    fill = 128 - 8 * len(parts)
    return jnp.concatenate(parts + [jnp.zeros((fill, PART), f32)], axis=0).T


def mass_rows(mass):
    a, b, c = split3(mass)
    return jnp.concatenate([a, b, c, jnp.zeros((13, PART), f32)], axis=0).astype(bf16)


def halves(w):
    hi = w.astype(bf16)
    return hi, (w - hi.astype(f32)).astype(bf16)


def request_kernel(pos, vel, mass, smooth, counts, dest, target, state, req, slot, used):
    lane = lax.broadcasted_iota(i32, (1, PART), 1)

    def cell(c, _):
        live = jnp.where(lane < counts[c], mass[pl.ds(c, 1), :], 0.0)
        state[c] = jnp.concatenate([pos[c], vel[c], smooth[pl.ds(c, 1), :], live], axis=0)
        return 0

    lax.fori_loop(0, CELLS, cell, 0)
    req[...] = jnp.full_like(req, -1)

    def clear(d, _):
        used[d] = 0
        return 0

    lax.fori_loop(0, req.shape[0], clear, 0)
    short = lax.broadcasted_iota(i32, (1, 128), 1)

    def entry(e, _):
        d = dest[e]
        k = used[d]
        used[d] = k + 1
        slot[e] = d * CAP + k
        req[d] = jnp.where(short == k, target[e], req[d])
        return 0

    lax.fori_loop(0, SEND, entry, 0)


def respond_kernel(state, goals, out):
    def one(s, _):
        goal = jnp.maximum(goals[s], 0)
        out[s] = state[goal]
        return 0

    lax.fori_loop(0, out.shape[0], one, 0, unroll=4)


def pipeline(count, rows_of, load, combine, store, work):
    load(0)

    def body(p, _):
        need = rows_of(p)
        low = 0
        for rows in ROWS:
            @pl.when((need > low) & (need <= rows))
            def _():
                sums = combine(jnp.maximum(p - 1, 0))
                work(p, rows)
                load(jnp.minimum(p + 1, count - 1))
                store(jnp.maximum(p - 1, 0), sums, p > 0)

            low = rows
        return 0

    lax.fori_loop(0, count, body, 0)
    store(count - 1, combine(count - 1), True)


def pack_plan(far, slot, proxy_cell, offset, block_own, live, filled):
    def clear(c, _):
        filled[c] = 0
        return 0

    lax.fori_loop(0, CELLS, clear, 0)

    def measure(e, _):
        mass = far[slot[e]][7:8]
        n = jnp.sum(jnp.where(mass > 0.0, 1.0, 0.0)).astype(i32)
        live[e] = n
        a = proxy_cell[e]
        offset[e] = filled[a]
        filled[a] = filled[a] + n
        return 0

    lax.fori_loop(0, SEND, measure, 0, unroll=8)

    def place(c, total):
        blocks = (filled[c] + PART - 1) // PART
        filled[c] = total * PART

        def name(t, _):
            block_own[total + t] = c
            return 0

        lax.fori_loop(0, blocks, name, 0)
        return total + blocks

    total = lax.fori_loop(0, CELLS, place, 0)

    def shift(e, _):
        offset[e] = offset[e] + filled[proxy_cell[e]]
        return 0

    lax.fori_loop(0, SEND, shift, 0, unroll=8)
    return total


def pack(target, rows, offset, n):
    t = offset // PART
    lane0 = offset - t * PART
    lane = lax.broadcasted_iota(i32, rows.shape, 1)
    turned = pltpu.roll(rows, lane0, 1)
    target[t] = jnp.where((lane >= lane0) & (lane < lane0 + n), turned, target[t])
    target[t + 1] = jnp.where(lane < lane0 + n - PART, turned, target[t + 1])


def unpack(source, offset):
    t = offset // PART
    lane0 = offset - t * PART
    first, second = source[t], source[t + 1]
    lane = lax.broadcasted_iota(i32, first.shape, 1)
    return pltpu.roll(jnp.where(lane >= lane0, first, second), lax.rem(PART - lane0, PART), 1)


def own_lists(pair_first, pair_offset, pa, po, ps, dummy):
    def one(e, _):
        pa[e] = e
        po[e] = e
        ps[e] = dummy
        a = pair_first[e]
        b = lax.rem(a + pair_offset[e], CELLS)
        pa[CELLS + e] = a
        po[CELLS + e] = b
        ps[CELLS + e] = b
        return 0

    lax.fori_loop(0, CELLS, one, 0)


def nn(a, b):
    return jnp.dot(a, b, preferred_element_type=f32)


def nt(a, b):
    return lax.dot_general(a, b, (((1,), (1,)), ((), ())), preferred_element_type=f32)


def density_weights(r2, total_h):
    inv = pltpu.reciprocal(total_h, approx=True)
    inv2 = inv * inv
    q2 = jnp.maximum(r2, TINY) * inv2
    q = q2 * lax.rsqrt(q2)
    u = 2.0 - q
    t = jnp.maximum(u, 0.0)
    return jnp.minimum(t * t * t, 4.0 - 3.0 * (q2 * u)) * (inv2 * inv)


def density_pairs(count, counts, pa, po, ps, bf, cj, hj, at, bh, dist, ws, acc1, acc2):
    def load(p):
        dist[...] = nn(at[pa[p]], bf[po[p]])

    def work(p, rows):
        a = pa[p]
        h_j = hj[po[p]]
        for c in range(0, rows, CHUNK):
            h_i = bh[a, c : c + CHUNK, :]
            w = density_weights(
                dist[c : c + CHUNK, :], jnp.concatenate([h_i, h_i], axis=1) + h_j
            )
            hi, lo = halves(w)
            ws[c : c + CHUNK, :] = hi
            ws[PART + c : PART + c + CHUNK, :] = lo

    def combine(p):
        own = cj[pa[p]]
        second = nn(jnp.concatenate([own, own], axis=1), ws[...])
        first = nt(cj[po[p]], ws[...])
        return first[0:8, 0:PART] + first[0:8, PART:], second[0:8]

    def store(p, sums, valid):
        if valid is True:
            acc1[pa[p]] += sums[0]
            acc2[ps[p]] += sums[1]
        else:
            keep = jnp.where(valid, 1.0, 0.0)
            acc1[pa[p]] += sums[0] * keep
            acc2[ps[p]] += sums[1] * keep

    ws[...] = jnp.zeros_like(ws)
    pipeline(count, lambda p: counts[pa[p]], load, combine, store, work)


def density_prepare_own(c, state, bf, cj, hj, at, bh):
    rows = state[c]
    full, norm, _ = basis(rows)
    bf[c] = stack16(right_parts(right_distance(full, norm)))
    cj[c] = mass_rows(rows[7:8])
    hj[c] = rows[6:7]
    t = columns(
        left_parts(left_distance(full, norm)) + [jnp.broadcast_to(rows[6:7], (8, PART))]
    )
    at[c] = t[:, 0:48].astype(bf16)
    bh[c] = jnp.broadcast_to(t[:, 48:49], (PART, 128))


def density_prepare_other(o, rows, bf, cj, hj):
    full, norm, _ = basis(rows)
    bf[o] = stack16(right_parts(right_distance(full, norm)))
    cj[o] = mass_rows(rows[7:8])
    hj[o] = rows[6:7]


def own_density_kernel(
    state, counts, pair_first, pair_offset, total, acc1, acc2, bf, cj, hj, at, bh, dist, ws, pa, po, ps
):
    lax.fori_loop(
        0, CELLS, lambda c, _: density_prepare_own(c, state, bf, cj, hj, at, bh) or 0, 0
    )
    own_lists(pair_first, pair_offset, pa, po, ps, CELLS)
    acc1[...] = jnp.zeros_like(acc1)
    acc2[...] = jnp.zeros_like(acc2)
    density_pairs(CELLS + PAIRS, counts, pa, po, ps, bf, cj, hj, at, bh, dist, ws, acc1, acc2)
    total[...] = acc1[...] + acc2[0:CELLS]


def far_density_kernel(
    state, far, counts, slot, proxy_cell, acc1, ret, blocks, offset, block_own, live, size, acc2,
    bf, cj, hj, at, bh, dist, ws, pa, po, ps, filled,
):
    lax.fori_loop(
        0, CELLS, lambda c, _: density_prepare_own(c, state, bf, cj, hj, at, bh) or 0, 0
    )
    total = pack_plan(far, slot, proxy_cell, offset, block_own, live, filled)
    size[0] = total
    blocks[...] = jnp.zeros_like(blocks)

    def fill(e, _):
        pack(blocks, far[slot[e]], offset[e], live[e])
        return 0

    lax.fori_loop(0, SEND, fill, 0, unroll=4)

    def other(t, _):
        density_prepare_other(CELLS + t, blocks[t], bf, cj, hj)
        pa[t] = block_own[t]
        po[t] = CELLS + t
        ps[t] = t
        acc2[t] = jnp.zeros((8, PART), f32)
        return 0

    lax.fori_loop(0, total, other, 0)
    acc1[...] = jnp.zeros_like(acc1)
    density_pairs(total, counts, pa, po, ps, bf, cj, hj, at, bh, dist, ws, acc1, acc2)

    def back(e, _):
        ret[slot[e]] = jnp.sum(unpack(acc2, offset[e])[0:3], axis=0, keepdims=True)
        return 0

    lax.fori_loop(0, SEND, back, 0, unroll=4)


def combine_density_kernel(
    back, goals, near, far, energy, counts, density, fluid, answer, sums
):
    sums[...] = jnp.zeros_like(sums)

    def one(s, _):
        goal = goals[s]
        sums[jnp.where(goal < 0, CELLS, goal)] += back[s]
        return 0

    lax.fori_loop(0, back.shape[0], one, 0, unroll=2)
    lane = lax.broadcasted_iota(i32, (1, PART), 1)

    def cell(c, _):
        both = near[c] + far[c]
        raw = W_SCALE * (jnp.sum(both[0:3], axis=0, keepdims=True) + sums[c])
        here = lane < counts[c]
        density[pl.ds(c, 1), :] = jnp.where(here, raw, 0.0)
        fluid[c] = jnp.concatenate(
            [jnp.where(here, raw, 1.0), energy[pl.ds(c, 1), :]], axis=0
        )
        return 0

    lax.fori_loop(0, CELLS, cell, 0)

    def send(s, _):
        answer[s] = fluid[jnp.maximum(goals[s], 0)]
        return 0

    lax.fori_loop(0, answer.shape[0], send, 0, unroll=4)


def force_weights(r2, s, total_h, total_c, total_p, total_r):
    inv = pltpu.reciprocal(total_h, approx=True)
    inv2 = inv * inv
    q2 = jnp.maximum(r2, TINY) * inv2
    rs = lax.rsqrt(q2)
    q = q2 * rs
    u = 2.0 - q
    t = jnp.maximum(u, 0.0)
    grad = jnp.where(q < 1.0, 3.0 * u - 2.0, t * t * rs)
    m = jnp.minimum(s, 0.0) * (inv * pltpu.reciprocal(q2 + 0.01, approx=True))
    visc = m * (m - total_c) * pltpu.reciprocal(total_r, approx=True)
    return (total_p + visc) * (grad * (inv2 * inv2 * inv))


def force_fluid(fluid):
    rho, u = fluid[0:1], fluid[1:2]
    pressure = (GAMMA - 1.0) * u / rho
    sound = jnp.sqrt(GAMMA * (GAMMA - 1.0) * u)
    return pressure, sound, 4.0 * rho


def force_pairs(count, counts, pa, po, ps, refs, acc1, acc2):
    bd, bs, cf, ad, as_, row, col, dist, appr, ws = refs

    def load(p):
        a, o = pa[p], po[p]
        dist[...] = nn(ad[a], bd[o])
        appr[...] = nn(as_[a], bs[o])

    def work(p, rows):
        a, o = pa[p], po[p]
        side = row[o]

        def total(k, c):
            v = col[a, k, c : c + CHUNK, :]
            return jnp.concatenate([v, v], axis=1) + side[k : k + 1]

        for c in range(0, rows, CHUNK):
            w = force_weights(
                dist[c : c + CHUNK, :],
                appr[c : c + CHUNK, :],
                total(0, c),
                total(1, c),
                total(2, c),
                total(3, c),
            )
            hi, lo = halves(w)
            ws[c : c + CHUNK, :] = hi
            ws[PART + c : PART + c + CHUNK, :] = lo

    def fold(x):
        return x[0:8] + x[8:16] + x[16:24]

    def combine(p):
        own = cf[pa[p]]
        second = fold(nn(jnp.concatenate([own, own], axis=1), ws[...]))
        first = fold(nt(cf[po[p]], ws[...]))
        return first[:, 0:PART] + first[:, PART:], second

    def store(p, sums, valid):
        if valid is True:
            acc1[pa[p]] += sums[0]
            acc2[ps[p]] += sums[1]
        else:
            keep = jnp.where(valid, 1.0, 0.0)
            acc1[pa[p]] += sums[0] * keep
            acc2[ps[p]] += sums[1] * keep

    ws[...] = jnp.zeros_like(ws)
    pipeline(count, lambda p: counts[pa[p]], load, combine, store, work)


def force_prepare_other(o, rows, fluid, bd, bs, cf, row):
    full, norm, cross = basis(rows)
    bd[o] = stack16(right_parts(right_distance(full, norm)))
    bs[o] = stack16(right_parts(full))
    cf[o] = stack16(list(split3(rows[7:8] * full)))
    pressure, sound, rho4 = force_fluid(fluid)
    row[o] = jnp.concatenate(
        [rows[6:7], sound, pressure, rho4, jnp.zeros((4, PART), f32)], axis=0
    )
    return full, norm, cross


def force_prepare_own(c, rows, fluid, bd, bs, cf, row, ad, as_, col):
    full, norm, cross = force_prepare_other(c, rows, fluid, bd, bs, cf, row)
    t = columns(left_parts(left_distance(full, norm)) + [row[c]])
    ad[c] = t[:, 0:48].astype(bf16)
    for k in range(4):
        col[c, k] = jnp.broadcast_to(t[:, 48 + k : 49 + k], (PART, 128))
    as_[c] = columns(left_parts(left_approach(full, cross)))[:, 0:48].astype(bf16)


def force_sums(rows, sums):
    full, _, cross = basis(rows)
    count = sums[7:8]
    accel = (-0.5 * K_SCALE) * (full[0:3] * count - sums[0:3])
    mixed = jnp.sum(full[3:6] * sums[0:3] + full[0:3] * sums[3:6], axis=0, keepdims=True)
    heat = (0.25 * K_SCALE) * (cross * count - mixed + sums[6:7])
    return jnp.concatenate([accel, heat], axis=0)


def own_force_kernel(
    state, fluid, counts, pair_first, pair_offset, total, acc1, acc2,
    bd, bs, cf, ad, as_, row, col, dist, appr, ws, pa, po, ps,
):
    def mine(c, _):
        force_prepare_own(c, state[c], fluid[c], bd, bs, cf, row, ad, as_, col)
        return 0

    lax.fori_loop(0, CELLS, mine, 0)
    own_lists(pair_first, pair_offset, pa, po, ps, CELLS)
    acc1[...] = jnp.zeros_like(acc1)
    acc2[...] = jnp.zeros_like(acc2)
    refs = (bd, bs, cf, ad, as_, row, col, dist, appr, ws)
    force_pairs(CELLS + PAIRS, counts, pa, po, ps, refs, acc1, acc2)
    total[...] = acc1[...] + acc2[0:CELLS]


def far_force_kernel(
    state, fluid, blocks, far_fluid, counts, slot, offset, block_own, live, size, acc1, ret, acc2,
    fluids, bd, bs, cf, ad, as_, row, col, dist, appr, ws, pa, po, ps,
):
    def mine(c, _):
        force_prepare_own(c, state[c], fluid[c], bd, bs, cf, row, ad, as_, col)
        return 0

    lax.fori_loop(0, CELLS, mine, 0)
    fluids[...] = jnp.ones_like(fluids)

    def fill(e, _):
        pack(fluids, far_fluid[slot[e]], offset[e], live[e])
        return 0

    lax.fori_loop(0, SEND, fill, 0, unroll=4)
    total = size[0]

    def other(t, _):
        force_prepare_other(CELLS + t, blocks[t], fluids[t], bd, bs, cf, row)
        pa[t] = block_own[t]
        po[t] = CELLS + t
        ps[t] = t
        return 0

    lax.fori_loop(0, total, other, 0)
    acc1[...] = jnp.zeros_like(acc1)
    acc2[...] = jnp.zeros_like(acc2)
    refs = (bd, bs, cf, ad, as_, row, col, dist, appr, ws)
    force_pairs(total, counts, pa, po, ps, refs, acc1, acc2)

    def turn(t, _):
        acc2[t, 0:4] = force_sums(blocks[t], acc2[t])
        return 0

    lax.fori_loop(0, total, turn, 0)

    def back(e, _):
        ret[slot[e]] = unpack(acc2, offset[e])[0:4]
        return 0

    lax.fori_loop(0, SEND, back, 0, unroll=4)


def finish_kernel(
    back, goals, near, far, state, energy, counts, mig_cell, mig_dest, accel, leave, sums, moved, used
):
    sums[...] = jnp.zeros_like(sums)

    def one(s, _):
        goal = goals[s]
        sums[jnp.where(goal < 0, CELLS, goal)] += back[s]
        return 0

    lax.fori_loop(0, back.shape[0], one, 0, unroll=2)
    lane = lax.broadcasted_iota(i32, (1, PART), 1)

    def cell(c, _):
        rows = state[c]
        here = lane < counts[c]
        total = jnp.where(here, force_sums(rows, near[c] + far[c]) + sums[c], 0.0)
        accel[c] = total
        new_vel = rows[3:6] + STEP * total[0:3]
        new_pos = rows[0:3] + STEP * new_vel
        new_energy = energy[pl.ds(c, 1), :] + STEP * total[3:4]
        kicked = jnp.concatenate(
            [new_pos, new_vel, rows[7:8], rows[6:7], new_energy], axis=0
        )
        moved[c] = jnp.where(here, kicked, 0.0)
        return 0

    lax.fori_loop(0, CELLS, cell, 0)
    leave[...] = jnp.zeros_like(leave)

    def clear(d, _):
        used[d] = 0
        return 0

    lax.fori_loop(0, leave.shape[0] // CAPM, clear, 0)

    def entry(e, _):
        d = mig_dest[e]
        k = used[d]
        used[d] = k + 1
        leave[d * CAPM + k] = moved[mig_cell[e]]
        return 0

    lax.fori_loop(0, mig_cell.shape[0], entry, 0)


def density_scratch(others):
    return [
        pltpu.VMEM((others, 48, PART), bf16),
        pltpu.VMEM((others, 16, PART), bf16),
        pltpu.VMEM((others, 1, PART), f32),
        pltpu.VMEM((CELLS, PART, 48), bf16),
        pltpu.VMEM((CELLS, PART, 128), f32),
        pltpu.VMEM((PART, PART), f32),
        pltpu.VMEM((2 * PART, PART), bf16),
    ] + [pltpu.SMEM((BLOCKS,), i32)] * 3


def force_scratch(others):
    return [
        pltpu.VMEM((others, 48, PART), bf16),
        pltpu.VMEM((others, 48, PART), bf16),
        pltpu.VMEM((others, 24, PART), bf16),
        pltpu.VMEM((CELLS, PART, 48), bf16),
        pltpu.VMEM((CELLS, PART, 48), bf16),
        pltpu.VMEM((others, 8, PART), f32),
        pltpu.VMEM((CELLS, 4, PART, 128), f32),
        pltpu.VMEM((PART, PART), f32),
        pltpu.VMEM((PART, PART), f32),
        pltpu.VMEM((2 * PART, PART), bf16),
    ] + [pltpu.SMEM((BLOCKS,), i32)] * 3


def exchange(x, axes):
    return lax.all_to_all(x, axes, split_axis=0, concat_axis=0, tiled=True)


def local(
    position, velocity, mass, smoothing, energy, counts, proxy_cell, proxy_dest,
    proxy_target, pair_first, pair_offset, mig_cell, mig_dest,
):
    devices = lax.axis_size(("rows", "cols"))
    col_count = lax.axis_size("cols")
    slots = devices * CAP
    both = ("rows", "cols")
    state, req, slot = kernel_call(
        request_kernel,
        (shape(CELLS, 8, PART), shape(devices, 1, 128, dtype=i32), shape(SEND, dtype=i32)),
        [VMEM] * 4 + [SMEM] * 3,
        (VMEM, VMEM, SMEM),
        [pltpu.SMEM((devices,), i32)],
        moved=2**20,
    )(position, velocity, mass, smoothing, counts, proxy_dest[:, 0], proxy_target)
    goals = exchange(req, both)[:, 0, 0:CAP].reshape(slots)
    near = kernel_call(
        own_density_kernel,
        shape(CELLS, 8, PART),
        [VMEM] + [SMEM] * 3,
        VMEM,
        [pltpu.VMEM((CELLS, 8, PART), f32), pltpu.VMEM((CELLS + 1, 8, PART), f32)]
        + density_scratch(CELLS),
        flops=32 * PART * PART * 300,
        moved=2**20,
    )(state, counts, pair_first, pair_offset)
    answer = kernel_call(
        respond_kernel, shape(slots, 8, PART), [VMEM, SMEM], VMEM, moved=4 * 2**20
    )(state, goals)
    far = exchange(answer, both)
    far_sums, ret, blocks, offset, block_own, live, size = kernel_call(
        far_density_kernel,
        (
            shape(CELLS, 8, PART),
            shape(slots, 1, PART),
            shape(BLOCKS + 1, 8, PART),
            shape(SEND, dtype=i32),
            shape(BLOCKS, dtype=i32),
            shape(SEND, dtype=i32),
            shape(1, dtype=i32),
        ),
        [VMEM] * 2 + [SMEM] * 3,
        (VMEM,) * 3 + (SMEM,) * 4,
        [pltpu.VMEM((BLOCKS + 1, 8, PART), f32)]
        + density_scratch(CELLS + BLOCKS)
        + [pltpu.SMEM((CELLS,), i32)],
        flops=128 * PART * PART * 300,
        moved=2**20,
    )(state, far, counts, slot, proxy_cell)
    back = exchange(ret, both)
    density, fluid, answer2 = kernel_call(
        combine_density_kernel,
        (shape(CELLS, PART), shape(CELLS, 2, PART), shape(slots, 2, PART)),
        [VMEM, SMEM] + [VMEM] * 3 + [SMEM],
        (VMEM, VMEM, VMEM),
        [pltpu.VMEM((CELLS + 1, 1, PART), f32)],
        moved=2**20,
    )(back, goals, near, far_sums, energy, counts)
    far_fluid = exchange(answer2, both)
    near_force = kernel_call(
        own_force_kernel,
        shape(CELLS, 8, PART),
        [VMEM] * 2 + [SMEM] * 3,
        VMEM,
        [pltpu.VMEM((CELLS, 8, PART), f32), pltpu.VMEM((CELLS + 1, 8, PART), f32)]
        + force_scratch(CELLS),
        flops=32 * PART * PART * 600,
        moved=2**20,
    )(state, fluid, counts, pair_first, pair_offset)
    far_force, ret4 = kernel_call(
        far_force_kernel,
        (shape(CELLS, 8, PART), shape(slots, 4, PART)),
        [VMEM] * 4 + [SMEM] * 6,
        (VMEM, VMEM),
        [pltpu.VMEM((BLOCKS + 1, 8, PART), f32), pltpu.VMEM((BLOCKS + 1, 2, PART), f32)]
        + force_scratch(CELLS + BLOCKS),
        flops=128 * PART * PART * 600,
        moved=2**20,
    )(state, fluid, blocks, far_fluid, counts, slot, offset, block_own, live, size)
    back4 = exchange(ret4, both)
    accel, leave = kernel_call(
        finish_kernel,
        (shape(CELLS, 4, PART), shape(col_count * CAPM, 9, PART)),
        [VMEM, SMEM] + [VMEM] * 4 + [SMEM] * 3,
        (VMEM, VMEM),
        [
            pltpu.VMEM((CELLS + 1, 4, PART), f32),
            pltpu.VMEM((CELLS, 9, PART), f32),
            pltpu.SMEM((col_count,), i32),
        ],
        moved=2**20,
    )(back4, goals, near_force, far_force, state, energy, counts, mig_cell, mig_dest[:, 0])
    arrived = exchange(leave, "cols")
    return (density, accel, arrived)


def solution(mesh):
    lead = ("rows", "cols")
    one, two, three = P(lead), P(lead, None), P(lead, None, None)
    return jax.shard_map(
        local,
        mesh=mesh,
        in_specs=(three, three, two, two, two, one, one, two, one, one, one, one, two),
        out_specs=(two, three, three),
        check_vma=False,
    )
```

```python
import jax
import jax.numpy as jnp
from jax import lax
from jax.experimental import pallas as pl
from jax.experimental.pallas import tpu as pltpu
from jax.sharding import PartitionSpec as P

CAP = 2
CAPM = 2
CELLS = 16
SEND = 128
PAIRS = 16
PART = 256

GAMMA = 5.0 / 3.0
STEP = 0.02
PI = 3.141592653589793
W_SCALE = 2.0 / PI
K_SCALE = -24.0 / PI
TINY = 1e-12
CHUNK = 32
ROWS = (128, 160, 192, 224, 256)
BLOCKS = SEND + CELLS
EARLY, LATE = 42, 48
DEPTH = 4

f32, bf16, i32 = jnp.float32, jnp.bfloat16, jnp.int32
VMEM = pl.BlockSpec(memory_space=pltpu.VMEM)
ANY = pl.BlockSpec(memory_space=pl.ANY)
SMEM = pl.BlockSpec(memory_space=pltpu.SMEM)
LIMIT = 56 * 2**20


def shape(*dims, dtype=f32):
    return jax.ShapeDtypeStruct(dims, dtype)


def kernel_call(body, out_shape, in_specs, out_specs, scratch=(), flops=0, moved=0):
    return pl.pallas_call(
        body,
        out_shape=out_shape,
        in_specs=in_specs,
        out_specs=out_specs,
        scratch_shapes=list(scratch),
        compiler_params=pltpu.CompilerParams(vmem_limit_bytes=LIMIT),
        cost_estimate=pl.CostEstimate(flops=flops, bytes_accessed=moved, transcendentals=0),
    )


def sublane():
    return lax.broadcasted_iota(i32, (8, PART), 0)


def split3(x):
    a = x.astype(bf16).astype(f32)
    b = (x - a).astype(bf16).astype(f32)
    return a, b, x - a - b


def left_parts(x):
    a, b, c = split3(x)
    return [a, a, b, b, a, c]


def right_parts(x):
    a, b, c = split3(x)
    return [a, b, a, b, c, a]


def stack16(parts):
    return jnp.concatenate(parts, axis=0).astype(bf16)


def basis(rows):
    row = sublane()
    place = jnp.where(row < 3, 2.0 * rows - 1.0, rows)
    first = place[0:3]
    norm = jnp.sum(first * first, axis=0, keepdims=True)
    cross = jnp.sum(first * place[3:6], axis=0, keepdims=True)
    full = jnp.where(row < 6, place, jnp.where(row == 6, cross, 1.0))
    return full, norm, cross


def right_distance(full, norm):
    row = sublane()
    return jnp.where(
        row < 3, full, jnp.where(row == 3, norm, jnp.where(row == 4, 1.0, 0.0))
    )


def left_distance(full, norm):
    row = sublane()
    return jnp.where(
        row < 3, -2.0 * full, jnp.where(row == 3, 1.0, jnp.where(row == 4, norm, 0.0))
    )


def left_approach(full, cross):
    return 4.0 * jnp.concatenate(
        [-full[3:6], -full[0:3], jnp.ones((1, PART), f32), cross], axis=0
    )


def columns(parts):
    fill = 128 - 8 * len(parts)
    return jnp.concatenate(parts + [jnp.zeros((fill, PART), f32)], axis=0).T


def mass_rows(mass):
    a, b, c = split3(mass)
    return jnp.concatenate([a, b, c, jnp.zeros((13, PART), f32)], axis=0).astype(bf16)


def halves(w):
    hi = w.astype(bf16)
    return hi, (w - hi.astype(f32)).astype(bf16)


def request_kernel(pos, vel, mass, smooth, counts, dest, target, state, req, slot, used):
    lane = lax.broadcasted_iota(i32, (1, PART), 1)

    def cell(c, _):
        live = jnp.where(lane < counts[c], mass[pl.ds(c, 1), :], 0.0)
        state[c] = jnp.concatenate([pos[c], vel[c], smooth[pl.ds(c, 1), :], live], axis=0)
        return 0

    lax.fori_loop(0, CELLS, cell, 0)
    req[...] = jnp.full_like(req, -1)

    def clear(d, _):
        used[d] = 0
        return 0

    lax.fori_loop(0, req.shape[0], clear, 0)
    short = lax.broadcasted_iota(i32, (1, 128), 1)

    def entry(e, _):
        d = dest[e]
        k = used[d]
        used[d] = k + 1
        slot[e] = d * CAP + k
        req[d] = jnp.where(short == k, target[e], req[d])
        return 0

    lax.fori_loop(0, SEND, entry, 0)


def respond_kernel(state, goals, out):
    def one(s, _):
        goal = jnp.maximum(goals[s], 0)
        out[s] = state[goal]
        return 0

    lax.fori_loop(0, out.shape[0], one, 0, unroll=4)


def by_rows(need, step):
    low = 0
    for rows in ROWS:
        pl.when((need > low) & (need <= rows))(lambda rows=rows: step(rows))
        low = rows


def pipeline(first, count, rows_of, prepare, load, combine, store, work):
    last = first + count - 1

    def clamp(p):
        return jnp.minimum(p, last)

    for k in range(3):
        prepare(clamp(first + k))
    load(first, 0)

    def body(t, _):
        p = first + 2 * t

        def step(rows):
            before = jnp.maximum(p - 1, first)
            sums = combine(before, 1)
            work(p, 0, rows)
            load(p + 1, 1)
            sums0 = combine(p, 0)
            work(p + 1, 1, rows)
            load(clamp(p + 2), 0)
            store(before, sums, t > 0)
            store(p, sums0, True)
            prepare(clamp(p + 3))
            prepare(clamp(p + 4))

        by_rows(jnp.maximum(rows_of(p), rows_of(p + 1)), step)
        return 0

    lax.fori_loop(0, count // 2, body, 0)
    store(last, combine(last, 1), True)


def keep_sums(acc1, acc2, a, s, sums, valid):
    if valid is not True:
        keep = jnp.where(valid, 1.0, 0.0)
        sums = (sums[0] * keep, sums[1] * keep)
    acc1[a] += sums[0]
    acc2[s] += sums[1]


def pack_plan(far, slot, proxy_cell, offset, block_own, live, filled):
    def clear(c, _):
        filled[c] = 0
        return 0

    lax.fori_loop(0, CELLS, clear, 0)

    def measure(e, _):
        mass = far[slot[e]][7:8]
        n = jnp.sum(jnp.where(mass > 0.0, 1.0, 0.0)).astype(i32)
        live[e] = n
        a = proxy_cell[e]
        offset[e] = filled[a]
        filled[a] = filled[a] + n
        return 0

    lax.fori_loop(0, SEND, measure, 0, unroll=16)

    def place(c, total):
        blocks = (filled[c] + PART - 1) // PART
        filled[c] = total * PART

        def name(t, _):
            block_own[total + t] = c
            return 0

        lax.fori_loop(0, blocks, name, 0)
        return total + blocks

    total = lax.fori_loop(0, CELLS, place, 0)

    def shift(e, _):
        offset[e] = offset[e] + filled[proxy_cell[e]]
        return 0

    lax.fori_loop(0, SEND, shift, 0, unroll=8)
    block_own[total] = block_own[total - 1]
    return total + lax.rem(total, 2)


def pack(target, rows, offset, n):
    t = offset // PART
    lane0 = offset - t * PART
    lane = lax.broadcasted_iota(i32, rows.shape, 1)
    turned = pltpu.roll(rows, lane0, 1)
    target[t] = jnp.where((lane >= lane0) & (lane < lane0 + n), turned, target[t])
    target[t + 1] = jnp.where(lane < lane0 + n - PART, turned, target[t + 1])


def unpack(source, offset):
    t = offset // PART
    lane0 = offset - t * PART
    first, second = source[t], source[t + 1]
    lane = lax.broadcasted_iota(i32, first.shape, 1)
    return pltpu.roll(jnp.where(lane >= lane0, first, second), lax.rem(PART - lane0, PART), 1)


def own_lists(pair_first, pair_offset, pa, po, ps, dummy):
    def one(e, _):
        pa[e] = e
        po[e] = e
        ps[e] = dummy
        a = pair_first[e]
        b = lax.rem(a + pair_offset[e], CELLS)
        pa[CELLS + e] = a
        po[CELLS + e] = b
        ps[CELLS + e] = b
        return 0

    lax.fori_loop(0, CELLS, one, 0)


def nn(a, b):
    return jnp.dot(a, b, preferred_element_type=f32)


def nt(a, b):
    return lax.dot_general(a, b, (((1,), (1,)), ((), ())), preferred_element_type=f32)


def density_weights(r2, total_h):
    inv = pltpu.reciprocal(total_h, approx=True)
    inv2 = inv * inv
    q2 = jnp.maximum(r2, TINY) * inv2
    q = q2 * lax.rsqrt(q2)
    u = 2.0 - q
    t = jnp.maximum(u, 0.0)
    return jnp.minimum(t * t * t, 4.0 - 3.0 * (q2 * u)) * (inv2 * inv)


def density_pairs(count, counts, pa, po, ps, refs, prepare, acc1, acc2):
    bf, own_m, other_m, hj, at, bh, dist, ws = refs

    def load(p, side):
        dist[side][...] = nn(at[pa(p)], bf[po(p)])

    def work(p, side, rows):
        a = pa(p)
        h_j = hj[po(p)]
        for c in range(0, rows, CHUNK):
            h_i = bh[a, c : c + CHUNK, :]
            w = density_weights(
                dist[side][c : c + CHUNK, :], jnp.concatenate([h_i, h_i], axis=1) + h_j
            )
            hi, lo = halves(w)
            ws[side][c : c + CHUNK, :] = hi
            ws[side][PART + c : PART + c + CHUNK, :] = lo

    def combine(p, side):
        own = own_m[pa(p)]
        second = nn(jnp.concatenate([own, own], axis=1), ws[side][...])
        first = nt(other_m[po(p)], ws[side][...])
        return first[0:8, 0:PART] + first[0:8, PART:], second[0:8]

    def store(p, sums, valid):
        keep_sums(acc1, acc2, pa(p), ps(p), sums, valid)

    for side in range(2):
        ws[side][...] = jnp.zeros_like(ws[side])
    pipeline(0, count, lambda p: counts[pa(p)], prepare, load, combine, store, work)


def density_prepare(o, rows, bf, cj, hj):
    full, norm, cross = basis(rows)
    bf[o] = stack16(right_parts(right_distance(full, norm)))
    cj[o] = mass_rows(rows[7:8])
    hj[o] = rows[6:7]
    return full, norm, cross


def own_density_kernel(
    state, counts, pair_first, pair_offset, total, at, as_, bh, cj,
    acc1, acc2, bf, hj, dist0, dist1, ws0, ws1, pa, po, ps,
):
    def mine(c, _):
        rows = state[c]
        full, norm, cross = density_prepare(c, rows, bf, cj, hj)
        t = columns(
            left_parts(left_distance(full, norm))
            + [jnp.broadcast_to(rows[6:7], (8, PART))]
            + left_parts(left_approach(full, cross))
        )
        at[c] = t[:, 0:48].astype(bf16)
        as_[c] = t[:, 56:104].astype(bf16)
        bh[c] = jnp.broadcast_to(t[:, 48:49], (PART, 128))
        return 0

    lax.fori_loop(0, CELLS, mine, 0, unroll=2)
    own_lists(pair_first, pair_offset, pa, po, ps, CELLS)
    acc1[...] = jnp.zeros_like(acc1)
    acc2[...] = jnp.zeros_like(acc2)
    refs = (bf, cj, cj, hj, at, bh, (dist0, dist1), (ws0, ws1))
    density_pairs(
        CELLS + PAIRS, counts, lambda p: pa[p], lambda p: po[p], lambda p: ps[p], refs,
        lambda p: None, acc1, acc2,
    )
    total[...] = acc1[...] + acc2[0:CELLS]


def far_density_kernel(
    state, far, counts, slot, proxy_cell, at, bh, own_m,
    acc1, ret, blocks, offset, block_own, live, size,
    acc2, bf, cj, hj, dist0, dist1, ws0, ws1, filled,
):
    total = pack_plan(far, slot, proxy_cell, offset, block_own, live, filled)
    size[0] = total
    blocks[...] = jnp.zeros_like(blocks)

    def fill(e, _):
        pack(blocks, far[slot[e]], offset[e], live[e])
        return 0

    lax.fori_loop(0, SEND, fill, 0, unroll=8)
    acc2[...] = jnp.zeros_like(acc2)
    acc1[...] = jnp.zeros_like(acc1)
    refs = (bf, own_m, cj, hj, at, bh, (dist0, dist1), (ws0, ws1))
    same = lambda p: p
    density_pairs(
        total, counts, lambda p: block_own[p], same, same, refs,
        lambda p: density_prepare(p, blocks[p], bf, cj, hj), acc1, acc2,
    )

    def back(e, _):
        ret[slot[e]] = jnp.sum(unpack(acc2, offset[e])[0:3], axis=0, keepdims=True)
        return 0

    lax.fori_loop(0, SEND, back, 0, unroll=8)


def combine_density_kernel(
    back, goals, near, far, energy, counts, density, fluid, answer, sums
):
    sums[...] = jnp.zeros_like(sums)

    def one(s, _):
        goal = goals[s]
        sums[jnp.where(goal < 0, CELLS, goal)] += back[s]
        return 0

    lax.fori_loop(0, back.shape[0], one, 0, unroll=2)
    lane = lax.broadcasted_iota(i32, (1, PART), 1)

    def cell(c, _):
        both = near[c] + far[c]
        raw = W_SCALE * (jnp.sum(both[0:3], axis=0, keepdims=True) + sums[c])
        here = lane < counts[c]
        density[pl.ds(c, 1), :] = jnp.where(here, raw, 0.0)
        fluid[c] = jnp.concatenate(
            [jnp.where(here, raw, 1.0), energy[pl.ds(c, 1), :]], axis=0
        )
        return 0

    lax.fori_loop(0, CELLS, cell, 0)

    def send(s, _):
        answer[s] = fluid[jnp.maximum(goals[s], 0)]
        return 0

    lax.fori_loop(0, answer.shape[0], send, 0, unroll=4)


def slope_weights(r2, s, total_h):
    inv = pltpu.reciprocal(total_h, approx=True)
    inv2 = inv * inv
    q2 = jnp.maximum(r2, TINY) * inv2
    rs = lax.rsqrt(q2)
    q = q2 * rs
    u = 2.0 - q
    t = jnp.maximum(u, 0.0)
    grad = jnp.where(q < 1.0, 3.0 * u - 2.0, t * t * rs)
    m = jnp.minimum(s, 0.0) * (inv * pltpu.reciprocal(q2 + 0.01, approx=True))
    return grad * (inv2 * inv2 * inv), m


def fluid_weights(grad, m, total_c, total_p, total_r):
    return (total_p + m * (m - total_c) * pltpu.reciprocal(total_r, approx=True)) * grad


def force_fluid(fluid):
    rho, u = fluid[0:1], fluid[1:2]
    pressure = (GAMMA - 1.0) * u / rho
    sound = jnp.sqrt(GAMMA * (GAMMA - 1.0) * u)
    return pressure, sound, 4.0 * rho


def two_wide(col, row):
    return jnp.concatenate([col, col], axis=1) + row


def put_halves(ws, c, w):
    hi, lo = halves(w)
    ws[c : c + CHUNK, :] = hi
    ws[PART + c : PART + c + CHUNK, :] = lo


def fluid_work(ws, col, side_row, a, rows, grads):
    for c in range(0, rows, CHUNK):
        grad, m = grads(c)
        total = [
            two_wide(col[a, k, c : c + CHUNK, :], side_row[k + 1 : k + 2]) for k in range(3)
        ]
        put_halves(ws, c, fluid_weights(grad, m, *total))


def fold(x):
    return x[0:8] + x[8:16] + x[16:24]


def force_combine(own, other, ws):
    second = fold(nn(jnp.concatenate([own, own], axis=1), ws[...]))
    first = fold(nt(other, ws[...]))
    return first[:, 0:PART] + first[:, PART:], second


def full_force(first, count, counts, pa, po, ps, refs, prepare, acc1, acc2):
    bd, bs, own_cf, other_cf, at, as_, bh, row, col, dist, appr, ws = refs

    def load(p, side):
        a, o = pa(p), po(p)
        dist[side][...] = nn(at[a], bd[o])
        appr[side][...] = nn(as_[a], bs[o])

    def work(p, side, rows):
        a = pa(p)
        side_row = row[po(p)]

        def grads(c):
            return slope_weights(
                dist[side][c : c + CHUNK, :],
                appr[side][c : c + CHUNK, :],
                two_wide(bh[a, c : c + CHUNK, :], side_row[0:1]),
            )

        fluid_work(ws[side], col, side_row, a, rows, grads)

    def combine(p, side):
        return force_combine(own_cf[pa(p)], other_cf[po(p)], ws[side])

    def store(p, sums, valid):
        keep_sums(acc1, acc2, pa(p), ps(p), sums, valid)

    pipeline(first, count, lambda p: counts[pa(p)], prepare, load, combine, store, work)


def geometry_prepare(o, rows, bd, bs):
    full, norm, cross = basis(rows)
    bd[o] = stack16(right_parts(right_distance(full, norm)))
    bs[o] = stack16(right_parts(full))
    return full


def fluid_prepare(o, rows, full, fluid, cf, row):
    cf[o] = stack16(list(split3(rows[7:8] * full)))
    pressure, sound, rho4 = force_fluid(fluid)
    row[o] = jnp.concatenate(
        [rows[6:7], sound, pressure, rho4, jnp.zeros((4, PART), f32)], axis=0
    )


def own_fluid_columns(c, row, col):
    t = columns([row[c]])
    for k in range(3):
        col[c, k] = jnp.broadcast_to(t[:, k + 1 : k + 2], (PART, 128))


def slope_kernel(
    state_after, blocks, counts, block_own, size, at, as_, bh, out,
    bd, bs, hj, dist0, dist1, appr0, appr1, buf, sems, *, first,
):
    del state_after
    dist, appr = (dist0, dist1), (appr0, appr1)
    count = jnp.clip(size[0] - first, 0, out.shape[0])
    last = first + count - 1

    def clamp(p):
        return jnp.minimum(p, last)

    def prepare(p):
        rows = blocks[p]
        geometry_prepare(p - first, rows, bd, bs)
        hj[p - first] = rows[6:7]

    def load(p, side):
        a = block_own[p]
        dist[side][...] = nn(at[a], bd[p - first])
        appr[side][...] = nn(as_[a], bs[p - first])

    def copy(t):
        k = lax.rem(t, DEPTH)
        return pltpu.make_async_copy(buf.at[k], out.at[pl.ds(2 * t, 2)], sems.at[k])

    def work(p, side, rows, k):
        a = block_own[p]
        h_j = hj[p - first]
        for c in range(0, rows, CHUNK):
            grad, m = slope_weights(
                dist[side][c : c + CHUNK, :],
                appr[side][c : c + CHUNK, :],
                two_wide(bh[a, c : c + CHUNK, :], h_j),
            )
            buf[k, side, 0, c : c + CHUNK, :] = grad
            buf[k, side, 1, c : c + CHUNK, :] = m

    @pl.when(count > 0)
    def _():
        for k in range(3):
            prepare(clamp(first + k))
        load(first, 0)

    def body(t, _):
        p = first + 2 * t
        k = lax.rem(t, DEPTH)
        pl.when(t >= DEPTH)(lambda: copy(t - DEPTH).wait())

        def step(rows):
            load(p + 1, 1)
            work(p, 0, rows, k)
            work(p + 1, 1, rows, k)
            load(clamp(p + 2), 0)
            prepare(clamp(p + 3))
            prepare(clamp(p + 4))

        by_rows(jnp.maximum(counts[block_own[p]], counts[block_own[p + 1]]), step)
        copy(t).start()
        return 0

    steps = count // 2
    lax.fori_loop(0, steps, body, 0)

    def drain(t, _):
        copy(t).wait()
        return 0

    lax.fori_loop(jnp.maximum(steps - DEPTH, 0), steps, drain, 0)


def force_sums(rows, sums):
    full, _, cross = basis(rows)
    count = sums[7:8]
    accel = (-0.5 * K_SCALE) * (full[0:3] * count - sums[0:3])
    mixed = jnp.sum(full[3:6] * sums[0:3] + full[0:3] * sums[3:6], axis=0, keepdims=True)
    heat = (0.25 * K_SCALE) * (cross * count - mixed + sums[6:7])
    return jnp.concatenate([accel, heat], axis=0)


def own_force_kernel(
    after, state, fluid, counts, pair_first, pair_offset, at, as_, bh, total,
    acc1, acc2, bd, bs, cf, row, col, dist0, dist1, appr0, appr1, ws0, ws1, pa, po, ps,
):
    del after

    def mine(c, _):
        rows = state[c]
        fluid_prepare(c, rows, geometry_prepare(c, rows, bd, bs), fluid[c], cf, row)
        own_fluid_columns(c, row, col)
        return 0

    lax.fori_loop(0, CELLS, mine, 0, unroll=2)
    own_lists(pair_first, pair_offset, pa, po, ps, CELLS)
    acc1[...] = jnp.zeros_like(acc1)
    acc2[...] = jnp.zeros_like(acc2)
    ws0[...] = jnp.zeros_like(ws0)
    ws1[...] = jnp.zeros_like(ws1)
    refs = (bd, bs, cf, cf, at, as_, bh, row, col, (dist0, dist1), (appr0, appr1), (ws0, ws1))
    full_force(
        0, CELLS + PAIRS, counts, lambda p: pa[p], lambda p: po[p], lambda p: ps[p], refs,
        lambda p: None, acc1, acc2,
    )
    total[...] = acc1[...] + acc2[0:CELLS]


def far_force_kernel(
    state, fluid, blocks, far_fluid, counts, slot, offset, block_own, live, size, at, as_, bh,
    ready0, ready1, acc1, ret,
    acc2, fluids, bd, bs, own_cf, own_row, cf, row, col,
    dist0, dist1, appr0, appr1, ws0, ws1, buf, sems,
):
    total = size[0]
    half = ready0.shape[0] // 2
    steps = jnp.minimum(total, ready0.shape[0] + ready1.shape[0]) // 2

    def start(t):
        k = lax.rem(t, DEPTH)

        @pl.when(t < half)
        def _():
            pltpu.make_async_copy(ready0.at[pl.ds(2 * t, 2)], buf.at[k], sems.at[k]).start()

        @pl.when(t >= half)
        def _():
            pltpu.make_async_copy(
                ready1.at[pl.ds(2 * (t - half), 2)], buf.at[k], sems.at[k]
            ).start()

    def wait(t):
        k = lax.rem(t, DEPTH)
        pltpu.make_async_copy(ready0.at[pl.ds(0, 2)], buf.at[k], sems.at[k]).wait()

    for t in range(DEPTH - 1):
        pl.when(t < steps)(lambda t=t: start(t))

    def mine(c, _):
        rows = state[c]
        fluid_prepare(c, rows, basis(rows)[0], fluid[c], own_cf, own_row)
        own_fluid_columns(c, own_row, col)
        return 0

    lax.fori_loop(0, CELLS, mine, 0, unroll=2)
    fluids[...] = jnp.ones_like(fluids)

    def fill(e, _):
        pack(fluids, far_fluid[slot[e]], offset[e], live[e])
        return 0

    lax.fori_loop(0, SEND, fill, 0, unroll=8)
    acc1[...] = jnp.zeros_like(acc1)
    acc2[...] = jnp.zeros_like(acc2)
    ws0[...] = jnp.zeros_like(ws0)
    ws1[...] = jnp.zeros_like(ws1)
    ws = (ws0, ws1)

    def prepare(p):
        rows = blocks[p]
        fluid_prepare(p, rows, basis(rows)[0], fluids[p], cf, row)

    last = 2 * steps - 1
    for k in range(2):
        prepare(jnp.int32(k))

    def combine(p, side):
        return force_combine(own_cf[block_own[p]], cf[p], ws[side])

    def store(p, sums, valid):
        keep_sums(acc1, acc2, block_own[p], p, sums, valid)

    def body(t, _):
        p = 2 * t
        k = lax.rem(t, DEPTH)
        pl.when(t + DEPTH - 1 < steps)(lambda: start(t + DEPTH - 1))
        wait(t)

        def work(p, side, rows):
            def grads(c):
                return buf[k, side, 0, c : c + CHUNK, :], buf[k, side, 1, c : c + CHUNK, :]

            fluid_work(ws[side], col, row[p], block_own[p], rows, grads)

        def step(rows):
            before = jnp.maximum(p - 1, 0)
            sums = combine(before, 1)
            work(p, 0, rows)
            sums0 = combine(p, 0)
            work(p + 1, 1, rows)
            store(before, sums, t > 0)
            store(p, sums0, True)
            prepare(jnp.minimum(p + 2, last))
            prepare(jnp.minimum(p + 3, last))

        by_rows(jnp.maximum(counts[block_own[p]], counts[block_own[p + 1]]), step)
        return 0

    lax.fori_loop(0, steps, body, 0)
    store(last, combine(last, 1), True)

    @pl.when(total > 2 * steps)
    def _():
        def rest(p):
            rows = blocks[p]
            fluid_prepare(p, rows, geometry_prepare(p, rows, bd, bs), fluids[p], cf, row)

        refs = (
            bd, bs, own_cf, cf, at, as_, bh, row, col, (dist0, dist1), (appr0, appr1), ws,
        )
        same = lambda p: p
        full_force(
            2 * steps, total - 2 * steps, counts, lambda p: block_own[p], same, same, refs,
            rest, acc1, acc2,
        )

    def turn(t, _):
        acc2[t, 0:4] = force_sums(blocks[t], acc2[t])
        return 0

    lax.fori_loop(0, total // 2, lambda t, _: turn(2 * t, 0) + turn(2 * t + 1, 0), 0)

    def back(e, _):
        ret[slot[e]] = unpack(acc2, offset[e])[0:4]
        return 0

    lax.fori_loop(0, SEND, back, 0, unroll=8)


def finish_kernel(
    back, goals, near, far, state, energy, counts, mig_cell, mig_dest, accel, leave, sums, moved, used
):
    sums[...] = jnp.zeros_like(sums)

    def one(s, _):
        goal = goals[s]
        sums[jnp.where(goal < 0, CELLS, goal)] += back[s]
        return 0

    lax.fori_loop(0, back.shape[0], one, 0, unroll=2)
    lane = lax.broadcasted_iota(i32, (1, PART), 1)

    def cell(c, _):
        rows = state[c]
        here = lane < counts[c]
        total = jnp.where(here, force_sums(rows, near[c] + far[c]) + sums[c], 0.0)
        accel[c] = total
        new_vel = rows[3:6] + STEP * total[0:3]
        new_pos = rows[0:3] + STEP * new_vel
        new_energy = energy[pl.ds(c, 1), :] + STEP * total[3:4]
        kicked = jnp.concatenate(
            [new_pos, new_vel, rows[7:8], rows[6:7], new_energy], axis=0
        )
        moved[c] = jnp.where(here, kicked, 0.0)
        return 0

    lax.fori_loop(0, CELLS, cell, 0)
    leave[...] = jnp.zeros_like(leave)

    def clear(d, _):
        used[d] = 0
        return 0

    lax.fori_loop(0, leave.shape[0] // CAPM, clear, 0)

    def entry(e, _):
        d = mig_dest[e]
        k = used[d]
        used[d] = k + 1
        leave[d * CAPM + k] = moved[mig_cell[e]]
        return 0

    lax.fori_loop(0, mig_cell.shape[0], entry, 0)


def vmem(*dims, dtype=f32):
    return pltpu.VMEM(dims, dtype)


def smem(*dims):
    return pltpu.SMEM(dims, i32)


WS = [vmem(2 * PART, PART, dtype=bf16)] * 2
SQUARE = [vmem(PART, PART)] * 2


def own_density(state, counts, pair_first, pair_offset):
    return kernel_call(
        own_density_kernel,
        (
            shape(CELLS, 8, PART),
            shape(CELLS, PART, 48, dtype=bf16),
            shape(CELLS, PART, 48, dtype=bf16),
            shape(CELLS, PART, 128),
            shape(CELLS, 16, PART, dtype=bf16),
        ),
        [VMEM] + [SMEM] * 3,
        (VMEM,) * 5,
        [
            vmem(CELLS, 8, PART),
            vmem(CELLS + 1, 8, PART),
            vmem(CELLS, 48, PART, dtype=bf16),
            vmem(CELLS, 1, PART),
        ]
        + SQUARE
        + WS
        + [smem(CELLS + PAIRS)] * 3,
        flops=32 * PART * PART * 300,
        moved=2**20,
    )(state, counts, pair_first, pair_offset)


def far_density(state, far, counts, slot, proxy_cell, at, bh, own_m):
    return kernel_call(
        far_density_kernel,
        (
            shape(CELLS, 8, PART),
            shape(far.shape[0], 1, PART),
            shape(BLOCKS + 1, 8, PART),
            shape(SEND, dtype=i32),
            shape(BLOCKS, dtype=i32),
            shape(SEND, dtype=i32),
            shape(1, dtype=i32),
        ),
        [VMEM] * 2 + [SMEM] * 3 + [VMEM] * 3,
        (VMEM,) * 3 + (SMEM,) * 4,
        [
            vmem(BLOCKS + 1, 8, PART),
            vmem(BLOCKS, 48, PART, dtype=bf16),
            vmem(BLOCKS, 16, PART, dtype=bf16),
            vmem(BLOCKS, 1, PART),
        ]
        + SQUARE
        + WS
        + [smem(CELLS)],
        flops=128 * PART * PART * 300,
        moved=2**20,
    )(state, far, counts, slot, proxy_cell, at, bh, own_m)


def slopes(after, first, count, blocks, counts, block_own, size, at, as_, bh):
    def body(*refs):
        slope_kernel(*refs, first=first)

    return kernel_call(
        body,
        shape(count, 2, PART, PART),
        [ANY, VMEM] + [SMEM] * 3 + [VMEM] * 3,
        ANY,
        [
            vmem(count, 48, PART, dtype=bf16),
            vmem(count, 48, PART, dtype=bf16),
            vmem(count, 1, PART),
        ]
        + SQUARE * 2
        + [vmem(DEPTH, 2, 2, PART, PART), pltpu.SemaphoreType.DMA((DEPTH,))],
        flops=count * PART * PART * 400,
        moved=count * 2**19,
    )(after, blocks, counts, block_own, size, at, as_, bh)


def far_force(
    state, fluid, far_fluid, counts, slot, blocks, offset, block_own, live, size, at, as_, bh,
    ready0, ready1,
):
    return kernel_call(
        far_force_kernel,
        (shape(CELLS, 8, PART), shape(far_fluid.shape[0], 4, PART)),
        [VMEM] * 4 + [SMEM] * 6 + [VMEM] * 3 + [ANY] * 2,
        (VMEM, VMEM),
        [
            vmem(BLOCKS + 1, 8, PART),
            vmem(BLOCKS + 1, 2, PART),
            vmem(BLOCKS, 48, PART, dtype=bf16),
            vmem(BLOCKS, 48, PART, dtype=bf16),
            vmem(CELLS, 24, PART, dtype=bf16),
            vmem(CELLS, 8, PART),
            vmem(BLOCKS, 24, PART, dtype=bf16),
            vmem(BLOCKS, 8, PART),
            vmem(CELLS, 3, PART, 128),
        ]
        + SQUARE * 2
        + WS
        + [vmem(DEPTH, 2, 2, PART, PART), pltpu.SemaphoreType.DMA((DEPTH,))],
        flops=128 * PART * PART * 300,
        moved=2**20,
    )(
        state, fluid, blocks, far_fluid, counts, slot, offset, block_own, live, size,
        at, as_, bh, ready0, ready1,
    )


def own_force(after, state, fluid, counts, pair_first, pair_offset, at, as_, bh):
    return kernel_call(
        own_force_kernel,
        shape(CELLS, 8, PART),
        [ANY] + [VMEM] * 2 + [SMEM] * 3 + [VMEM] * 3,
        VMEM,
        [
            vmem(CELLS, 8, PART),
            vmem(CELLS + 1, 8, PART),
            vmem(CELLS, 48, PART, dtype=bf16),
            vmem(CELLS, 48, PART, dtype=bf16),
            vmem(CELLS, 24, PART, dtype=bf16),
            vmem(CELLS, 8, PART),
            vmem(CELLS, 3, PART, 128),
        ]
        + SQUARE * 2
        + WS
        + [smem(CELLS + PAIRS)] * 3,
        flops=32 * PART * PART * 600,
        moved=2**20,
    )(after, state, fluid, counts, pair_first, pair_offset, at, as_, bh)


def exchange(x, axes):
    return lax.all_to_all(x, axes, split_axis=0, concat_axis=0, tiled=True)


def local(
    position, velocity, mass, smoothing, energy, counts, proxy_cell, proxy_dest,
    proxy_target, pair_first, pair_offset, mig_cell, mig_dest,
):
    devices = lax.axis_size(("rows", "cols"))
    col_count = lax.axis_size("cols")
    slots = devices * CAP
    both = ("rows", "cols")
    state, req, slot = kernel_call(
        request_kernel,
        (shape(CELLS, 8, PART), shape(devices, 1, 128, dtype=i32), shape(SEND, dtype=i32)),
        [VMEM] * 4 + [SMEM] * 3,
        (VMEM, VMEM, SMEM),
        [pltpu.SMEM((devices,), i32)],
        moved=2**20,
    )(position, velocity, mass, smoothing, counts, proxy_dest[:, 0], proxy_target)
    goals = exchange(req, both)[:, 0, 0:CAP].reshape(slots)
    near, at, as_, bh, own_m = own_density(state, counts, pair_first, pair_offset)
    answer = kernel_call(
        respond_kernel, shape(slots, 8, PART), [VMEM, SMEM], VMEM, moved=4 * 2**20
    )(state, goals)
    far = exchange(answer, both)
    far_sums, ret, *plan = far_density(state, far, counts, slot, proxy_cell, at, bh, own_m)
    blocks, offset, block_own, live, size = plan
    ready0 = slopes(far_sums, 0, EARLY, blocks, counts, block_own, size, at, as_, bh)
    back = exchange(ret, both)
    density, fluid, answer2 = kernel_call(
        combine_density_kernel,
        (shape(CELLS, PART), shape(CELLS, 2, PART), shape(slots, 2, PART)),
        [VMEM, SMEM] + [VMEM] * 3 + [SMEM],
        (VMEM, VMEM, VMEM),
        [pltpu.VMEM((CELLS + 1, 1, PART), f32)],
        moved=2**20,
    )(back, goals, near, far_sums, energy, counts)
    far_fluid = exchange(answer2, both)
    ready1 = slopes(fluid, EARLY, LATE, blocks, counts, block_own, size, at, as_, bh)
    far_force_sums, ret4 = far_force(
        state, fluid, far_fluid, counts, slot, *plan, at, as_, bh, ready0, ready1
    )
    near_force = own_force(
        far_force_sums, state, fluid, counts, pair_first, pair_offset, at, as_, bh
    )
    back4 = exchange(ret4, both)
    accel, leave = kernel_call(
        finish_kernel,
        (shape(CELLS, 4, PART), shape(col_count * CAPM, 9, PART)),
        [VMEM, SMEM] + [VMEM] * 4 + [SMEM] * 3,
        (VMEM, VMEM),
        [
            pltpu.VMEM((CELLS + 1, 4, PART), f32),
            pltpu.VMEM((CELLS, 9, PART), f32),
            pltpu.SMEM((col_count,), i32),
        ],
        moved=2**20,
    )(back4, goals, near_force, far_force_sums, state, energy, counts, mig_cell, mig_dest[:, 0])
    arrived = exchange(leave, "cols")
    return (density, accel, arrived)


def solution(mesh):
    lead = ("rows", "cols")
    one, two, three = P(lead), P(lead, None), P(lead, None, None)
    return jax.shard_map(
        local,
        mesh=mesh,
        in_specs=(three, three, two, two, two, one, one, two, one, one, one, one, two),
        out_specs=(two, three, three),
        check_vma=False,
    )
```

```python
import jax
import jax.numpy as jnp
from jax import lax
from jax.experimental import pallas as pl
from jax.experimental.pallas import tpu as pltpu
from jax.sharding import PartitionSpec as P

CAP = 2
CAPM = 2
CELLS = 16
SEND = 128
PAIRS = 16
PART = 256

GAMMA = 5.0 / 3.0
STEP = 0.02
PI = 3.141592653589793
W_SCALE = 2.0 / PI
K_SCALE = -24.0 / PI
TINY = 1e-12
CHUNK = 32
ROWS = (128, 160, 192, 224, 256)
BLOCKS = SEND + CELLS
EARLY, LATE = 42, 50
DEPTH = 4

f32, bf16, i32 = jnp.float32, jnp.bfloat16, jnp.int32
VMEM = pl.BlockSpec(memory_space=pltpu.VMEM)
ANY = pl.BlockSpec(memory_space=pl.ANY)
SMEM = pl.BlockSpec(memory_space=pltpu.SMEM)
LIMIT = 56 * 2**20


def shape(*dims, dtype=f32):
    return jax.ShapeDtypeStruct(dims, dtype)


def kernel_call(body, out_shape, in_specs, out_specs, scratch=(), flops=0, moved=0):
    return pl.pallas_call(
        body,
        out_shape=out_shape,
        in_specs=in_specs,
        out_specs=out_specs,
        scratch_shapes=list(scratch),
        compiler_params=pltpu.CompilerParams(vmem_limit_bytes=LIMIT),
        cost_estimate=pl.CostEstimate(flops=flops, bytes_accessed=moved, transcendentals=0),
    )


def sublane():
    return lax.broadcasted_iota(i32, (8, PART), 0)


def split3(x):
    a = x.astype(bf16).astype(f32)
    b = (x - a).astype(bf16).astype(f32)
    return a, b, x - a - b


def left_parts(x):
    a, b, c = split3(x)
    return [a, a, b, b, a, c]


def right_parts(x):
    a, b, c = split3(x)
    return [a, b, a, b, c, a]


def stack16(parts):
    return jnp.concatenate(parts, axis=0).astype(bf16)


def basis(rows):
    row = sublane()
    place = jnp.where(row < 3, 2.0 * rows - 1.0, rows)
    first = place[0:3]
    norm = jnp.sum(first * first, axis=0, keepdims=True)
    cross = jnp.sum(first * place[3:6], axis=0, keepdims=True)
    full = jnp.where(row < 6, place, jnp.where(row == 6, cross, 1.0))
    return full, norm, cross


def right_distance(full, norm):
    row = sublane()
    return jnp.where(
        row < 3, full, jnp.where(row == 3, norm, jnp.where(row == 4, 1.0, 0.0))
    )


def left_distance(full, norm):
    row = sublane()
    return jnp.where(
        row < 3, -2.0 * full, jnp.where(row == 3, 1.0, jnp.where(row == 4, norm, 0.0))
    )


def left_approach(full, cross):
    return 4.0 * jnp.concatenate(
        [-full[3:6], -full[0:3], jnp.ones((1, PART), f32), cross], axis=0
    )


def columns(parts):
    fill = 128 - 8 * len(parts)
    return jnp.concatenate(parts + [jnp.zeros((fill, PART), f32)], axis=0).T


def halves(w):
    hi = w.astype(bf16)
    return hi, (w - hi.astype(f32)).astype(bf16)


def request_kernel(dest, target, req, slot, used):
    req[...] = jnp.full_like(req, -1)

    def clear(d, _):
        used[d] = 0
        return 0

    lax.fori_loop(0, req.shape[0], clear, 0, unroll=8)
    short = lax.broadcasted_iota(i32, (1, 128), 1)

    def entry(e, _):
        d = dest[e]
        k = used[d]
        used[d] = k + 1
        slot[e] = d * CAP + k
        req[d] = jnp.where(short == k, target[e], req[d])
        return 0

    lax.fori_loop(0, SEND, entry, 0, unroll=4)


def respond_kernel(state, goals, out):
    def one(s, _):
        goal = jnp.maximum(goals[s], 0)
        out[s] = state[goal]
        return 0

    lax.fori_loop(0, out.shape[0], one, 0, unroll=4)


def by_rows(need, step):
    low = 0
    for rows in ROWS:
        pl.when((need > low) & (need <= rows))(lambda rows=rows: step(rows))
        low = rows


def pipeline(first, count, rows_of, prepare, load, combine, store, work):
    last = first + count - 1

    def clamp(p):
        return jnp.minimum(p, last)

    for k in range(3):
        prepare(clamp(first + k))
    load(first, 0)

    def body(t, _):
        p = first + 2 * t

        def step(rows):
            before = jnp.maximum(p - 1, first)
            sums = combine(before, 1)
            work(p, 0, rows)
            load(p + 1, 1)
            sums0 = combine(p, 0)
            work(p + 1, 1, rows)
            load(clamp(p + 2), 0)
            store(before, sums, t > 0)
            store(p, sums0, True)
            prepare(clamp(p + 3))
            prepare(clamp(p + 4))

        by_rows(jnp.maximum(rows_of(p), rows_of(p + 1)), step)
        return 0

    lax.fori_loop(0, count // 2, body, 0)
    store(last, combine(last, 1), True)


def keep_sums(acc1, acc2, a, s, sums, valid):
    if valid is not True:
        keep = jnp.where(valid, 1.0, 0.0)
        sums = (sums[0] * keep, sums[1] * keep)
    acc1[a] += sums[0]
    acc2[s] += sums[1]


def pack_plan(far, slot, proxy_cell, offset, block_own, live, filled):
    def clear(c, _):
        filled[c] = 0
        return 0

    lax.fori_loop(0, CELLS, clear, 0)

    def measure(e, _):
        mass = far[slot[e]][7:8]
        n = jnp.sum(jnp.where(mass > 0.0, 1.0, 0.0)).astype(i32)
        live[e] = n
        a = proxy_cell[e]
        offset[e] = filled[a]
        filled[a] = filled[a] + n
        return 0

    lax.fori_loop(0, SEND, measure, 0, unroll=16)

    def place(c, total):
        blocks = (filled[c] + PART - 1) // PART
        filled[c] = total * PART

        def name(t, _):
            block_own[total + t] = c
            return 0

        lax.fori_loop(0, blocks, name, 0)
        return total + blocks

    total = lax.fori_loop(0, CELLS, place, 0)

    def shift(e, _):
        offset[e] = offset[e] + filled[proxy_cell[e]]
        return 0

    lax.fori_loop(0, SEND, shift, 0, unroll=8)
    block_own[total] = block_own[total - 1]
    return total + lax.rem(total, 2)


def pack(target, rows, offset, n):
    t = offset // PART
    lane0 = offset - t * PART
    lane = lax.broadcasted_iota(i32, rows.shape, 1)
    turned = pltpu.roll(rows, lane0, 1)
    pltpu.store(target.at[t], turned, mask=(lane >= lane0) & (lane < lane0 + n))
    pltpu.store(target.at[t + 1], turned, mask=lane < lane0 + n - PART)


def unpack(source, offset):
    t = offset // PART
    lane0 = offset - t * PART
    first, second = source[t], source[t + 1]
    lane = lax.broadcasted_iota(i32, first.shape, 1)
    return pltpu.roll(jnp.where(lane >= lane0, first, second), lax.rem(PART - lane0, PART), 1)


def own_lists(pair_first, pair_offset, pa, po, ps, dummy):
    def one(e, _):
        pa[e] = e
        po[e] = e
        ps[e] = dummy
        a = pair_first[e]
        b = lax.rem(a + pair_offset[e], CELLS)
        pa[CELLS + e] = a
        po[CELLS + e] = b
        ps[CELLS + e] = b
        return 0

    lax.fori_loop(0, CELLS, one, 0)


def nn(a, b):
    return jnp.dot(a, b, preferred_element_type=f32)


def nt(a, b):
    return lax.dot_general(a, b, (((1,), (1,)), ((), ())), preferred_element_type=f32)


def density_weights(r2, total_h):
    inv = pltpu.reciprocal(total_h, approx=True)
    inv2 = inv * inv
    q2 = jnp.maximum(r2, TINY) * inv2
    q = q2 * lax.rsqrt(q2)
    u = 2.0 - q
    t = jnp.maximum(u, 0.0)
    return jnp.minimum(t * t * t, 4.0 - 3.0 * (q2 * u)) * (inv2 * inv)


def two_wide(col, row):
    return jnp.concatenate([col, col], axis=1) + row


def density_pairs(count, counts, pa, po, ps, refs, prepare, acc1, acc2):
    bf, hj, mj, at, bh, bm, dist = refs

    def load(p, side):
        dist[side][...] = nn(at[pa(p)], bf[po(p)])

    def work(p, side, rows):
        a, o = pa(p), po(p)
        h_j, m_j = hj[o], mj[o]
        second = jnp.zeros((8, PART), f32)
        for c in range(0, rows, CHUNK):
            w = density_weights(
                dist[side][c : c + CHUNK, :], two_wide(bh[a, c : c + CHUNK, :], h_j)
            )
            first = w * m_j
            acc1[a, c : c + CHUNK, :] += first[:, 0:128] + first[:, 128:256]
            m_i = bm[a, c : c + CHUNK, :]
            other = w * jnp.concatenate([m_i, m_i], axis=1)
            second += jnp.sum(other.reshape(CHUNK // 8, 8, PART), axis=0)
        acc2[ps(p)] += jnp.sum(second, axis=0, keepdims=True)

    last = count - 1

    def clamp(p):
        return jnp.minimum(p, last)

    for k in range(3):
        prepare(clamp(k))
    load(0, 0)

    def body(t, _):
        p = 2 * t

        def step(rows):
            load(p + 1, 1)
            work(p, 0, rows)
            work(p + 1, 1, rows)
            load(clamp(p + 2), 0)
            prepare(clamp(p + 3))
            prepare(clamp(p + 4))

        by_rows(jnp.maximum(counts[pa(p)], counts[pa(p + 1)]), step)
        return 0

    lax.fori_loop(0, count // 2, body, 0)


def column_sums(x):
    return jnp.sum(x.T, axis=0, keepdims=True)


def expand(cols, at, as_, bh, bm):
    def one(c, _):
        t = cols[c]
        at[c] = t[:, 0:48].astype(bf16)
        if as_ is not None:
            as_[c] = t[:, 56:104].astype(bf16)
        bh[c] = jnp.broadcast_to(t[:, 54:55], (PART, 128))
        if bm is not None:
            bm[c] = jnp.broadcast_to(t[:, 55:56], (PART, 128))
        return 0

    lax.fori_loop(0, CELLS, one, 0, unroll=2)


def density_prepare(o, rows, bf, hj, mj):
    full, norm, cross = basis(rows)
    bf[o] = stack16(right_parts(right_distance(full, norm)))
    hj[o] = rows[6:7]
    mj[o] = rows[7:8]
    return full, norm, cross


def own_density_kernel(
    pos, vel, mass, smooth, counts, pair_first, pair_offset, near, state, cols,
    acc1, acc2, at, bh, bm, bf, hj, mj, dist0, dist1, pa, po, ps,
):
    lane = lax.broadcasted_iota(i32, (1, PART), 1)

    def mine(c, _):
        live = jnp.where(lane < counts[c], mass[pl.ds(c, 1), :], 0.0)
        rows = jnp.concatenate([pos[c], vel[c], smooth[pl.ds(c, 1), :], live], axis=0)
        state[c] = rows
        full, norm, cross = density_prepare(c, rows, bf, hj, mj)
        cols[c] = columns(
            left_parts(left_distance(full, norm))
            + [rows]
            + left_parts(left_approach(full, cross))
        )
        return 0

    lax.fori_loop(0, CELLS, mine, 0, unroll=2)
    expand(cols, at, None, bh, bm)
    own_lists(pair_first, pair_offset, pa, po, ps, CELLS)
    acc1[...] = jnp.zeros_like(acc1)
    acc2[...] = jnp.zeros_like(acc2)
    refs = (bf, hj, mj, at, bh, bm, (dist0, dist1))
    density_pairs(
        CELLS + PAIRS, counts, lambda p: pa[p], lambda p: po[p], lambda p: ps[p], refs,
        lambda p: None, acc1, acc2,
    )

    def total(c, _):
        near[c] = column_sums(acc1[c]) + acc2[c]
        return 0

    lax.fori_loop(0, CELLS, total, 0, unroll=2)


def far_density_kernel(
    far, counts, slot, proxy_cell, cols,
    acc1, ret, blocks, offset, block_own, live, size,
    acc2, at, bh, bm, bf, hj, mj, dist0, dist1, filled,
):
    total = pack_plan(far, slot, proxy_cell, offset, block_own, live, filled)
    size[0] = total
    expand(cols, at, None, bh, bm)
    blocks[...] = jnp.zeros_like(blocks)

    def fill(e, _):
        pack(blocks, far[slot[e]], offset[e], live[e])
        return 0

    lax.fori_loop(0, SEND, fill, 0, unroll=8)
    acc2[...] = jnp.zeros_like(acc2)
    acc1[...] = jnp.zeros_like(acc1)
    refs = (bf, hj, mj, at, bh, bm, (dist0, dist1))
    same = lambda p: p
    density_pairs(
        total, counts, lambda p: block_own[p], same, same, refs,
        lambda p: density_prepare(p, blocks[p], bf, hj, mj), acc1, acc2,
    )

    def back(e, _):
        ret[slot[e]] = unpack(acc2, offset[e])
        return 0

    lax.fori_loop(0, SEND, back, 0, unroll=8)


def add_by_goal(back, goals, sums):
    for part in sums:
        part[...] = jnp.zeros_like(part)

    def one(t, _):
        for k, part in enumerate(sums):
            s = t * len(sums) + k
            goal = goals[s]
            part[jnp.where(goal < 0, CELLS, goal)] += back[s]
        return 0

    lax.fori_loop(0, back.shape[0] // len(sums), one, 0, unroll=2)


def combine_density_kernel(
    after, back, goals, near, far, energy, counts, density, fluid, answer, *sums
):
    del after
    add_by_goal(back, goals, sums)
    lane = lax.broadcasted_iota(i32, (1, PART), 1)

    def cell(c, _):
        raw = W_SCALE * (near[c] + far[c] + sum(part[c] for part in sums))
        here = lane < counts[c]
        density[pl.ds(c, 1), :] = jnp.where(here, raw, 0.0)
        fluid[c] = jnp.concatenate(
            [jnp.where(here, raw, 1.0), energy[pl.ds(c, 1), :]], axis=0
        )
        return 0

    lax.fori_loop(0, CELLS, cell, 0, unroll=4)

    def send(s, _):
        answer[s] = fluid[jnp.maximum(goals[s], 0)]
        return 0

    lax.fori_loop(0, answer.shape[0], send, 0, unroll=8)


def slope_weights(r2, s, total_h):
    inv = pltpu.reciprocal(total_h, approx=True)
    inv2 = inv * inv
    q2 = jnp.maximum(r2, TINY) * inv2
    rs = lax.rsqrt(q2)
    q = q2 * rs
    u = 2.0 - q
    t = jnp.maximum(u, 0.0)
    grad = jnp.where(q < 1.0, 3.0 * u - 2.0, t * t * rs)
    m = jnp.minimum(s, 0.0) * (inv * pltpu.reciprocal(q2 + 0.01, approx=True))
    return grad * (inv2 * inv2 * inv), m


def fluid_weights(grad, m, total_c, total_p, total_r):
    return (total_p + m * (m - total_c) * pltpu.reciprocal(total_r, approx=True)) * grad


def force_fluid(fluid):
    rho, u = fluid[0:1], fluid[1:2]
    pressure = (GAMMA - 1.0) * u / rho
    sound = jnp.sqrt(GAMMA * (GAMMA - 1.0) * u)
    return pressure, sound, 4.0 * rho


def put_halves(ws, c, w):
    hi, lo = halves(w)
    ws[c : c + CHUNK, :] = hi
    ws[PART + c : PART + c + CHUNK, :] = lo


def fluid_work(ws, col, side_row, a, rows, grads):
    for c in range(0, rows, CHUNK):
        grad, m = grads(c)
        total = [
            two_wide(col[a, k, c : c + CHUNK, :], side_row[k + 1 : k + 2]) for k in range(3)
        ]
        put_halves(ws, c, fluid_weights(grad, m, *total))


def fold(x):
    return x[0:8] + x[8:16] + x[16:24]


def force_combine(own, other, ws):
    second = fold(nn(jnp.concatenate([own, own], axis=1), ws[...]))
    first = fold(nt(other, ws[...]))
    return first[:, 0:PART] + first[:, PART:], second


def full_force(first, count, counts, pa, po, refs, prepare, store):
    bd, bs, own_cf, other_cf, at, as_, bh, row, col, dist, appr, ws = refs

    def load(p, side):
        a, o = pa(p), po(p)
        dist[side][...] = nn(at[a], bd[o])
        appr[side][...] = nn(as_[a], bs[o])

    def work(p, side, rows):
        a = pa(p)
        side_row = row[po(p)]

        def grads(c):
            return slope_weights(
                dist[side][c : c + CHUNK, :],
                appr[side][c : c + CHUNK, :],
                two_wide(bh[a, c : c + CHUNK, :], side_row[0:1]),
            )

        fluid_work(ws[side], col, side_row, a, rows, grads)

    def combine(p, side):
        return force_combine(own_cf[pa(p)], other_cf[po(p)], ws[side])

    pipeline(first, count, lambda p: counts[pa(p)], prepare, load, combine, store, work)


def geometry_prepare(o, rows, bd, bs):
    full, norm, cross = basis(rows)
    bd[o] = stack16(right_parts(right_distance(full, norm)))
    bs[o] = stack16(right_parts(full))
    return full


def fluid_prepare(o, rows, full, fluid, cf, row):
    cf[o] = stack16(list(split3(rows[7:8] * full)))
    pressure, sound, rho4 = force_fluid(fluid)
    row[o] = jnp.concatenate(
        [rows[6:7], sound, pressure, rho4, jnp.zeros((4, PART), f32)], axis=0
    )


def own_fluid_columns(c, row, col):
    t = columns([row[c]])
    for k in range(3):
        col[c, k] = jnp.broadcast_to(t[:, k + 1 : k + 2], (PART, 128))


def slope_kernel(
    fluid, acc1, blocks, counts, block_own, size, cols, out, far_sums,
    at, as_, bh, bd, bs, hj, dist0, dist1, appr0, appr1, buf, sems, *, first,
):
    del fluid
    expand(cols, at, as_, bh, None)
    if first == 0:

        def total(c, _):
            far_sums[c] = column_sums(acc1[c])
            return 0

        lax.fori_loop(0, CELLS, total, 0, unroll=2)
    else:
        far_sums[...] = jnp.zeros_like(far_sums)
    dist, appr = (dist0, dist1), (appr0, appr1)
    count = jnp.clip(size[0] - first, 0, out.shape[0])
    last = first + count - 1

    def clamp(p):
        return jnp.minimum(p, last)

    def prepare(p):
        rows = blocks[p]
        geometry_prepare(p - first, rows, bd, bs)
        hj[p - first] = rows[6:7]

    def load(p, side):
        a = block_own[p]
        dist[side][...] = nn(at[a], bd[p - first])
        appr[side][...] = nn(as_[a], bs[p - first])

    def copy(t):
        k = lax.rem(t, DEPTH)
        return pltpu.make_async_copy(buf.at[k], out.at[pl.ds(2 * t, 2)], sems.at[k])

    def work(p, side, rows, k):
        a = block_own[p]
        h_j = hj[p - first]
        for c in range(0, rows, CHUNK):
            grad, m = slope_weights(
                dist[side][c : c + CHUNK, :],
                appr[side][c : c + CHUNK, :],
                two_wide(bh[a, c : c + CHUNK, :], h_j),
            )
            buf[k, side, 0, c : c + CHUNK, :] = grad
            buf[k, side, 1, c : c + CHUNK, :] = m

    @pl.when(count > 0)
    def _():
        for k in range(3):
            prepare(clamp(first + k))
        load(first, 0)

    def body(t, _):
        p = first + 2 * t
        k = lax.rem(t, DEPTH)
        pl.when(t >= DEPTH)(lambda: copy(t - DEPTH).wait())

        def step(rows):
            load(p + 1, 1)
            work(p, 0, rows, k)
            work(p + 1, 1, rows, k)
            load(clamp(p + 2), 0)
            prepare(clamp(p + 3))
            prepare(clamp(p + 4))

        by_rows(jnp.maximum(counts[block_own[p]], counts[block_own[p + 1]]), step)
        copy(t).start()
        return 0

    steps = count // 2
    lax.fori_loop(0, steps, body, 0)

    def drain(t, _):
        copy(t).wait()
        return 0

    lax.fori_loop(jnp.maximum(steps - DEPTH, 0), steps, drain, 0)


def force_sums(rows, sums):
    full, _, cross = basis(rows)
    count = sums[7:8]
    accel = (-0.5 * K_SCALE) * (full[0:3] * count - sums[0:3])
    mixed = jnp.sum(full[3:6] * sums[0:3] + full[0:3] * sums[3:6], axis=0, keepdims=True)
    heat = (0.25 * K_SCALE) * (cross * count - mixed + sums[6:7])
    return jnp.concatenate([accel, heat], axis=0)


def own_force_kernel(
    after, state, fluid, counts, pair_first, pair_offset, cols, total,
    acc1, acc2, at, as_, bh, bd, bs, cf, row, col, dist0, dist1, appr0, appr1, ws0, ws1, pa, po, ps,
):
    del after
    expand(cols, at, as_, bh, None)

    def mine(c, _):
        rows = state[c]
        fluid_prepare(c, rows, geometry_prepare(c, rows, bd, bs), fluid[c], cf, row)
        own_fluid_columns(c, row, col)
        return 0

    lax.fori_loop(0, CELLS, mine, 0, unroll=2)
    own_lists(pair_first, pair_offset, pa, po, ps, CELLS)
    acc1[...] = jnp.zeros_like(acc1)
    acc2[...] = jnp.zeros_like(acc2)
    ws0[...] = jnp.zeros_like(ws0)
    ws1[...] = jnp.zeros_like(ws1)
    refs = (bd, bs, cf, cf, at, as_, bh, row, col, (dist0, dist1), (appr0, appr1), (ws0, ws1))
    full_force(
        0, CELLS + PAIRS, counts, lambda p: pa[p], lambda p: po[p], refs, lambda p: None,
        lambda p, sums, valid: keep_sums(acc1, acc2, pa[p], ps[p], sums, valid),
    )
    total[...] = acc1[...] + acc2[0:CELLS]


def far_force_kernel(
    state, fluid, blocks, far_fluid, counts, slot, offset, block_own, live, size, cols_far,
    ready0, ready1, acc1, ret,
    acc2, cols, at, as_, bh, fluids, bd, bs, own_cf, own_row, cf, row, col,
    dist0, dist1, appr0, appr1, ws0, ws1, buf, sems,
):
    total = size[0]
    half = ready0.shape[0] // 2
    steps = jnp.minimum(total, ready0.shape[0] + ready1.shape[0]) // 2

    def start(t):
        k = lax.rem(t, DEPTH)

        @pl.when(t < half)
        def _():
            pltpu.make_async_copy(ready0.at[pl.ds(2 * t, 2)], buf.at[k], sems.at[k]).start()

        @pl.when(t >= half)
        def _():
            pltpu.make_async_copy(
                ready1.at[pl.ds(2 * (t - half), 2)], buf.at[k], sems.at[k]
            ).start()

    def wait(t):
        k = lax.rem(t, DEPTH)
        pltpu.make_async_copy(ready0.at[pl.ds(0, 2)], buf.at[k], sems.at[k]).wait()

    for t in range(DEPTH - 1):
        pl.when(t < steps)(lambda t=t: start(t))

    def mine(c, _):
        rows = state[c]
        fluid_prepare(c, rows, basis(rows)[0], fluid[c], own_cf, own_row)
        own_fluid_columns(c, own_row, col)
        return 0

    lax.fori_loop(0, CELLS, mine, 0, unroll=2)
    fluids[...] = jnp.ones_like(fluids)

    def fill(e, _):
        pack(fluids, far_fluid[slot[e]], offset[e], live[e])
        return 0

    lax.fori_loop(0, SEND, fill, 0, unroll=8)
    acc1[...] = jnp.zeros_like(acc1)
    acc2[...] = jnp.zeros_like(acc2)
    ws0[...] = jnp.zeros_like(ws0)
    ws1[...] = jnp.zeros_like(ws1)
    ws = (ws0, ws1)

    def prepare(p):
        rows = blocks[p]
        fluid_prepare(p, rows, basis(rows)[0], fluids[p], cf, row)

    last = 2 * steps - 1
    for k in range(2):
        prepare(jnp.int32(k))

    def combine(p, side):
        return force_combine(own_cf[block_own[p]], cf[p], ws[side])

    def store(p, sums, valid):
        first, second = sums
        if valid is not True:
            first = first * jnp.where(valid, 1.0, 0.0)
        acc1[block_own[p]] += first
        acc2[p] = force_sums(blocks[p], second)

    def body(t, _):
        p = 2 * t
        k = lax.rem(t, DEPTH)
        pl.when(t + DEPTH - 1 < steps)(lambda: start(t + DEPTH - 1))
        wait(t)

        def work(p, side, rows):
            def grads(c):
                return buf[k, side, 0, c : c + CHUNK, :], buf[k, side, 1, c : c + CHUNK, :]

            fluid_work(ws[side], col, row[p], block_own[p], rows, grads)

        def step(rows):
            before = jnp.maximum(p - 1, 0)
            sums = combine(before, 1)
            work(p, 0, rows)
            sums0 = combine(p, 0)
            work(p + 1, 1, rows)
            store(before, sums, t > 0)
            store(p, sums0, True)
            prepare(jnp.minimum(p + 2, last))
            prepare(jnp.minimum(p + 3, last))

        by_rows(jnp.maximum(counts[block_own[p]], counts[block_own[p + 1]]), step)
        return 0

    lax.fori_loop(0, steps, body, 0)
    store(last, combine(last, 1), True)

    @pl.when(total > 2 * steps)
    def _():
        pltpu.sync_copy(cols_far, cols)
        expand(cols, at, as_, bh, None)

        def rest(p):
            rows = blocks[p]
            fluid_prepare(p, rows, geometry_prepare(p, rows, bd, bs), fluids[p], cf, row)

        refs = (
            bd, bs, own_cf, cf, at, as_, bh, row, col, (dist0, dist1), (appr0, appr1), ws,
        )
        same = lambda p: p
        full_force(
            2 * steps, total - 2 * steps, counts, lambda p: block_own[p], same, refs, rest, store,
        )

    def back(e, _):
        ret[slot[e]] = unpack(acc2, offset[e])
        return 0

    lax.fori_loop(0, SEND, back, 0, unroll=8)


def finish_kernel(
    back, goals, near, far, state, energy, counts, mig_cell, mig_dest, accel, leave, moved, used, *sums
):
    add_by_goal(back, goals, sums)
    lane = lax.broadcasted_iota(i32, (1, PART), 1)

    def cell(c, _):
        rows = state[c]
        here = lane < counts[c]
        total = jnp.where(
            here, force_sums(rows, near[c] + far[c]) + sum(part[c] for part in sums), 0.0
        )
        accel[c] = total
        new_vel = rows[3:6] + STEP * total[0:3]
        new_pos = rows[0:3] + STEP * new_vel
        new_energy = energy[pl.ds(c, 1), :] + STEP * total[3:4]
        kicked = jnp.concatenate(
            [new_pos, new_vel, rows[7:8], rows[6:7], new_energy], axis=0
        )
        moved[c] = jnp.where(here, kicked, 0.0)
        return 0

    lax.fori_loop(0, CELLS, cell, 0)
    leave[...] = jnp.zeros_like(leave)

    def clear(d, _):
        used[d] = 0
        return 0

    lax.fori_loop(0, leave.shape[0], clear, 0)

    def entry(e, _):
        d = mig_dest[e]
        k = used[d]
        used[d] = k + 1
        full = moved[mig_cell[e]]
        for r in range(9):
            leave[d, r, pl.ds(k, 1), :] = full[r : r + 1]
        return 0

    lax.fori_loop(0, mig_cell.shape[0], entry, 0)


def inbox_kernel(came, out):
    for d in range(came.shape[0]):
        full = came[d]
        for k in range(CAPM):
            out[d * CAPM + k] = full[:, k, :]


def vmem(*dims, dtype=f32):
    return pltpu.VMEM(dims, dtype)


def smem(*dims):
    return pltpu.SMEM(dims, i32)


WS = [vmem(2 * PART, PART, dtype=bf16)] * 2
SQUARE = [vmem(PART, PART)] * 2


def own_density(position, velocity, mass, smoothing, counts, pair_first, pair_offset):
    return kernel_call(
        own_density_kernel,
        (
            shape(CELLS, 1, PART),
            shape(CELLS, 8, PART),
            shape(CELLS, PART, 128),
        ),
        [VMEM] * 4 + [SMEM] * 3,
        (VMEM,) * 3,
        [
            vmem(CELLS, PART, 128),
            vmem(CELLS + 1, 1, PART),
            vmem(CELLS, PART, 48, dtype=bf16),
            vmem(CELLS, PART, 128),
            vmem(CELLS, PART, 128),
            vmem(CELLS, 48, PART, dtype=bf16),
            vmem(CELLS, 1, PART),
            vmem(CELLS, 1, PART),
        ]
        + SQUARE
        + [smem(CELLS + PAIRS)] * 3,
        flops=32 * PART * PART * 300,
        moved=2**20,
    )(position, velocity, mass, smoothing, counts, pair_first, pair_offset)


def far_density(far, counts, slot, proxy_cell, cols):
    return kernel_call(
        far_density_kernel,
        (
            shape(CELLS, PART, 128),
            shape(far.shape[0], 1, PART),
            shape(BLOCKS + 1, 8, PART),
            shape(SEND, dtype=i32),
            shape(BLOCKS, dtype=i32),
            shape(SEND, dtype=i32),
            shape(1, dtype=i32),
        ),
        [VMEM] + [SMEM] * 3 + [VMEM],
        (VMEM,) * 3 + (SMEM,) * 4,
        [
            vmem(BLOCKS + 1, 1, PART),
            vmem(CELLS, PART, 48, dtype=bf16),
            vmem(CELLS, PART, 128),
            vmem(CELLS, PART, 128),
            vmem(BLOCKS, 48, PART, dtype=bf16),
            vmem(BLOCKS, 1, PART),
            vmem(BLOCKS, 1, PART),
        ]
        + SQUARE
        + [smem(CELLS)],
        flops=128 * PART * PART * 300,
        moved=2**20,
    )(far, counts, slot, proxy_cell, cols)


def slopes(fluid, acc1, first, count, blocks, counts, block_own, size, cols):
    def body(*refs):
        slope_kernel(*refs, first=first)

    return kernel_call(
        body,
        (shape(count, 2, PART, PART), shape(CELLS, 1, PART)),
        [ANY, VMEM if first == 0 else ANY, VMEM] + [SMEM] * 3 + [VMEM],
        (ANY, VMEM),
        [
            vmem(CELLS, PART, 48, dtype=bf16),
            vmem(CELLS, PART, 48, dtype=bf16),
            vmem(CELLS, PART, 128),
            vmem(count, 48, PART, dtype=bf16),
            vmem(count, 48, PART, dtype=bf16),
            vmem(count, 1, PART),
        ]
        + SQUARE * 2
        + [vmem(DEPTH, 2, 2, PART, PART), pltpu.SemaphoreType.DMA((DEPTH,))],
        flops=count * PART * PART * 400,
        moved=count * 2**19,
    )(fluid, acc1, blocks, counts, block_own, size, cols)


def far_force(
    state, fluid, far_fluid, counts, slot, blocks, offset, block_own, live, size, cols,
    ready0, ready1,
):
    return kernel_call(
        far_force_kernel,
        (shape(CELLS, 8, PART), shape(far_fluid.shape[0], 4, PART)),
        [VMEM] * 4 + [SMEM] * 6 + [ANY] * 3,
        (VMEM, VMEM),
        [
            vmem(BLOCKS + 1, 4, PART),
            vmem(CELLS, PART, 128),
            vmem(CELLS, PART, 48, dtype=bf16),
            vmem(CELLS, PART, 48, dtype=bf16),
            vmem(CELLS, PART, 128),
            vmem(BLOCKS + 1, 2, PART),
            vmem(BLOCKS, 48, PART, dtype=bf16),
            vmem(BLOCKS, 48, PART, dtype=bf16),
            vmem(CELLS, 24, PART, dtype=bf16),
            vmem(CELLS, 8, PART),
            vmem(BLOCKS, 24, PART, dtype=bf16),
            vmem(BLOCKS, 8, PART),
            vmem(CELLS, 3, PART, 128),
        ]
        + SQUARE * 2
        + WS
        + [vmem(DEPTH, 2, 2, PART, PART), pltpu.SemaphoreType.DMA((DEPTH,))],
        flops=128 * PART * PART * 300,
        moved=2**20,
    )(
        state, fluid, blocks, far_fluid, counts, slot, offset, block_own, live, size,
        cols, ready0, ready1,
    )


def own_force(after, state, fluid, counts, pair_first, pair_offset, cols):
    return kernel_call(
        own_force_kernel,
        shape(CELLS, 8, PART),
        [ANY] + [VMEM] * 2 + [SMEM] * 3 + [VMEM],
        VMEM,
        [
            vmem(CELLS, 8, PART),
            vmem(CELLS + 1, 8, PART),
            vmem(CELLS, PART, 48, dtype=bf16),
            vmem(CELLS, PART, 48, dtype=bf16),
            vmem(CELLS, PART, 128),
            vmem(CELLS, 48, PART, dtype=bf16),
            vmem(CELLS, 48, PART, dtype=bf16),
            vmem(CELLS, 24, PART, dtype=bf16),
            vmem(CELLS, 8, PART),
            vmem(CELLS, 3, PART, 128),
        ]
        + SQUARE * 2
        + WS
        + [smem(CELLS + PAIRS)] * 3,
        flops=32 * PART * PART * 600,
        moved=2**20,
    )(after, state, fluid, counts, pair_first, pair_offset, cols)


def exchange(x, axes):
    return lax.all_to_all(x, axes, split_axis=0, concat_axis=0, tiled=True)


def local(
    position, velocity, mass, smoothing, energy, counts, proxy_cell, proxy_dest,
    proxy_target, pair_first, pair_offset, mig_cell, mig_dest,
):
    devices = lax.axis_size(("rows", "cols"))
    col_count = lax.axis_size("cols")
    slots = devices * CAP
    both = ("rows", "cols")
    req, slot = kernel_call(
        request_kernel,
        (shape(devices, 1, 128, dtype=i32), shape(SEND, dtype=i32)),
        [SMEM] * 2,
        (VMEM, SMEM),
        [smem(devices)],
        moved=2**20,
    )(proxy_dest[:, 0], proxy_target)
    goals = exchange(req, both)[:, 0, 0:CAP].reshape(slots)
    near, state, cols = own_density(
        position, velocity, mass, smoothing, counts, pair_first, pair_offset
    )
    answer = kernel_call(
        respond_kernel, shape(slots, 8, PART), [VMEM, SMEM], VMEM, moved=4 * 2**20
    )(state, goals)
    far = exchange(answer, both)
    acc1, ret, *plan = far_density(far, counts, slot, proxy_cell, cols)
    blocks, offset, block_own, live, size = plan
    ready0, far_sums = slopes(near, acc1, 0, EARLY, blocks, counts, block_own, size, cols)
    back = exchange(ret, both)
    density, fluid, answer2 = kernel_call(
        combine_density_kernel,
        (shape(CELLS, PART), shape(CELLS, 2, PART), shape(slots, 2, PART)),
        [ANY, VMEM, SMEM] + [VMEM] * 3 + [SMEM],
        (VMEM, VMEM, VMEM),
        [vmem(CELLS + 1, 1, PART)] * 4,
        moved=2**20,
    )(ready0, back, goals, near, far_sums, energy, counts)
    far_fluid = exchange(answer2, both)
    ready1, _ = slopes(fluid, acc1, EARLY, LATE, blocks, counts, block_own, size, cols)
    far_force_sums, ret4 = far_force(
        state, fluid, far_fluid, counts, slot, *plan, cols, ready0, ready1
    )
    near_force = own_force(
        far_force_sums, state, fluid, counts, pair_first, pair_offset, cols
    )
    back4 = exchange(ret4, both)
    accel, leave = kernel_call(
        finish_kernel,
        (shape(CELLS, 4, PART), shape(col_count, 9, CAPM, PART)),
        [VMEM, SMEM] + [VMEM] * 4 + [SMEM] * 3,
        (VMEM, VMEM),
        [vmem(CELLS, 9, PART), smem(col_count)] + [vmem(CELLS + 1, 4, PART)] * 4,
        moved=2**20,
    )(
        back4, goals, near_force, far_force_sums, state, energy, counts, mig_cell,
        mig_dest[:, 0],
    )
    arrived = kernel_call(
        inbox_kernel, shape(col_count * CAPM, 9, PART), [VMEM], VMEM, moved=2**20
    )(exchange(leave, "cols"))
    return (density, accel, arrived)


def solution(mesh):
    lead = ("rows", "cols")
    one, two, three = P(lead), P(lead, None), P(lead, None, None)
    return jax.shard_map(
        local,
        mesh=mesh,
        in_specs=(three, three, two, two, two, one, one, two, one, one, one, one, two),
        out_specs=(two, three, three),
        check_vma=False,
    )
```

```python
import jax
import jax.numpy as jnp
from jax import lax
from jax.experimental import pallas as pl
from jax.experimental.pallas import tpu as pltpu
from jax.sharding import PartitionSpec as P

CAP = 2
CAPM = 2
CELLS = 16
SEND = 128
PAIRS = 16
PART = 256

GAMMA = 5.0 / 3.0
STEP = 0.02
PI = 3.141592653589793
W_SCALE = 2.0 / PI
K_SCALE = -24.0 / PI
TINY = 1e-12
CHUNK = 32
ROWS = (128, 160, 192, 224, 256)
BLOCKS = SEND + CELLS
EARLY, LATE = 32, 60
DEPTH = 4
RING = 8

f32, bf16, i32 = jnp.float32, jnp.bfloat16, jnp.int32
VMEM = pl.BlockSpec(memory_space=pltpu.VMEM)
ANY = pl.BlockSpec(memory_space=pl.ANY)
SMEM = pl.BlockSpec(memory_space=pltpu.SMEM)
LIMIT = 56 * 2**20


def shape(*dims, dtype=f32):
    return jax.ShapeDtypeStruct(dims, dtype)


def kernel_call(body, out_shape, in_specs, out_specs, scratch=(), flops=0, moved=0):
    return pl.pallas_call(
        body,
        out_shape=out_shape,
        in_specs=in_specs,
        out_specs=out_specs,
        scratch_shapes=list(scratch),
        compiler_params=pltpu.CompilerParams(vmem_limit_bytes=LIMIT),
        cost_estimate=pl.CostEstimate(flops=flops, bytes_accessed=moved, transcendentals=0),
    )


def sublane():
    return lax.broadcasted_iota(i32, (8, PART), 0)


def split3(x):
    a = x.astype(bf16).astype(f32)
    b = (x - a).astype(bf16).astype(f32)
    return a, b, x - a - b


def left_parts(x):
    a, b, c = split3(x)
    return [a, a, b, b, a, c]


def right_parts(x):
    a, b, c = split3(x)
    return [a, b, a, b, c, a]


def stack16(parts):
    return jnp.concatenate(parts, axis=0).astype(bf16)


def basis(rows):
    row = sublane()
    place = jnp.where(row < 3, 2.0 * rows - 1.0, rows)
    first = place[0:3]
    norm = jnp.sum(first * first, axis=0, keepdims=True)
    cross = jnp.sum(first * place[3:6], axis=0, keepdims=True)
    full = jnp.where(row < 6, place, jnp.where(row == 6, cross, 1.0))
    return full, norm, cross


def right_distance(full, norm):
    row = sublane()
    return jnp.where(
        row < 3, full, jnp.where(row == 3, norm, jnp.where(row == 4, 1.0, 0.0))
    )


def left_distance(full, norm):
    row = sublane()
    return jnp.where(
        row < 3, -2.0 * full, jnp.where(row == 3, 1.0, jnp.where(row == 4, norm, 0.0))
    )


def left_approach(full, cross):
    return 4.0 * jnp.concatenate(
        [-full[3:6], -full[0:3], jnp.ones((1, PART), f32), cross], axis=0
    )


def columns(parts):
    fill = 128 - 8 * len(parts)
    return jnp.concatenate(parts + [jnp.zeros((fill, PART), f32)], axis=0).T


def halves(w):
    hi = w.astype(bf16)
    return hi, (w - hi.astype(f32)).astype(bf16)


def request_kernel(dest, target, req, slot, used):
    req[...] = jnp.full_like(req, -1)

    def clear(d, _):
        used[d] = 0
        return 0

    lax.fori_loop(0, req.shape[0], clear, 0, unroll=8)
    short = lax.broadcasted_iota(i32, (1, 128), 1)

    def entry(e, _):
        d = dest[e]
        k = used[d]
        used[d] = k + 1
        slot[e] = d * CAP + k
        req[d] = jnp.where(short == k, target[e], req[d])
        return 0

    lax.fori_loop(0, SEND, entry, 0, unroll=4)


def respond_kernel(state, goals, out):
    def one(s, _):
        goal = jnp.maximum(goals[s], 0)
        out[s] = state[goal]
        return 0

    lax.fori_loop(0, out.shape[0], one, 0, unroll=4)


def by_rows(need, step):
    low = 0
    for rows in ROWS:
        pl.when((need > low) & (need <= rows))(lambda rows=rows: step(rows))
        low = rows


def pipeline(first, count, rows_of, prepare, load, combine, store, work):
    last = first + count - 1

    def clamp(p):
        return jnp.minimum(p, last)

    for k in range(3):
        prepare(clamp(first + k))
    load(first, 0)

    def body(t, _):
        p = first + 2 * t

        def step(rows):
            before = jnp.maximum(p - 1, first)
            sums = combine(before, 1)
            work(p, 0, rows)
            load(p + 1, 1)
            sums0 = combine(p, 0)
            work(p + 1, 1, rows)
            load(clamp(p + 2), 0)
            store(before, sums, t > 0)
            store(p, sums0, True)
            prepare(clamp(p + 3))
            prepare(clamp(p + 4))

        by_rows(jnp.maximum(rows_of(p), rows_of(p + 1)), step)
        return 0

    lax.fori_loop(0, count // 2, body, 0)
    store(last, combine(last, 1), True)


def keep_sums(acc1, acc2, a, s, sums, valid):
    if valid is not True:
        keep = jnp.where(valid, 1.0, 0.0)
        sums = (sums[0] * keep, sums[1] * keep)
    acc1[a] += sums[0]
    acc2[s] += sums[1]


def pack_plan(far, slot, proxy_cell, offset, block_own, live, filled):
    def clear(c, _):
        filled[c] = 0
        return 0

    lax.fori_loop(0, CELLS, clear, 0)

    def measure(e, _):
        mass = far[slot[e]][7:8]
        n = jnp.sum(jnp.where(mass > 0.0, 1.0, 0.0)).astype(i32)
        live[e] = n
        a = proxy_cell[e]
        offset[e] = filled[a]
        filled[a] = filled[a] + n
        return 0

    lax.fori_loop(0, SEND, measure, 0, unroll=16)

    def place(c, total):
        blocks = (filled[c] + PART - 1) // PART
        filled[c] = total * PART

        def name(t, _):
            block_own[total + t] = c
            return 0

        lax.fori_loop(0, blocks, name, 0)
        return total + blocks

    total = lax.fori_loop(0, CELLS, place, 0)

    def shift(e, _):
        offset[e] = offset[e] + filled[proxy_cell[e]]
        return 0

    lax.fori_loop(0, SEND, shift, 0, unroll=8)
    block_own[total] = block_own[total - 1]
    return total + lax.rem(total, 2)


def pack(target, rows, offset, n):
    t = offset // PART
    lane0 = offset - t * PART
    lane = lax.broadcasted_iota(i32, rows.shape, 1)
    turned = pltpu.roll(rows, lane0, 1)
    pltpu.store(target.at[t], turned, mask=(lane >= lane0) & (lane < lane0 + n))
    pltpu.store(target.at[t + 1], turned, mask=lane < lane0 + n - PART)


def unpack(source, offset):
    t = offset // PART
    lane0 = offset - t * PART
    first, second = source[t], source[t + 1]
    lane = lax.broadcasted_iota(i32, first.shape, 1)
    return pltpu.roll(jnp.where(lane >= lane0, first, second), lax.rem(PART - lane0, PART), 1)


def own_lists(pair_first, pair_offset, pa, po, ps, dummy):
    def one(e, _):
        pa[e] = e
        po[e] = e
        ps[e] = dummy
        a = pair_first[e]
        b = lax.rem(a + pair_offset[e], CELLS)
        pa[CELLS + e] = a
        po[CELLS + e] = b
        ps[CELLS + e] = b
        return 0

    lax.fori_loop(0, CELLS, one, 0)


def nn(a, b):
    return jnp.dot(a, b, preferred_element_type=f32)


def nt(a, b):
    return lax.dot_general(a, b, (((1,), (1,)), ((), ())), preferred_element_type=f32)


def density_weights(r2, total_h):
    inv = pltpu.reciprocal(total_h, approx=True)
    inv2 = inv * inv
    q2 = jnp.maximum(r2, TINY) * inv2
    q = q2 * lax.rsqrt(q2)
    u = 2.0 - q
    t = jnp.maximum(u, 0.0)
    return jnp.minimum(t * t * t, 4.0 - 3.0 * (q2 * u)) * (inv2 * inv)


def two_wide(col, row):
    return jnp.concatenate([col, col], axis=1) + row


def density_pairs(count, counts, pa, po, ps, refs, prepare, acc1, acc2):
    bf, hj, mj, cols, bh, bm, dist = refs

    def load(p, side):
        dist[side][...] = nn(cols[pa(p)], bf[lax.rem(po(p), bf.shape[0])])

    def work(p, side, rows):
        a, o = pa(p), po(p)
        h_j, m_j = hj[o], mj[o]
        second = jnp.zeros((8, PART), f32)
        for c in range(0, rows, CHUNK):
            w = density_weights(
                dist[side][c : c + CHUNK, :], two_wide(bh[a, c : c + CHUNK, :], h_j)
            )
            first = w * m_j
            acc1[a, c : c + CHUNK, :] += first[:, 0:128] + first[:, 128:256]
            m_i = bm[a, c : c + CHUNK, :]
            other = w * jnp.concatenate([m_i, m_i], axis=1)
            second += jnp.sum(other.reshape(CHUNK // 8, 8, PART), axis=0)
        acc2[ps(p)] += jnp.sum(second, axis=0, keepdims=True)

    last = count - 1

    def clamp(p):
        return jnp.minimum(p, last)

    for k in range(3):
        prepare(clamp(k))
    load(0, 0)

    def body(t, _):
        p = 2 * t

        def step(rows):
            load(p + 1, 1)
            work(p, 0, rows)
            work(p + 1, 1, rows)
            load(clamp(p + 2), 0)
            prepare(clamp(p + 3))
            prepare(clamp(p + 4))

        by_rows(jnp.maximum(counts[pa(p)], counts[pa(p + 1)]), step)
        return 0

    lax.fori_loop(0, count // 2, body, 0)


def column_sums(x):
    return jnp.sum(x.T, axis=0, keepdims=True)


def spreader(lanes):
    row = lax.broadcasted_iota(i32, (128, 128 * len(lanes)), 0)
    block = lax.broadcasted_iota(i32, (128, 128 * len(lanes)), 1) // 128
    hit = row < 0
    for n, k in enumerate(lanes):
        hit |= (block == n) & ((row == k) | (row == k + 8) | (row == k + 16))
    return jnp.where(hit, 1.0, 0.0).astype(bf16)


def expand(cols, bh, bm=None):
    matrix = spreader((102,) if bm is None else (102, 103))

    def one(c, _):
        wide = nn(cols[c], matrix)
        bh[c] = wide[:, 0:128]
        if bm is not None:
            bm[c] = wide[:, 128:256]
        return 0

    lax.fori_loop(0, CELLS, one, 0, unroll=4)


def put_right(ref, o, start, parts):
    ref[lax.rem(o, ref.shape[0]), start : start + 48, :] = stack16(right_parts(parts))


def density_prepare(o, rows, bf, hj, mj):
    full, norm, cross = basis(rows)
    put_right(bf, o, 0, right_distance(full, norm))
    hj[o] = rows[6:7]
    mj[o] = rows[7:8]
    return full, norm, cross


def state_kernel(pos, vel, mass, smooth, counts, state, cols):
    lane = lax.broadcasted_iota(i32, (1, PART), 1)

    def mine(c, _):
        one = pl.ds(c, 1)
        live = jnp.where(lane < counts[c], mass[one, :], 0.0)
        rows = jnp.concatenate(
            [pos[k, one, :] for k in range(3)]
            + [vel[k, one, :] for k in range(3)]
            + [smooth[one, :], live],
            axis=0,
        )
        state[c] = rows
        full, norm, cross = basis(rows)
        cols[c] = columns(
            left_parts(left_distance(full, norm))
            + left_parts(left_approach(full, cross))
            + list(split3(rows))
        ).astype(bf16)
        return 0

    lax.fori_loop(0, CELLS, mine, 0, unroll=4)


def own_density_kernel(
    after, state, cols, counts, pair_first, pair_offset, near,
    acc1, acc2, bh, bm, bf, hj, mj, dist0, dist1, pa, po, ps,
):
    del after
    expand(cols, bh, bm)
    bf[...] = jnp.zeros_like(bf)

    def mine(c, _):
        density_prepare(c, state[c], bf, hj, mj)
        return 0

    lax.fori_loop(0, CELLS, mine, 0, unroll=2)
    own_lists(pair_first, pair_offset, pa, po, ps, CELLS)
    acc1[...] = jnp.zeros_like(acc1)
    acc2[...] = jnp.zeros_like(acc2)
    refs = (bf, hj, mj, cols, bh, bm, (dist0, dist1))
    density_pairs(
        CELLS + PAIRS, counts, lambda p: pa[p], lambda p: po[p], lambda p: ps[p], refs,
        lambda p: None, acc1, acc2,
    )

    def total(c, _):
        near[c] = column_sums(acc1[c]) + acc2[c]
        return 0

    lax.fori_loop(0, CELLS, total, 0, unroll=2)


def far_density_kernel(
    near, far, counts, slot, proxy_cell, cols,
    acc1, ret, blocks, offset, block_own, live, size,
    acc2, bh, bm, bf, hj, mj, dist0, dist1, filled,
):
    del near
    total = pack_plan(far, slot, proxy_cell, offset, block_own, live, filled)
    size[0] = total
    expand(cols, bh, bm)
    bf[...] = jnp.zeros_like(bf)
    blocks[...] = jnp.zeros_like(blocks)

    def fill(e, _):
        pack(blocks, far[slot[e]], offset[e], live[e])
        return 0

    lax.fori_loop(0, SEND, fill, 0, unroll=8)
    acc2[...] = jnp.zeros_like(acc2)
    acc1[...] = jnp.zeros_like(acc1)
    refs = (bf, hj, mj, cols, bh, bm, (dist0, dist1))
    same = lambda p: p
    density_pairs(
        total, counts, lambda p: block_own[p], same, same, refs,
        lambda p: density_prepare(p, blocks[p], bf, hj, mj), acc1, acc2,
    )

    def back(e, _):
        ret[slot[e]] = unpack(acc2, offset[e])
        return 0

    lax.fori_loop(0, SEND, back, 0, unroll=8)


def add_by_goal(back, goals, sums):
    for part in sums:
        part[...] = jnp.zeros_like(part)

    def one(t, _):
        for k, part in enumerate(sums):
            s = t * len(sums) + k
            goal = goals[s]
            part[jnp.where(goal < 0, CELLS, goal)] += back[s]
        return 0

    lax.fori_loop(0, back.shape[0] // len(sums), one, 0, unroll=2)


def combine_density_kernel(
    after, back, goals, near, far, energy, counts, density, fluid, answer, *sums
):
    del after
    add_by_goal(back, goals, sums)
    lane = lax.broadcasted_iota(i32, (1, PART), 1)

    def cell(c, _):
        raw = W_SCALE * (near[c] + far[c] + sum(part[c] for part in sums))
        here = lane < counts[c]
        density[pl.ds(c, 1), :] = jnp.where(here, raw, 0.0)
        fluid[c] = jnp.concatenate(
            [jnp.where(here, raw, 1.0), energy[pl.ds(c, 1), :]], axis=0
        )
        return 0

    lax.fori_loop(0, CELLS, cell, 0, unroll=4)

    def send(s, _):
        answer[s] = fluid[jnp.maximum(goals[s], 0)]
        return 0

    lax.fori_loop(0, answer.shape[0], send, 0, unroll=8)


def slope_weights(r2, s, total_h):
    inv = pltpu.reciprocal(total_h, approx=True)
    inv2 = inv * inv
    q2 = jnp.maximum(r2, TINY) * inv2
    rs = lax.rsqrt(q2)
    q = q2 * rs
    u = 2.0 - q
    t = jnp.maximum(u, 0.0)
    grad = jnp.where(q < 1.0, 3.0 * u - 2.0, t * t * rs)
    m = jnp.minimum(s, 0.0) * (inv * pltpu.reciprocal(q2 + 0.01, approx=True))
    return grad * (inv2 * inv2 * inv), m


def fluid_weights(grad, m, total_c, total_p, total_r):
    return (total_p + m * (m - total_c) * pltpu.reciprocal(total_r, approx=True)) * grad


def force_fluid(fluid):
    rho, u = fluid[0:1], fluid[1:2]
    pressure = (GAMMA - 1.0) * u / rho
    sound = jnp.sqrt(GAMMA * (GAMMA - 1.0) * u)
    return pressure, sound, 4.0 * rho


def put_halves(ws, c, w):
    hi, lo = halves(w)
    ws[c : c + CHUNK, :] = hi
    ws[PART + c : PART + c + CHUNK, :] = lo


def fluid_work(ws, col, side_row, a, rows, grads):
    for c in range(0, rows, CHUNK):
        grad, m = grads(c)
        total = [
            two_wide(col[a, k, c : c + CHUNK, :], side_row[k + 1 : k + 2]) for k in range(3)
        ]
        put_halves(ws, c, fluid_weights(grad, m, *total))


def fold(x):
    return x[0:8] + x[8:16] + x[16:24]


def force_combine(own, other, ws):
    second = fold(nn(jnp.concatenate([own, own], axis=1), ws[...]))
    first = fold(nt(other, ws[...]))
    return first[:, 0:PART] + first[:, PART:], second


def full_force(first, count, counts, pa, po, refs, prepare, store):
    bd, bs, own_cf, other_cf, cols, bh, row, col, dist, appr, ws = refs

    def load(p, side):
        a, o = pa(p), lax.rem(po(p), bd.shape[0])
        dist[side][...] = nn(cols[a], bd[o])
        appr[side][...] = nn(cols[a], bs[o])

    def work(p, side, rows):
        a = pa(p)
        side_row = row[po(p)]

        def grads(c):
            return slope_weights(
                dist[side][c : c + CHUNK, :],
                appr[side][c : c + CHUNK, :],
                two_wide(bh[a, c : c + CHUNK, :], side_row[0:1]),
            )

        fluid_work(ws[side], col, side_row, a, rows, grads)

    def combine(p, side):
        return force_combine(own_cf[pa(p)], other_cf[po(p)], ws[side])

    pipeline(first, count, lambda p: counts[pa(p)], prepare, load, combine, store, work)


def geometry_prepare(o, rows, bd, bs):
    full, norm, cross = basis(rows)
    put_right(bd, o, 0, right_distance(full, norm))
    put_right(bs, o, 48, full)
    return full


def fluid_prepare(o, rows, full, fluid, cf, row):
    cf[o] = stack16(list(split3(rows[7:8] * full)))
    pressure, sound, rho4 = force_fluid(fluid)
    row[o] = jnp.concatenate(
        [rows[6:7], sound, pressure, rho4, jnp.zeros((4, PART), f32)], axis=0
    )


def own_fluid_columns(c, row, col, matrix):
    wide = nn(columns(list(split3(row[c]))).astype(bf16), matrix)
    for k in range(3):
        col[c, k] = wide[:, 128 * k : 128 * (k + 1)]


def slope_kernel(
    fluid, acc1, blocks, counts, block_own, size, cols, out, far_sums,
    bh, bd, bs, hj, dist0, dist1, appr0, appr1, buf, sems, *, first,
):
    del fluid
    expand(cols, bh)
    bd[...] = jnp.zeros_like(bd)
    bs[...] = jnp.zeros_like(bs)
    if first == 0:

        def total(c, _):
            far_sums[c] = column_sums(acc1[c])
            return 0

        lax.fori_loop(0, CELLS, total, 0, unroll=2)
    else:
        far_sums[...] = jnp.zeros_like(far_sums)
    dist, appr = (dist0, dist1), (appr0, appr1)
    count = jnp.clip(size[0] - first, 0, out.shape[0])
    last = first + count - 1

    def clamp(p):
        return jnp.minimum(p, last)

    def prepare(p):
        rows = blocks[p]
        geometry_prepare(p, rows, bd, bs)
        hj[p - first] = rows[6:7]

    def load(p, side):
        a = block_own[p]
        o = lax.rem(p, RING)
        dist[side][...] = nn(cols[a], bd[o])
        appr[side][...] = nn(cols[a], bs[o])

    def copy(t, rows):
        k = lax.rem(t, DEPTH)
        return pltpu.make_async_copy(
            buf.at[k, :, :, pl.ds(0, rows), :],
            out.at[pl.ds(2 * t, 2), :, pl.ds(0, rows), :],
            sems.at[k],
        )

    def need(t):
        p = first + 2 * t
        return jnp.maximum(counts[block_own[p]], counts[block_own[p + 1]])

    def wait(t):
        by_rows(need(t), lambda rows: copy(t, rows).wait())

    def work(p, side, rows, k):
        a = block_own[p]
        h_j = hj[p - first]
        for c in range(0, rows, CHUNK):
            grad, m = slope_weights(
                dist[side][c : c + CHUNK, :],
                appr[side][c : c + CHUNK, :],
                two_wide(bh[a, c : c + CHUNK, :], h_j),
            )
            buf[k, side, 0, c : c + CHUNK, :] = grad
            buf[k, side, 1, c : c + CHUNK, :] = m

    @pl.when(count > 0)
    def _():
        for k in range(3):
            prepare(clamp(first + k))
        load(first, 0)

    def body(t, _):
        p = first + 2 * t
        k = lax.rem(t, DEPTH)
        pl.when(t >= DEPTH)(lambda: wait(t - DEPTH))

        def step(rows):
            load(p + 1, 1)
            work(p, 0, rows, k)
            work(p + 1, 1, rows, k)
            load(clamp(p + 2), 0)
            prepare(clamp(p + 3))
            prepare(clamp(p + 4))
            copy(t, rows).start()

        by_rows(need(t), step)
        return 0

    steps = count // 2
    lax.fori_loop(0, steps, body, 0)

    def drain(t, _):
        wait(t)
        return 0

    lax.fori_loop(jnp.maximum(steps - DEPTH, 0), steps, drain, 0)


def force_sums(rows, sums):
    full, _, cross = basis(rows)
    count = sums[7:8]
    accel = (-0.5 * K_SCALE) * (full[0:3] * count - sums[0:3])
    mixed = jnp.sum(full[3:6] * sums[0:3] + full[0:3] * sums[3:6], axis=0, keepdims=True)
    heat = (0.25 * K_SCALE) * (cross * count - mixed + sums[6:7])
    return jnp.concatenate([accel, heat], axis=0)


def own_force_kernel(
    after, state, fluid, counts, pair_first, pair_offset, cols, total,
    acc1, acc2, bh, bd, bs, cf, row, col, dist0, dist1, appr0, appr1, ws0, ws1, pa, po, ps,
):
    del after
    expand(cols, bh)
    bd[...] = jnp.zeros_like(bd)
    bs[...] = jnp.zeros_like(bs)
    matrix = spreader((1, 2, 3))

    def mine(c, _):
        rows = state[c]
        fluid_prepare(c, rows, geometry_prepare(c, rows, bd, bs), fluid[c], cf, row)
        own_fluid_columns(c, row, col, matrix)
        return 0

    lax.fori_loop(0, CELLS, mine, 0, unroll=2)
    own_lists(pair_first, pair_offset, pa, po, ps, CELLS)
    acc1[...] = jnp.zeros_like(acc1)
    acc2[...] = jnp.zeros_like(acc2)
    ws0[...] = jnp.zeros_like(ws0)
    ws1[...] = jnp.zeros_like(ws1)
    refs = (bd, bs, cf, cf, cols, bh, row, col, (dist0, dist1), (appr0, appr1), (ws0, ws1))
    full_force(
        0, CELLS + PAIRS, counts, lambda p: pa[p], lambda p: po[p], refs, lambda p: None,
        lambda p, sums, valid: keep_sums(acc1, acc2, pa[p], ps[p], sums, valid),
    )
    total[...] = acc1[...] + acc2[0:CELLS]


def far_force_kernel(
    state, fluid, blocks, far_fluid, counts, slot, offset, block_own, live, size, cols_far,
    ready0, ready1, acc1, ret,
    acc2, cols, bh, fluids, bd, bs, own_cf, own_row, cf, row, col,
    dist0, dist1, appr0, appr1, ws0, ws1, buf, sems,
):
    total = size[0]
    half = ready0.shape[0] // 2
    steps = jnp.minimum(total, ready0.shape[0] + ready1.shape[0]) // 2

    def need(t):
        return jnp.maximum(counts[block_own[2 * t]], counts[block_own[2 * t + 1]])

    def copy(ready, t, k, rows):
        return pltpu.make_async_copy(
            ready.at[pl.ds(2 * t, 2), :, pl.ds(0, rows), :],
            buf.at[k, :, :, pl.ds(0, rows), :],
            sems.at[k],
        )

    def start(t):
        k = lax.rem(t, DEPTH)

        @pl.when(t < half)
        def _():
            by_rows(need(t), lambda rows: copy(ready0, t, k, rows).start())

        @pl.when(t >= half)
        def _():
            by_rows(need(t), lambda rows: copy(ready1, t - half, k, rows).start())

    for t in range(DEPTH - 1):
        pl.when(t < steps)(lambda t=t: start(t))

    matrix = spreader((1, 2, 3))

    def mine(c, _):
        rows = state[c]
        fluid_prepare(c, rows, basis(rows)[0], fluid[c], own_cf, own_row)
        own_fluid_columns(c, own_row, col, matrix)
        return 0

    lax.fori_loop(0, CELLS, mine, 0, unroll=2)
    fluids[...] = jnp.ones_like(fluids)

    def fill(e, _):
        pack(fluids, far_fluid[slot[e]], offset[e], live[e])
        return 0

    lax.fori_loop(0, SEND, fill, 0, unroll=8)
    acc1[...] = jnp.zeros_like(acc1)
    acc2[...] = jnp.zeros_like(acc2)
    ws0[...] = jnp.zeros_like(ws0)
    ws1[...] = jnp.zeros_like(ws1)
    ws = (ws0, ws1)

    def prepare(p):
        rows = blocks[p]
        fluid_prepare(p, rows, basis(rows)[0], fluids[p], cf, row)

    last = 2 * steps - 1
    for k in range(2):
        prepare(jnp.int32(k))

    def combine(p, side):
        return force_combine(own_cf[block_own[p]], cf[p], ws[side])

    def store(p, sums, valid):
        first, second = sums
        if valid is not True:
            first = first * jnp.where(valid, 1.0, 0.0)
        acc1[block_own[p]] += first
        acc2[p] = force_sums(blocks[p], second)

    def body(t, _):
        p = 2 * t
        k = lax.rem(t, DEPTH)
        pl.when(t + DEPTH - 1 < steps)(lambda: start(t + DEPTH - 1))

        def work(p, side, rows):
            def grads(c):
                return buf[k, side, 0, c : c + CHUNK, :], buf[k, side, 1, c : c + CHUNK, :]

            fluid_work(ws[side], col, row[p], block_own[p], rows, grads)

        def step(rows):
            copy(ready0, 0, k, rows).wait()
            before = jnp.maximum(p - 1, 0)
            sums = combine(before, 1)
            work(p, 0, rows)
            sums0 = combine(p, 0)
            work(p + 1, 1, rows)
            store(before, sums, t > 0)
            store(p, sums0, True)
            prepare(jnp.minimum(p + 2, last))
            prepare(jnp.minimum(p + 3, last))

        by_rows(need(t), step)
        return 0

    lax.fori_loop(0, steps, body, 0)
    store(last, combine(last, 1), True)

    @pl.when(total > 2 * steps)
    def _():
        pltpu.sync_copy(cols_far, cols)
        expand(cols, bh)
        bd[...] = jnp.zeros_like(bd)
        bs[...] = jnp.zeros_like(bs)

        def rest(p):
            rows = blocks[p]
            fluid_prepare(p, rows, geometry_prepare(p, rows, bd, bs), fluids[p], cf, row)

        refs = (
            bd, bs, own_cf, cf, cols, bh, row, col, (dist0, dist1), (appr0, appr1), ws,
        )
        same = lambda p: p
        full_force(
            2 * steps, total - 2 * steps, counts, lambda p: block_own[p], same, refs, rest, store,
        )

    def back(e, _):
        ret[slot[e]] = unpack(acc2, offset[e])
        return 0

    lax.fori_loop(0, SEND, back, 0, unroll=8)


def finish_kernel(
    back, goals, near, far, state, energy, counts, mig_cell, mig_dest, accel, leave, moved, used, *sums
):
    add_by_goal(back, goals, sums)
    lane = lax.broadcasted_iota(i32, (1, PART), 1)

    def cell(c, _):
        rows = state[c]
        here = lane < counts[c]
        total = jnp.where(
            here, force_sums(rows, near[c] + far[c]) + sum(part[c] for part in sums), 0.0
        )
        accel[c] = total
        new_vel = rows[3:6] + STEP * total[0:3]
        new_pos = rows[0:3] + STEP * new_vel
        new_energy = energy[pl.ds(c, 1), :] + STEP * total[3:4]
        kicked = jnp.concatenate(
            [new_pos, new_vel, rows[7:8], rows[6:7], new_energy], axis=0
        )
        moved[c] = jnp.where(here, kicked, 0.0)
        return 0

    lax.fori_loop(0, CELLS, cell, 0)
    leave[...] = jnp.zeros_like(leave)

    def clear(d, _):
        used[d] = 0
        return 0

    lax.fori_loop(0, leave.shape[0], clear, 0)

    def entry(e, _):
        d = mig_dest[e]
        k = used[d]
        used[d] = k + 1
        full = moved[mig_cell[e]]
        for r in range(9):
            leave[d, r, pl.ds(k, 1), :] = full[r : r + 1]
        return 0

    lax.fori_loop(0, mig_cell.shape[0], entry, 0)


def inbox_kernel(came, out):
    for d in range(came.shape[0]):
        for r in range(came.shape[1]):
            out[r, d * CAPM : (d + 1) * CAPM, :] = came[d, r]


def vmem(*dims, dtype=f32):
    return pltpu.VMEM(dims, dtype)


def smem(*dims):
    return pltpu.SMEM(dims, i32)


WS = [vmem(2 * PART, PART, dtype=bf16)] * 2
SQUARE = [vmem(PART, PART)] * 2


def cell_state(position, velocity, mass, smoothing, counts):
    return kernel_call(
        state_kernel,
        (shape(CELLS, 8, PART), shape(CELLS, PART, 128, dtype=bf16)),
        [VMEM] * 4 + [SMEM],
        (VMEM, VMEM),
        flops=2**20,
        moved=2**22,
    )(position, velocity, mass, smoothing, counts)


def own_density(after, state, cols, counts, pair_first, pair_offset):
    return kernel_call(
        own_density_kernel,
        shape(CELLS, 1, PART),
        [ANY] + [VMEM] * 2 + [SMEM] * 3,
        VMEM,
        [
            vmem(CELLS, PART, 128),
            vmem(CELLS + 1, 1, PART),
            vmem(CELLS, PART, 128),
            vmem(CELLS, PART, 128),
            vmem(CELLS, 128, PART, dtype=bf16),
            vmem(CELLS, 1, PART),
            vmem(CELLS, 1, PART),
        ]
        + SQUARE
        + [smem(CELLS + PAIRS)] * 3,
        flops=32 * PART * PART * 300,
        moved=2**20,
    )(after, state, cols, counts, pair_first, pair_offset)


def far_density(near, far, counts, slot, proxy_cell, cols):
    return kernel_call(
        far_density_kernel,
        (
            shape(CELLS, PART, 128),
            shape(far.shape[0], 1, PART),
            shape(BLOCKS + 1, 8, PART),
            shape(SEND, dtype=i32),
            shape(BLOCKS, dtype=i32),
            shape(SEND, dtype=i32),
            shape(1, dtype=i32),
        ),
        [ANY, VMEM] + [SMEM] * 3 + [VMEM],
        (VMEM,) * 3 + (SMEM,) * 4,
        [
            vmem(BLOCKS + 1, 1, PART),
            vmem(CELLS, PART, 128),
            vmem(CELLS, PART, 128),
            vmem(RING, 128, PART, dtype=bf16),
            vmem(BLOCKS, 1, PART),
            vmem(BLOCKS, 1, PART),
        ]
        + SQUARE
        + [smem(CELLS)],
        flops=128 * PART * PART * 300,
        moved=2**20,
    )(near, far, counts, slot, proxy_cell, cols)


def slopes(fluid, acc1, first, count, blocks, counts, block_own, size, cols):
    def body(*refs):
        slope_kernel(*refs, first=first)

    return kernel_call(
        body,
        (shape(count, 2, PART, PART), shape(CELLS, 1, PART)),
        [ANY, VMEM if first == 0 else ANY, VMEM] + [SMEM] * 3 + [VMEM],
        (ANY, VMEM),
        [
            vmem(CELLS, PART, 128),
            vmem(RING, 128, PART, dtype=bf16),
            vmem(RING, 128, PART, dtype=bf16),
            vmem(count, 1, PART),
        ]
        + SQUARE * 2
        + [vmem(DEPTH, 2, 2, PART, PART), pltpu.SemaphoreType.DMA((DEPTH,))],
        flops=count * PART * PART * 400,
        moved=count * 2**19,
    )(fluid, acc1, blocks, counts, block_own, size, cols)


def far_force(
    state, fluid, far_fluid, counts, slot, blocks, offset, block_own, live, size, cols,
    ready0, ready1,
):
    return kernel_call(
        far_force_kernel,
        (shape(CELLS, 8, PART), shape(far_fluid.shape[0], 4, PART)),
        [VMEM] * 4 + [SMEM] * 6 + [ANY] * 3,
        (VMEM, VMEM),
        [
            vmem(BLOCKS + 1, 4, PART),
            vmem(CELLS, PART, 128, dtype=bf16),
            vmem(CELLS, PART, 128),
            vmem(BLOCKS + 1, 2, PART),
            vmem(RING, 128, PART, dtype=bf16),
            vmem(RING, 128, PART, dtype=bf16),
            vmem(CELLS, 24, PART, dtype=bf16),
            vmem(CELLS, 8, PART),
            vmem(BLOCKS, 24, PART, dtype=bf16),
            vmem(BLOCKS, 8, PART),
            vmem(CELLS, 3, PART, 128),
        ]
        + SQUARE * 2
        + WS
        + [vmem(DEPTH, 2, 2, PART, PART), pltpu.SemaphoreType.DMA((DEPTH,))],
        flops=128 * PART * PART * 300,
        moved=2**20,
    )(
        state, fluid, blocks, far_fluid, counts, slot, offset, block_own, live, size,
        cols, ready0, ready1,
    )


def own_force(after, state, fluid, counts, pair_first, pair_offset, cols):
    return kernel_call(
        own_force_kernel,
        shape(CELLS, 8, PART),
        [ANY] + [VMEM] * 2 + [SMEM] * 3 + [VMEM],
        VMEM,
        [
            vmem(CELLS, 8, PART),
            vmem(CELLS + 1, 8, PART),
            vmem(CELLS, PART, 128),
            vmem(CELLS, 128, PART, dtype=bf16),
            vmem(CELLS, 128, PART, dtype=bf16),
            vmem(CELLS, 24, PART, dtype=bf16),
            vmem(CELLS, 8, PART),
            vmem(CELLS, 3, PART, 128),
        ]
        + SQUARE * 2
        + WS
        + [smem(CELLS + PAIRS)] * 3,
        flops=32 * PART * PART * 600,
        moved=2**20,
    )(after, state, fluid, counts, pair_first, pair_offset, cols)


def exchange(x, axes):
    return lax.all_to_all(x, axes, split_axis=0, concat_axis=0, tiled=True)


def local(
    position, velocity, mass, smoothing, energy, counts, proxy_cell, proxy_dest,
    proxy_target, pair_first, pair_offset, mig_cell, mig_dest,
):
    devices = lax.axis_size(("rows", "cols"))
    col_count = lax.axis_size("cols")
    slots = devices * CAP
    both = ("rows", "cols")
    req, slot = kernel_call(
        request_kernel,
        (shape(devices, 1, 128, dtype=i32), shape(SEND, dtype=i32)),
        [SMEM] * 2,
        (VMEM, SMEM),
        [smem(devices)],
        moved=2**20,
    )(proxy_dest[:, 0], proxy_target)
    goals = exchange(req, both)[:, 0, 0:CAP].reshape(slots)
    state, cols = cell_state(
        position.transpose(1, 0, 2), velocity.transpose(1, 0, 2), mass, smoothing, counts
    )
    answer = kernel_call(
        respond_kernel, shape(slots, 8, PART), [VMEM, SMEM], VMEM, moved=4 * 2**20
    )(state, goals)
    far = exchange(answer, both)
    near = own_density(answer, state, cols, counts, pair_first, pair_offset)
    acc1, ret, *plan = far_density(near, far, counts, slot, proxy_cell, cols)
    blocks, offset, block_own, live, size = plan
    ready0, far_sums = slopes(near, acc1, 0, EARLY, blocks, counts, block_own, size, cols)
    back = exchange(ret, both)
    density, fluid, answer2 = kernel_call(
        combine_density_kernel,
        (shape(CELLS, PART), shape(CELLS, 2, PART), shape(slots, 2, PART)),
        [ANY, VMEM, SMEM] + [VMEM] * 3 + [SMEM],
        (VMEM, VMEM, VMEM),
        [vmem(CELLS + 1, 1, PART)] * 4,
        moved=2**20,
    )(ready0, back, goals, near, far_sums, energy, counts)
    far_fluid = exchange(answer2, both)
    ready1, _ = slopes(fluid, acc1, EARLY, LATE, blocks, counts, block_own, size, cols)
    far_force_sums, ret4 = far_force(
        state, fluid, far_fluid, counts, slot, *plan, cols, ready0, ready1
    )
    near_force = own_force(
        far_force_sums, state, fluid, counts, pair_first, pair_offset, cols
    )
    back4 = exchange(ret4, both)
    accel, leave = kernel_call(
        finish_kernel,
        (shape(CELLS, 4, PART), shape(col_count, 9, CAPM, PART)),
        [VMEM, SMEM] + [VMEM] * 4 + [SMEM] * 3,
        (VMEM, VMEM),
        [vmem(CELLS, 9, PART), smem(col_count)] + [vmem(CELLS + 1, 4, PART)] * 4,
        moved=2**20,
    )(
        back4, goals, near_force, far_force_sums, state, energy, counts, mig_cell,
        mig_dest[:, 0],
    )
    arrived = kernel_call(
        inbox_kernel, shape(9, col_count * CAPM, PART), [VMEM], VMEM, moved=2**20
    )(exchange(leave, "cols"))
    return (density, accel, arrived.transpose(1, 0, 2))


def solution(mesh):
    lead = ("rows", "cols")
    one, two, three = P(lead), P(lead, None), P(lead, None, None)
    return jax.shard_map(
        local,
        mesh=mesh,
        in_specs=(three, three, two, two, two, one, one, two, one, one, one, one, two),
        out_specs=(two, three, three),
        check_vma=False,
    )
```

```python
import jax
import jax.numpy as jnp
from jax import lax
from jax.experimental import pallas as pl
from jax.experimental.pallas import tpu as pltpu
from jax.sharding import PartitionSpec as P

CAP = 2
CAPM = 2
CELLS = 16
SEND = 128
PAIRS = 16
PART = 256

GAMMA = 5.0 / 3.0
STEP = 0.02
PI = 3.141592653589793
W_SCALE = 2.0 / PI
K_SCALE = -24.0 / PI
TINY = 1e-12
CHUNK = 32
ROWS = (128, 160, 192, 224, 256)
BLOCKS = SEND + CELLS
RING = 8

f32, bf16, i32 = jnp.float32, jnp.bfloat16, jnp.int32
VMEM = pl.BlockSpec(memory_space=pltpu.VMEM)
ANY = pl.BlockSpec(memory_space=pl.ANY)
SMEM = pl.BlockSpec(memory_space=pltpu.SMEM)
LIMIT = 56 * 2**20


def shape(*dims, dtype=f32):
    return jax.ShapeDtypeStruct(dims, dtype)


def kernel_call(body, out_shape, in_specs, out_specs, scratch=(), flops=0, moved=0):
    return pl.pallas_call(
        body,
        out_shape=out_shape,
        in_specs=in_specs,
        out_specs=out_specs,
        scratch_shapes=list(scratch),
        compiler_params=pltpu.CompilerParams(vmem_limit_bytes=LIMIT),
        cost_estimate=pl.CostEstimate(flops=flops, bytes_accessed=moved, transcendentals=0),
    )


def sublane():
    return lax.broadcasted_iota(i32, (8, PART), 0)


def split3(x):
    a = x.astype(bf16).astype(f32)
    b = (x - a).astype(bf16).astype(f32)
    return a, b, x - a - b


def left_parts(x):
    a, b, c = split3(x)
    return [a, a, b, b, a, c]


def right_parts(x):
    a, b, c = split3(x)
    return [a, b, a, b, c, a]


def stack16(parts):
    return jnp.concatenate(parts, axis=0).astype(bf16)


def basis(rows):
    row = sublane()
    place = jnp.where(row < 3, 2.0 * rows - 1.0, rows)
    first = place[0:3]
    norm = jnp.sum(first * first, axis=0, keepdims=True)
    cross = jnp.sum(first * place[3:6], axis=0, keepdims=True)
    full = jnp.where(row < 6, place, jnp.where(row == 6, cross, 1.0))
    return full, norm, cross


def right_distance(full, norm):
    row = sublane()
    return jnp.where(
        row < 3, full, jnp.where(row == 3, norm, jnp.where(row == 4, 1.0, 0.0))
    )


def left_distance(full, norm):
    row = sublane()
    return jnp.where(
        row < 3, -2.0 * full, jnp.where(row == 3, 1.0, jnp.where(row == 4, norm, 0.0))
    )


def left_approach(full, cross):
    return 4.0 * jnp.concatenate(
        [-full[3:6], -full[0:3], jnp.ones((1, PART), f32), cross], axis=0
    )


def columns(parts):
    fill = 128 - 8 * len(parts)
    return jnp.concatenate(parts + [jnp.zeros((fill, PART), f32)], axis=0).T


def halves(w):
    hi = w.astype(bf16)
    return hi, (w - hi.astype(f32)).astype(bf16)


def request_kernel(dest, target, req, slot, used):
    req[...] = jnp.full_like(req, -1)

    def clear(d, _):
        used[d] = 0
        return 0

    lax.fori_loop(0, req.shape[0], clear, 0, unroll=8)
    short = lax.broadcasted_iota(i32, (1, 128), 1)

    def entry(e, _):
        d = dest[e]
        k = used[d]
        used[d] = k + 1
        slot[e] = d * CAP + k
        req[d] = jnp.where(short == k, target[e], req[d])
        return 0

    lax.fori_loop(0, SEND, entry, 0, unroll=4)


def respond_kernel(state, goals, out):
    def one(s, _):
        goal = jnp.maximum(goals[s], 0)
        out[s] = state[goal]
        return 0

    lax.fori_loop(0, out.shape[0], one, 0, unroll=4)


def by_rows(need, step):
    low = 0
    for rows in ROWS:
        pl.when((need > low) & (need <= rows))(lambda rows=rows: step(rows))
        low = rows


def pipeline(first, count, rows_of, prepare, load, combine, store, work):
    last = first + count - 1

    def clamp(p):
        return jnp.minimum(p, last)

    for k in range(3):
        prepare(clamp(first + k))
    load(first, 0)

    def body(t, _):
        p = first + 2 * t

        def step(rows):
            before = jnp.maximum(p - 1, first)
            sums = combine(before, 1)
            work(p, 0, rows)
            load(p + 1, 1)
            sums0 = combine(p, 0)
            work(p + 1, 1, rows)
            load(clamp(p + 2), 0)
            store(before, sums, t > 0)
            store(p, sums0, True)
            prepare(clamp(p + 3))
            prepare(clamp(p + 4))

        by_rows(jnp.maximum(rows_of(p), rows_of(p + 1)), step)
        return 0

    lax.fori_loop(0, count // 2, body, 0)
    store(last, combine(last, 1), True)


def keep_sums(acc1, acc2, a, s, sums, valid):
    if valid is not True:
        keep = jnp.where(valid, 1.0, 0.0)
        sums = (sums[0] * keep, sums[1] * keep)
    acc1[a] += sums[0]
    acc2[s] += sums[1]


def pack_plan(far, slot, proxy_cell, offset, block_own, live, filled):
    def clear(c, _):
        filled[c] = 0
        return 0

    lax.fori_loop(0, CELLS, clear, 0)

    def measure(e, _):
        mass = far[slot[e]][7:8]
        n = jnp.sum(jnp.where(mass > 0.0, 1.0, 0.0)).astype(i32)
        live[e] = n
        a = proxy_cell[e]
        offset[e] = filled[a]
        filled[a] = filled[a] + n
        return 0

    lax.fori_loop(0, SEND, measure, 0, unroll=16)

    def place(c, total):
        blocks = (filled[c] + PART - 1) // PART
        filled[c] = total * PART

        def name(t, _):
            block_own[total + t] = c
            return 0

        lax.fori_loop(0, blocks, name, 0)
        return total + blocks

    total = lax.fori_loop(0, CELLS, place, 0)

    def shift(e, _):
        offset[e] = offset[e] + filled[proxy_cell[e]]
        return 0

    lax.fori_loop(0, SEND, shift, 0, unroll=8)
    block_own[total] = block_own[total - 1]
    return total + lax.rem(total, 2)


def pack(target, rows, offset, n):
    t = offset // PART
    lane0 = offset - t * PART
    lane = lax.broadcasted_iota(i32, rows.shape, 1)
    turned = pltpu.roll(rows, lane0, 1)
    pltpu.store(target.at[t], turned, mask=(lane >= lane0) & (lane < lane0 + n))
    pltpu.store(target.at[t + 1], turned, mask=lane < lane0 + n - PART)


def unpack(source, offset):
    t = offset // PART
    lane0 = offset - t * PART
    first, second = source[t], source[t + 1]
    lane = lax.broadcasted_iota(i32, first.shape, 1)
    return pltpu.roll(jnp.where(lane >= lane0, first, second), lax.rem(PART - lane0, PART), 1)


def own_lists(pair_first, pair_offset, pa, po, ps, dummy):
    def one(e, _):
        pa[e] = e
        po[e] = e
        ps[e] = dummy
        a = pair_first[e]
        b = lax.rem(a + pair_offset[e], CELLS)
        pa[CELLS + e] = a
        po[CELLS + e] = b
        ps[CELLS + e] = b
        return 0

    lax.fori_loop(0, CELLS, one, 0)


def nn(a, b):
    return jnp.dot(a, b, preferred_element_type=f32)


def nt(a, b):
    return lax.dot_general(a, b, (((1,), (1,)), ((), ())), preferred_element_type=f32)


def density_weights(r2, total_h):
    inv = pltpu.reciprocal(total_h, approx=True)
    inv2 = inv * inv
    q2 = jnp.maximum(r2, TINY) * inv2
    q = q2 * lax.rsqrt(q2)
    u = 2.0 - q
    t = jnp.maximum(u, 0.0)
    return jnp.minimum(t * t * t, 4.0 - 3.0 * (q2 * u)) * (inv2 * inv)


def two_wide(col, row):
    return jnp.concatenate([col, col], axis=1) + row


def density_pairs(count, counts, pa, po, ps, refs, prepare, acc1, acc2):
    bf, hj, mj, cols, bh, bm, dist = refs

    def load(p, side):
        dist[side][...] = nn(cols[pa(p)], bf[lax.rem(po(p), bf.shape[0])])

    def work(p, side, rows):
        a, o = pa(p), po(p)
        h_j, m_j = hj[o], mj[o]
        second = jnp.zeros((8, PART), f32)
        for c in range(0, rows, CHUNK):
            w = density_weights(
                dist[side][c : c + CHUNK, :], two_wide(bh[a, c : c + CHUNK, :], h_j)
            )
            first = w * m_j
            acc1[a, c : c + CHUNK, :] += first[:, 0:128] + first[:, 128:256]
            m_i = bm[a, c : c + CHUNK, :]
            other = w * jnp.concatenate([m_i, m_i], axis=1)
            second += jnp.sum(other.reshape(CHUNK // 8, 8, PART), axis=0)
        acc2[ps(p)] += jnp.sum(second, axis=0, keepdims=True)

    last = count - 1

    def clamp(p):
        return jnp.minimum(p, last)

    for k in range(3):
        prepare(clamp(k))
    load(0, 0)

    def body(t, _):
        p = 2 * t

        def step(rows):
            load(p + 1, 1)
            work(p, 0, rows)
            work(p + 1, 1, rows)
            load(clamp(p + 2), 0)
            prepare(clamp(p + 3))
            prepare(clamp(p + 4))

        by_rows(jnp.maximum(counts[pa(p)], counts[pa(p + 1)]), step)
        return 0

    lax.fori_loop(0, count // 2, body, 0)


def column_sums(x):
    return jnp.sum(x.T, axis=0, keepdims=True)


def spreader(lanes):
    row = lax.broadcasted_iota(i32, (128, 128 * len(lanes)), 0)
    block = lax.broadcasted_iota(i32, (128, 128 * len(lanes)), 1) // 128
    hit = row < 0
    for n, k in enumerate(lanes):
        hit |= (block == n) & ((row == k) | (row == k + 8) | (row == k + 16))
    return jnp.where(hit, 1.0, 0.0).astype(bf16)


def expand(cols, bh, bm=None):
    matrix = spreader((102,) if bm is None else (102, 103))

    def one(c, _):
        wide = nn(cols[c], matrix)
        bh[c] = wide[:, 0:128]
        if bm is not None:
            bm[c] = wide[:, 128:256]
        return 0

    lax.fori_loop(0, CELLS, one, 0, unroll=4)


def put_right(ref, o, start, parts):
    ref[lax.rem(o, ref.shape[0]), start : start + 48, :] = stack16(right_parts(parts))


def density_prepare(o, rows, bf, hj, mj):
    full, norm, cross = basis(rows)
    put_right(bf, o, 0, right_distance(full, norm))
    hj[o] = rows[6:7]
    mj[o] = rows[7:8]
    return full, norm, cross


def state_kernel(pos, vel, mass, smooth, counts, state, cols):
    lane = lax.broadcasted_iota(i32, (1, PART), 1)

    def mine(c, _):
        one = pl.ds(c, 1)
        live = jnp.where(lane < counts[c], mass[one, :], 0.0)
        rows = jnp.concatenate(
            [pos[k, one, :] for k in range(3)]
            + [vel[k, one, :] for k in range(3)]
            + [smooth[one, :], live],
            axis=0,
        )
        state[c] = rows
        full, norm, cross = basis(rows)
        cols[c] = columns(
            left_parts(left_distance(full, norm))
            + left_parts(left_approach(full, cross))
            + list(split3(rows))
        ).astype(bf16)
        return 0

    lax.fori_loop(0, CELLS, mine, 0, unroll=4)


def own_density_kernel(
    after, state, cols, counts, pair_first, pair_offset, near,
    acc1, acc2, bh, bm, bf, hj, mj, dist0, dist1, pa, po, ps,
):
    del after
    expand(cols, bh, bm)
    bf[...] = jnp.zeros_like(bf)

    def mine(c, _):
        density_prepare(c, state[c], bf, hj, mj)
        return 0

    lax.fori_loop(0, CELLS, mine, 0, unroll=2)
    own_lists(pair_first, pair_offset, pa, po, ps, CELLS)
    acc1[...] = jnp.zeros_like(acc1)
    acc2[...] = jnp.zeros_like(acc2)
    refs = (bf, hj, mj, cols, bh, bm, (dist0, dist1))
    density_pairs(
        CELLS + PAIRS, counts, lambda p: pa[p], lambda p: po[p], lambda p: ps[p], refs,
        lambda p: None, acc1, acc2,
    )

    def total(c, _):
        near[c] = column_sums(acc1[c]) + acc2[c]
        return 0

    lax.fori_loop(0, CELLS, total, 0, unroll=2)


def far_density_kernel(
    near, far, counts, slot, proxy_cell, cols,
    acc1, ret, blocks, offset, block_own, live, size,
    acc2, bh, bm, bf, hj, mj, dist0, dist1, filled,
):
    del near
    total = pack_plan(far, slot, proxy_cell, offset, block_own, live, filled)
    size[0] = total
    expand(cols, bh, bm)
    bf[...] = jnp.zeros_like(bf)
    blocks[...] = jnp.zeros_like(blocks)

    def fill(e, _):
        pack(blocks, far[slot[e]], offset[e], live[e])
        return 0

    lax.fori_loop(0, SEND, fill, 0, unroll=8)
    acc2[...] = jnp.zeros_like(acc2)
    acc1[...] = jnp.zeros_like(acc1)
    refs = (bf, hj, mj, cols, bh, bm, (dist0, dist1))
    same = lambda p: p
    density_pairs(
        total, counts, lambda p: block_own[p], same, same, refs,
        lambda p: density_prepare(p, blocks[p], bf, hj, mj), acc1, acc2,
    )

    def back(e, _):
        ret[slot[e]] = unpack(acc2, offset[e])
        return 0

    lax.fori_loop(0, SEND, back, 0, unroll=8)


def add_by_goal(back, goals, sums):
    for part in sums:
        part[...] = jnp.zeros_like(part)

    def one(t, _):
        for k, part in enumerate(sums):
            s = t * len(sums) + k
            goal = goals[s]
            part[jnp.where(goal < 0, CELLS, goal)] += back[s]
        return 0

    lax.fori_loop(0, back.shape[0] // len(sums), one, 0, unroll=2)


def combine_density_kernel(
    back, goals, near, far, energy, counts, density, fluid, answer, *sums
):
    add_by_goal(back, goals, sums)
    lane = lax.broadcasted_iota(i32, (1, PART), 1)

    def cell(c, _):
        raw = W_SCALE * (near[c] + far[c] + sum(part[c] for part in sums))
        here = lane < counts[c]
        density[pl.ds(c, 1), :] = jnp.where(here, raw, 0.0)
        fluid[c] = jnp.concatenate(
            [jnp.where(here, raw, 1.0), energy[pl.ds(c, 1), :]], axis=0
        )
        return 0

    lax.fori_loop(0, CELLS, cell, 0, unroll=4)

    def send(s, _):
        answer[s] = fluid[jnp.maximum(goals[s], 0)]
        return 0

    lax.fori_loop(0, answer.shape[0], send, 0, unroll=8)


def slope_weights(r2, s, total_h):
    inv = pltpu.reciprocal(total_h, approx=True)
    inv2 = inv * inv
    q2 = jnp.maximum(r2, TINY) * inv2
    rs = lax.rsqrt(q2)
    q = q2 * rs
    u = 2.0 - q
    t = jnp.maximum(u, 0.0)
    grad = jnp.where(q < 1.0, 3.0 * u - 2.0, t * t * rs)
    m = jnp.minimum(s, 0.0) * (inv * pltpu.reciprocal(q2 + 0.01, approx=True))
    return grad * (inv2 * inv2 * inv), m


def fluid_weights(grad, m, total_c, total_p, total_r):
    return (total_p + m * (m - total_c) * pltpu.reciprocal(total_r, approx=True)) * grad


def force_fluid(fluid):
    rho, u = fluid[0:1], fluid[1:2]
    pressure = (GAMMA - 1.0) * u / rho
    sound = jnp.sqrt(GAMMA * (GAMMA - 1.0) * u)
    return pressure, sound, 4.0 * rho


def put_halves(ws, c, w):
    hi, lo = halves(w)
    ws[c : c + CHUNK, :] = hi
    ws[PART + c : PART + c + CHUNK, :] = lo


def fluid_work(ws, col, side_row, a, rows, grads):
    for c in range(0, rows, CHUNK):
        grad, m = grads(c)
        total = [
            two_wide(col[a, k, c : c + CHUNK, :], side_row[k + 1 : k + 2]) for k in range(3)
        ]
        put_halves(ws, c, fluid_weights(grad, m, *total))


def fold(x):
    return x[0:8] + x[8:16] + x[16:24]


def force_combine(own, other, ws):
    second = fold(nn(jnp.concatenate([own, own], axis=1), ws[...]))
    first = fold(nt(other, ws[...]))
    return first[:, 0:PART] + first[:, PART:], second


def full_force(first, count, counts, pa, po, refs, prepare, store):
    bd, bs, own_cf, other_cf, cols, bh, row, col, dist, appr, ws = refs

    def load(p, side):
        a, o = pa(p), lax.rem(po(p), bd.shape[0])
        dist[side][...] = nn(cols[a], bd[o])
        appr[side][...] = nn(cols[a], bs[o])

    def work(p, side, rows):
        a = pa(p)
        side_row = row[po(p)]

        def grads(c):
            return slope_weights(
                dist[side][c : c + CHUNK, :],
                appr[side][c : c + CHUNK, :],
                two_wide(bh[a, c : c + CHUNK, :], side_row[0:1]),
            )

        fluid_work(ws[side], col, side_row, a, rows, grads)

    def combine(p, side):
        return force_combine(own_cf[pa(p)], other_cf[po(p)], ws[side])

    pipeline(first, count, lambda p: counts[pa(p)], prepare, load, combine, store, work)


def geometry_prepare(o, rows, bd, bs):
    full, norm, cross = basis(rows)
    put_right(bd, o, 0, right_distance(full, norm))
    put_right(bs, o, 48, full)
    return full


def fluid_prepare(o, rows, full, fluid, cf, row):
    cf[o] = stack16(list(split3(rows[7:8] * full)))
    pressure, sound, rho4 = force_fluid(fluid)
    row[o] = jnp.concatenate(
        [rows[6:7], sound, pressure, rho4, jnp.zeros((4, PART), f32)], axis=0
    )


def own_fluid_columns(c, row, col, matrix):
    wide = nn(columns(list(split3(row[c]))).astype(bf16), matrix)
    for k in range(3):
        col[c, k] = wide[:, 128 * k : 128 * (k + 1)]


def sums_kernel(acc1, out):
    def total(c, _):
        out[c] = column_sums(acc1[c])
        return 0

    lax.fori_loop(0, CELLS, total, 0, unroll=4)


def force_sums(rows, sums):
    full, _, cross = basis(rows)
    count = sums[7:8]
    accel = (-0.5 * K_SCALE) * (full[0:3] * count - sums[0:3])
    mixed = jnp.sum(full[3:6] * sums[0:3] + full[0:3] * sums[3:6], axis=0, keepdims=True)
    heat = (0.25 * K_SCALE) * (cross * count - mixed + sums[6:7])
    return jnp.concatenate([accel, heat], axis=0)


def own_force_kernel(
    state, fluid, counts, pair_first, pair_offset, cols, total,
    acc1, acc2, bh, bd, bs, cf, row, col, dist0, dist1, appr0, appr1, ws0, ws1, pa, po, ps,
):
    expand(cols, bh)
    bd[...] = jnp.zeros_like(bd)
    bs[...] = jnp.zeros_like(bs)
    matrix = spreader((1, 2, 3))

    def mine(c, _):
        rows = state[c]
        fluid_prepare(c, rows, geometry_prepare(c, rows, bd, bs), fluid[c], cf, row)
        own_fluid_columns(c, row, col, matrix)
        return 0

    lax.fori_loop(0, CELLS, mine, 0, unroll=2)
    own_lists(pair_first, pair_offset, pa, po, ps, CELLS)
    acc1[...] = jnp.zeros_like(acc1)
    acc2[...] = jnp.zeros_like(acc2)
    ws0[...] = jnp.zeros_like(ws0)
    ws1[...] = jnp.zeros_like(ws1)
    refs = (bd, bs, cf, cf, cols, bh, row, col, (dist0, dist1), (appr0, appr1), (ws0, ws1))
    full_force(
        0, CELLS + PAIRS, counts, lambda p: pa[p], lambda p: po[p], refs, lambda p: None,
        lambda p, sums, valid: keep_sums(acc1, acc2, pa[p], ps[p], sums, valid),
    )
    total[...] = acc1[...] + acc2[0:CELLS]


def far_force_kernel(
    near, state, fluid, blocks, far_fluid, counts, slot, offset, block_own, live, size, cols,
    acc1, ret,
    acc2, bh, fluids, bd, bs, own_cf, own_row, cf, row, col, dist0, dist1, appr0, appr1, ws0, ws1,
):
    del near
    total = size[0]
    matrix = spreader((1, 2, 3))

    def mine(c, _):
        rows = state[c]
        fluid_prepare(c, rows, basis(rows)[0], fluid[c], own_cf, own_row)
        own_fluid_columns(c, own_row, col, matrix)
        return 0

    lax.fori_loop(0, CELLS, mine, 0, unroll=2)
    expand(cols, bh)
    bd[...] = jnp.zeros_like(bd)
    bs[...] = jnp.zeros_like(bs)
    fluids[...] = jnp.ones_like(fluids)

    def fill(e, _):
        pack(fluids, far_fluid[slot[e]], offset[e], live[e])
        return 0

    lax.fori_loop(0, SEND, fill, 0, unroll=8)
    acc1[...] = jnp.zeros_like(acc1)
    ws0[...] = jnp.zeros_like(ws0)
    ws1[...] = jnp.zeros_like(ws1)

    def prepare(p):
        rows = blocks[p]
        fluid_prepare(p, rows, geometry_prepare(p, rows, bd, bs), fluids[p], cf, row)

    def store(p, sums, valid):
        first, second = sums
        if valid is not True:
            first = first * jnp.where(valid, 1.0, 0.0)
        acc1[block_own[p]] += first
        acc2[p] = force_sums(blocks[p], second)

    refs = (
        bd, bs, own_cf, cf, cols, bh, row, col, (dist0, dist1), (appr0, appr1), (ws0, ws1),
    )
    same = lambda p: p
    full_force(0, total, counts, lambda p: block_own[p], same, refs, prepare, store)

    def back(e, _):
        ret[slot[e]] = unpack(acc2, offset[e])
        return 0

    lax.fori_loop(0, SEND, back, 0, unroll=8)


def finish_kernel(
    back, goals, near, far, state, energy, counts, mig_cell, mig_dest, accel, leave, moved, used, *sums
):
    add_by_goal(back, goals, sums)
    lane = lax.broadcasted_iota(i32, (1, PART), 1)

    def cell(c, _):
        rows = state[c]
        here = lane < counts[c]
        total = jnp.where(
            here, force_sums(rows, near[c] + far[c]) + sum(part[c] for part in sums), 0.0
        )
        accel[c] = total
        new_vel = rows[3:6] + STEP * total[0:3]
        new_pos = rows[0:3] + STEP * new_vel
        new_energy = energy[pl.ds(c, 1), :] + STEP * total[3:4]
        kicked = jnp.concatenate(
            [new_pos, new_vel, rows[7:8], rows[6:7], new_energy], axis=0
        )
        moved[c] = jnp.where(here, kicked, 0.0)
        return 0

    lax.fori_loop(0, CELLS, cell, 0)
    leave[...] = jnp.zeros_like(leave)

    def clear(d, _):
        used[d] = 0
        return 0

    lax.fori_loop(0, leave.shape[0], clear, 0)

    def entry(e, _):
        d = mig_dest[e]
        k = used[d]
        used[d] = k + 1
        full = moved[mig_cell[e]]
        for r in range(9):
            leave[d, r, pl.ds(k, 1), :] = full[r : r + 1]
        return 0

    lax.fori_loop(0, mig_cell.shape[0], entry, 0)


def inbox_kernel(came, out):
    for d in range(came.shape[0]):
        for r in range(came.shape[1]):
            out[r, d * CAPM : (d + 1) * CAPM, :] = came[d, r]


def vmem(*dims, dtype=f32):
    return pltpu.VMEM(dims, dtype)


def smem(*dims):
    return pltpu.SMEM(dims, i32)


WS = [vmem(2 * PART, PART, dtype=bf16)] * 2
SQUARE = [vmem(PART, PART)] * 2


def cell_state(position, velocity, mass, smoothing, counts):
    return kernel_call(
        state_kernel,
        (shape(CELLS, 8, PART), shape(CELLS, PART, 128, dtype=bf16)),
        [VMEM] * 4 + [SMEM],
        (VMEM, VMEM),
        flops=2**20,
        moved=2**22,
    )(position, velocity, mass, smoothing, counts)


def own_density(after, state, cols, counts, pair_first, pair_offset):
    return kernel_call(
        own_density_kernel,
        shape(CELLS, 1, PART),
        [ANY] + [VMEM] * 2 + [SMEM] * 3,
        VMEM,
        [
            vmem(CELLS, PART, 128),
            vmem(CELLS + 1, 1, PART),
            vmem(CELLS, PART, 128),
            vmem(CELLS, PART, 128),
            vmem(CELLS, 128, PART, dtype=bf16),
            vmem(CELLS, 1, PART),
            vmem(CELLS, 1, PART),
        ]
        + SQUARE
        + [smem(CELLS + PAIRS)] * 3,
        flops=32 * PART * PART * 300,
        moved=2**20,
    )(after, state, cols, counts, pair_first, pair_offset)


def far_density(near, far, counts, slot, proxy_cell, cols):
    return kernel_call(
        far_density_kernel,
        (
            shape(CELLS, PART, 128),
            shape(far.shape[0], 1, PART),
            shape(BLOCKS + 1, 8, PART),
            shape(SEND, dtype=i32),
            shape(BLOCKS, dtype=i32),
            shape(SEND, dtype=i32),
            shape(1, dtype=i32),
        ),
        [ANY, VMEM] + [SMEM] * 3 + [VMEM],
        (VMEM,) * 3 + (SMEM,) * 4,
        [
            vmem(BLOCKS + 1, 1, PART),
            vmem(CELLS, PART, 128),
            vmem(CELLS, PART, 128),
            vmem(RING, 128, PART, dtype=bf16),
            vmem(BLOCKS, 1, PART),
            vmem(BLOCKS, 1, PART),
        ]
        + SQUARE
        + [smem(CELLS)],
        flops=128 * PART * PART * 300,
        moved=2**20,
    )(near, far, counts, slot, proxy_cell, cols)


def far_force(
    near, state, fluid, far_fluid, counts, slot, blocks, offset, block_own, live, size, cols
):
    return kernel_call(
        far_force_kernel,
        (shape(CELLS, 8, PART), shape(far_fluid.shape[0], 4, PART)),
        [ANY] + [VMEM] * 4 + [SMEM] * 6 + [VMEM],
        (VMEM, VMEM),
        [
            vmem(BLOCKS + 1, 4, PART),
            vmem(CELLS, PART, 128),
            vmem(BLOCKS + 1, 2, PART),
            vmem(RING, 128, PART, dtype=bf16),
            vmem(RING, 128, PART, dtype=bf16),
            vmem(CELLS, 24, PART, dtype=bf16),
            vmem(CELLS, 8, PART),
            vmem(BLOCKS, 24, PART, dtype=bf16),
            vmem(BLOCKS, 8, PART),
            vmem(CELLS, 3, PART, 128),
        ]
        + SQUARE * 2
        + WS,
        flops=128 * PART * PART * 600,
        moved=2**20,
    )(
        near, state, fluid, blocks, far_fluid, counts, slot, offset, block_own, live, size,
        cols,
    )


def own_force(state, fluid, counts, pair_first, pair_offset, cols):
    return kernel_call(
        own_force_kernel,
        shape(CELLS, 8, PART),
        [VMEM] * 2 + [SMEM] * 3 + [VMEM],
        VMEM,
        [
            vmem(CELLS, 8, PART),
            vmem(CELLS + 1, 8, PART),
            vmem(CELLS, PART, 128),
            vmem(CELLS, 128, PART, dtype=bf16),
            vmem(CELLS, 128, PART, dtype=bf16),
            vmem(CELLS, 24, PART, dtype=bf16),
            vmem(CELLS, 8, PART),
            vmem(CELLS, 3, PART, 128),
        ]
        + SQUARE * 2
        + WS
        + [smem(CELLS + PAIRS)] * 3,
        flops=32 * PART * PART * 600,
        moved=2**20,
    )(state, fluid, counts, pair_first, pair_offset, cols)


def exchange(x, axes):
    return lax.all_to_all(x, axes, split_axis=0, concat_axis=0, tiled=True)


def local(
    position, velocity, mass, smoothing, energy, counts, proxy_cell, proxy_dest,
    proxy_target, pair_first, pair_offset, mig_cell, mig_dest,
):
    devices = lax.axis_size(("rows", "cols"))
    col_count = lax.axis_size("cols")
    slots = devices * CAP
    both = ("rows", "cols")
    req, slot = kernel_call(
        request_kernel,
        (shape(devices, 1, 128, dtype=i32), shape(SEND, dtype=i32)),
        [SMEM] * 2,
        (VMEM, SMEM),
        [smem(devices)],
        moved=2**20,
    )(proxy_dest[:, 0], proxy_target)
    goals = exchange(req, both)[:, 0, 0:CAP].reshape(slots)
    state, cols = cell_state(
        position.transpose(1, 0, 2), velocity.transpose(1, 0, 2), mass, smoothing, counts
    )
    answer = kernel_call(
        respond_kernel, shape(slots, 8, PART), [VMEM, SMEM], VMEM, moved=4 * 2**20
    )(state, goals)
    far = exchange(answer, both)
    near = own_density(answer, state, cols, counts, pair_first, pair_offset)
    acc1, ret, *plan = far_density(near, far, counts, slot, proxy_cell, cols)
    far_sums = kernel_call(
        sums_kernel, shape(CELLS, 1, PART), [VMEM], VMEM, flops=2**20, moved=2**21
    )(acc1)
    back = exchange(ret, both)
    density, fluid, answer2 = kernel_call(
        combine_density_kernel,
        (shape(CELLS, PART), shape(CELLS, 2, PART), shape(slots, 2, PART)),
        [VMEM, SMEM] + [VMEM] * 3 + [SMEM],
        (VMEM, VMEM, VMEM),
        [vmem(CELLS + 1, 1, PART)] * 4,
        moved=2**20,
    )(back, goals, near, far_sums, energy, counts)
    far_fluid = exchange(answer2, both)
    near_force = own_force(state, fluid, counts, pair_first, pair_offset, cols)
    far_force_sums, ret4 = far_force(
        near_force, state, fluid, far_fluid, counts, slot, *plan, cols
    )
    back4 = exchange(ret4, both)
    accel, leave = kernel_call(
        finish_kernel,
        (shape(CELLS, 4, PART), shape(col_count, 9, CAPM, PART)),
        [VMEM, SMEM] + [VMEM] * 4 + [SMEM] * 3,
        (VMEM, VMEM),
        [vmem(CELLS, 9, PART), smem(col_count)] + [vmem(CELLS + 1, 4, PART)] * 4,
        moved=2**20,
    )(
        back4, goals, near_force, far_force_sums, state, energy, counts, mig_cell,
        mig_dest[:, 0],
    )
    arrived = kernel_call(
        inbox_kernel, shape(9, col_count * CAPM, PART), [VMEM], VMEM, moved=2**20
    )(exchange(leave, "cols"))
    return (density, accel, arrived.transpose(1, 0, 2))


def solution(mesh):
    lead = ("rows", "cols")
    one, two, three = P(lead), P(lead, None), P(lead, None, None)
    return jax.shard_map(
        local,
        mesh=mesh,
        in_specs=(three, three, two, two, two, one, one, two, one, one, one, one, two),
        out_specs=(two, three, three),
        check_vma=False,
    )
```

```python
import jax
import jax.numpy as jnp
from jax import lax
from jax.experimental import pallas as pl
from jax.experimental.pallas import tpu as pltpu
from jax.sharding import PartitionSpec as P

CAP = 2
CAPM = 2
CELLS = 16
SEND = 128
PAIRS = 16
PART = 256

GAMMA = 5.0 / 3.0
STEP = 0.02
PI = 3.141592653589793
W_SCALE = 2.0 / PI
K_SCALE = -24.0 / PI
TINY = 1e-12
CHUNK = 32
ROWS = (128, 160, 192, 224, 256)
BLOCKS = SEND + CELLS
RING = 8

f32, bf16, i32 = jnp.float32, jnp.bfloat16, jnp.int32
VMEM = pl.BlockSpec(memory_space=pltpu.VMEM)
ANY = pl.BlockSpec(memory_space=pl.ANY)
SMEM = pl.BlockSpec(memory_space=pltpu.SMEM)
LIMIT = 56 * 2**20


def shape(*dims, dtype=f32):
    return jax.ShapeDtypeStruct(dims, dtype)


def kernel_call(body, out_shape, in_specs, out_specs, scratch=(), flops=0, moved=0):
    return pl.pallas_call(
        body,
        out_shape=out_shape,
        in_specs=in_specs,
        out_specs=out_specs,
        scratch_shapes=list(scratch),
        compiler_params=pltpu.CompilerParams(vmem_limit_bytes=LIMIT),
        cost_estimate=pl.CostEstimate(flops=flops, bytes_accessed=moved, transcendentals=0),
    )


def sublane():
    return lax.broadcasted_iota(i32, (8, PART), 0)


def split3(x):
    a = x.astype(bf16).astype(f32)
    b = (x - a).astype(bf16).astype(f32)
    return a, b, x - a - b


def left_parts(x):
    a, b, c = split3(x)
    return [a, a, b, b, a, c]


def right_parts(x):
    a, b, c = split3(x)
    return [a, b, a, b, c, a]


def stack16(parts):
    return jnp.concatenate(parts, axis=0).astype(bf16)


def basis(rows):
    row = sublane()
    place = jnp.where(row < 3, 2.0 * rows - 1.0, rows)
    first = place[0:3]
    norm = jnp.sum(first * first, axis=0, keepdims=True)
    cross = jnp.sum(first * place[3:6], axis=0, keepdims=True)
    full = jnp.where(row < 6, place, jnp.where(row == 6, cross, 1.0))
    return full, norm, cross


def right_distance(full, norm):
    row = sublane()
    return jnp.where(
        row < 3, full, jnp.where(row == 3, norm, jnp.where(row == 4, 1.0, 0.0))
    )


def left_distance(full, norm):
    row = sublane()
    return jnp.where(
        row < 3, -2.0 * full, jnp.where(row == 3, 1.0, jnp.where(row == 4, norm, 0.0))
    )


def left_approach(full, cross):
    return 4.0 * jnp.concatenate(
        [-full[3:6], -full[0:3], jnp.ones((1, PART), f32), cross], axis=0
    )


def columns(parts):
    fill = 128 - 8 * len(parts)
    return jnp.concatenate(parts + [jnp.zeros((fill, PART), f32)], axis=0).T


def halves(w):
    hi = w.astype(bf16)
    return hi, (w - hi.astype(f32)).astype(bf16)


def request_kernel(dest, target, req, slot, used):
    req[...] = jnp.full_like(req, -1)

    def clear(d, _):
        used[d] = 0
        return 0

    lax.fori_loop(0, req.shape[0], clear, 0, unroll=8)
    short = lax.broadcasted_iota(i32, (1, 128), 1)

    def entry(e, _):
        d = dest[e]
        k = used[d]
        used[d] = k + 1
        slot[e] = d * CAP + k
        req[d] = jnp.where(short == k, target[e], req[d])
        return 0

    lax.fori_loop(0, SEND, entry, 0, unroll=4)


def respond_kernel(state, goals, out):
    def one(s, _):
        goal = jnp.maximum(goals[s], 0)
        out[s] = state[goal]
        return 0

    lax.fori_loop(0, out.shape[0], one, 0, unroll=4)


def by_rows(need, step):
    low = 0
    for rows in ROWS:
        pl.when((need > low) & (need <= rows))(lambda rows=rows: step(rows))
        low = rows


def pipeline(first, count, rows_of, prepare, load, combine, store, work):
    last = first + count - 1

    def clamp(p):
        return jnp.minimum(p, last)

    for k in range(3):
        prepare(clamp(first + k))
    load(first, 0)

    def body(t, _):
        p = first + 2 * t

        def step(rows):
            before = jnp.maximum(p - 1, first)
            sums = combine(before, 1)
            work(p, 0, rows)
            load(p + 1, 1)
            sums0 = combine(p, 0)
            work(p + 1, 1, rows)
            load(clamp(p + 2), 0)
            store(before, sums, t > 0)
            store(p, sums0, True)
            prepare(clamp(p + 3))
            prepare(clamp(p + 4))

        by_rows(jnp.maximum(rows_of(p), rows_of(p + 1)), step)
        return 0

    lax.fori_loop(0, count // 2, body, 0)
    store(last, combine(last, 1), True)


def keep_sums(acc1, acc2, a, s, sums, valid):
    if valid is not True:
        keep = jnp.where(valid, 1.0, 0.0)
        sums = (sums[0] * keep, sums[1] * keep)
    acc1[a] += sums[0]
    acc2[s] += sums[1]


def pack_plan(far, slot, proxy_cell, offset, block_own, live, filled):
    def clear(c, _):
        filled[c] = 0
        return 0

    lax.fori_loop(0, CELLS, clear, 0)

    def measure(e, _):
        mass = far[slot[e]][7:8]
        n = jnp.sum(jnp.where(mass > 0.0, 1.0, 0.0)).astype(i32)
        live[e] = n
        a = proxy_cell[e]
        offset[e] = filled[a]
        filled[a] = filled[a] + n
        return 0

    lax.fori_loop(0, SEND, measure, 0, unroll=16)

    def place(c, total):
        blocks = (filled[c] + PART - 1) // PART
        filled[c] = total * PART

        def name(t, _):
            block_own[total + t] = c
            return 0

        lax.fori_loop(0, blocks, name, 0)
        return total + blocks

    total = lax.fori_loop(0, CELLS, place, 0)

    def shift(e, _):
        offset[e] = offset[e] + filled[proxy_cell[e]]
        return 0

    lax.fori_loop(0, SEND, shift, 0, unroll=8)
    block_own[total] = block_own[total - 1]
    return total + lax.rem(total, 2)


def pack(target, rows, offset, n):
    t = offset // PART
    lane0 = offset - t * PART
    lane = lax.broadcasted_iota(i32, rows.shape, 1)
    turned = pltpu.roll(rows, lane0, 1)
    pltpu.store(target.at[t], turned, mask=(lane >= lane0) & (lane < lane0 + n))
    pltpu.store(target.at[t + 1], turned, mask=lane < lane0 + n - PART)


def unpack(source, offset):
    t = offset // PART
    lane0 = offset - t * PART
    first, second = source[t], source[t + 1]
    lane = lax.broadcasted_iota(i32, first.shape, 1)
    return pltpu.roll(jnp.where(lane >= lane0, first, second), lax.rem(PART - lane0, PART), 1)


def own_lists(pair_first, pair_offset, pa, po, ps, dummy):
    def one(e, _):
        pa[e] = e
        po[e] = e
        ps[e] = dummy
        a = pair_first[e]
        b = lax.rem(a + pair_offset[e], CELLS)
        pa[CELLS + e] = a
        po[CELLS + e] = b
        ps[CELLS + e] = b
        return 0

    lax.fori_loop(0, CELLS, one, 0)


def nn(a, b):
    return jnp.dot(a, b, preferred_element_type=f32)


def nt(a, b):
    return lax.dot_general(a, b, (((1,), (1,)), ((), ())), preferred_element_type=f32)


def density_weights(r2, total_h):
    inv = pltpu.reciprocal(total_h, approx=True)
    inv2 = inv * inv
    q2 = jnp.maximum(r2, TINY) * inv2
    q = q2 * lax.rsqrt(q2)
    u = 2.0 - q
    t = jnp.maximum(u, 0.0)
    return jnp.minimum(t * t * t, 4.0 - 3.0 * (q2 * u)) * (inv2 * inv)


def two_wide(col, row):
    return jnp.concatenate([col, col], axis=1) + row


def density_pairs(count, counts, pa, po, ps, refs, prepare, acc1, acc2):
    bf, hj, mj, cols, bh, bm, dist = refs

    def load(p, side):
        dist[side][...] = nn(cols[pa(p)], bf[lax.rem(po(p), bf.shape[0])])

    def work(p, side, rows):
        a, o = pa(p), po(p)
        h_j, m_j = hj[o], mj[o]
        second = jnp.zeros((8, PART), f32)
        for c in range(0, rows, CHUNK):
            w = density_weights(
                dist[side][c : c + CHUNK, :], two_wide(bh[a, c : c + CHUNK, :], h_j)
            )
            first = w * m_j
            acc1[a, c : c + CHUNK, :] += first[:, 0:128] + first[:, 128:256]
            m_i = bm[a, c : c + CHUNK, :]
            other = w * jnp.concatenate([m_i, m_i], axis=1)
            second += jnp.sum(other.reshape(CHUNK // 8, 8, PART), axis=0)
        acc2[ps(p)] += jnp.sum(second, axis=0, keepdims=True)

    last = count - 1

    def clamp(p):
        return jnp.minimum(p, last)

    for k in range(3):
        prepare(clamp(k))
    load(0, 0)

    def body(t, _):
        p = 2 * t

        def step(rows):
            load(p + 1, 1)
            work(p, 0, rows)
            work(p + 1, 1, rows)
            load(clamp(p + 2), 0)
            prepare(clamp(p + 3))
            prepare(clamp(p + 4))

        by_rows(jnp.maximum(counts[pa(p)], counts[pa(p + 1)]), step)
        return 0

    lax.fori_loop(0, count // 2, body, 0)


def column_sums(x):
    return jnp.sum(x.T, axis=0, keepdims=True)


def spreader(lanes):
    row = lax.broadcasted_iota(i32, (128, 128 * len(lanes)), 0)
    block = lax.broadcasted_iota(i32, (128, 128 * len(lanes)), 1) // 128
    hit = row < 0
    for n, k in enumerate(lanes):
        hit |= (block == n) & ((row == k) | (row == k + 8) | (row == k + 16))
    return jnp.where(hit, 1.0, 0.0).astype(bf16)


def expand(cols, bh, bm=None):
    matrix = spreader((102,) if bm is None else (102, 103))

    def one(c, _):
        wide = nn(cols[c], matrix)
        bh[c] = wide[:, 0:128]
        if bm is not None:
            bm[c] = wide[:, 128:256]
        return 0

    lax.fori_loop(0, CELLS, one, 0, unroll=4)


def put_right(ref, o, start, parts):
    ref[lax.rem(o, ref.shape[0]), start : start + 48, :] = stack16(right_parts(parts))


def density_prepare(o, rows, bf, hj, mj):
    full, norm, cross = basis(rows)
    put_right(bf, o, 0, right_distance(full, norm))
    hj[o] = rows[6:7]
    mj[o] = rows[7:8]
    return full, norm, cross


def state_kernel(pos, vel, mass, smooth, counts, state, cols):
    lane = lax.broadcasted_iota(i32, (1, PART), 1)

    def mine(c, _):
        one = pl.ds(c, 1)
        live = jnp.where(lane < counts[c], mass[one, :], 0.0)
        rows = jnp.concatenate(
            [pos[k, one, :] for k in range(3)]
            + [vel[k, one, :] for k in range(3)]
            + [smooth[one, :], live],
            axis=0,
        )
        state[c] = rows
        full, norm, cross = basis(rows)
        cols[c] = columns(
            left_parts(left_distance(full, norm))
            + left_parts(left_approach(full, cross))
            + list(split3(rows))
        ).astype(bf16)
        return 0

    lax.fori_loop(0, CELLS, mine, 0, unroll=4)


def own_density_kernel(
    after, state, cols, counts, pair_first, pair_offset, near,
    acc1, acc2, bh, bm, bf, hj, mj, dist0, dist1, pa, po, ps,
):
    del after
    expand(cols, bh, bm)
    bf[...] = jnp.zeros_like(bf)

    def mine(c, _):
        density_prepare(c, state[c], bf, hj, mj)
        return 0

    lax.fori_loop(0, CELLS, mine, 0, unroll=2)
    own_lists(pair_first, pair_offset, pa, po, ps, CELLS)
    acc1[...] = jnp.zeros_like(acc1)
    acc2[...] = jnp.zeros_like(acc2)
    refs = (bf, hj, mj, cols, bh, bm, (dist0, dist1))
    density_pairs(
        CELLS + PAIRS, counts, lambda p: pa[p], lambda p: po[p], lambda p: ps[p], refs,
        lambda p: None, acc1, acc2,
    )

    def total(c, _):
        near[c] = column_sums(acc1[c]) + acc2[c]
        return 0

    lax.fori_loop(0, CELLS, total, 0, unroll=2)


def far_density_kernel(
    near, far, counts, slot, proxy_cell, cols,
    acc1, ret, blocks, offset, block_own, live, size,
    acc2, bh, bm, bf, hj, mj, dist0, dist1, filled,
):
    del near
    total = pack_plan(far, slot, proxy_cell, offset, block_own, live, filled)
    size[0] = total
    expand(cols, bh, bm)
    bf[...] = jnp.zeros_like(bf)
    blocks[...] = jnp.zeros_like(blocks)

    def fill(e, _):
        pack(blocks, far[slot[e]], offset[e], live[e])
        return 0

    lax.fori_loop(0, SEND, fill, 0, unroll=8)
    acc2[...] = jnp.zeros_like(acc2)
    acc1[...] = jnp.zeros_like(acc1)
    refs = (bf, hj, mj, cols, bh, bm, (dist0, dist1))
    same = lambda p: p
    density_pairs(
        total, counts, lambda p: block_own[p], same, same, refs,
        lambda p: density_prepare(p, blocks[p], bf, hj, mj), acc1, acc2,
    )

    def back(e, _):
        ret[slot[e]] = unpack(acc2, offset[e])
        return 0

    lax.fori_loop(0, SEND, back, 0, unroll=8)


def add_by_goal(back, goals, sums):
    for part in sums:
        part[...] = jnp.zeros_like(part)

    def one(t, _):
        for k, part in enumerate(sums):
            s = t * len(sums) + k
            goal = goals[s]
            part[jnp.where(goal < 0, CELLS, goal)] += back[s]
        return 0

    lax.fori_loop(0, back.shape[0] // len(sums), one, 0, unroll=2)


def combine_density_kernel(
    back, goals, near, far, energy, counts, density, fluid, answer, *sums
):
    add_by_goal(back, goals, sums)
    lane = lax.broadcasted_iota(i32, (1, PART), 1)

    def cell(c, _):
        raw = W_SCALE * (near[c] + far[c] + sum(part[c] for part in sums))
        here = lane < counts[c]
        density[pl.ds(c, 1), :] = jnp.where(here, raw, 0.0)
        fluid[c] = jnp.concatenate(
            [jnp.where(here, raw, 1.0), energy[pl.ds(c, 1), :]], axis=0
        )
        return 0

    lax.fori_loop(0, CELLS, cell, 0, unroll=4)

    def send(s, _):
        answer[s] = fluid[jnp.maximum(goals[s], 0)]
        return 0

    lax.fori_loop(0, answer.shape[0], send, 0, unroll=8)


def slope_weights(r2, s, total_h):
    inv = pltpu.reciprocal(total_h, approx=True)
    inv2 = inv * inv
    q2 = jnp.maximum(r2, TINY) * inv2
    rs = lax.rsqrt(q2)
    q = q2 * rs
    u = 2.0 - q
    t = jnp.maximum(u, 0.0)
    grad = jnp.where(q < 1.0, 3.0 * u - 2.0, t * t * rs)
    m = jnp.minimum(s, 0.0) * (inv * pltpu.reciprocal(q2 + 0.01, approx=True))
    return grad * (inv2 * inv2 * inv), m


def fluid_weights(grad, m, total_c, total_p, total_r):
    return (total_p + m * (m - total_c) * pltpu.reciprocal(total_r, approx=True)) * grad


def force_fluid(fluid):
    rho, u = fluid[0:1], fluid[1:2]
    pressure = (GAMMA - 1.0) * u / rho
    sound = jnp.sqrt(GAMMA * (GAMMA - 1.0) * u)
    return pressure, sound, 4.0 * rho


def put_halves(ws, c, w):
    hi, lo = halves(w)
    ws[c : c + CHUNK, :] = hi
    ws[PART + c : PART + c + CHUNK, :] = lo


def fluid_work(ws, col, side_row, a, rows, grads):
    for c in range(0, rows, CHUNK):
        grad, m = grads(c)
        total = [
            two_wide(col[a, k, c : c + CHUNK, :], side_row[k + 1 : k + 2]) for k in range(3)
        ]
        put_halves(ws, c, fluid_weights(grad, m, *total))


def fold(x):
    return x[0:8] + x[8:16] + x[16:24]


def force_combine(own, other, ws):
    second = fold(nn(jnp.concatenate([own, own], axis=1), ws[...]))
    first = fold(nt(other, ws[...]))
    return first[:, 0:PART] + first[:, PART:], second


def full_force(first, count, counts, pa, po, refs, prepare, store):
    bd, bs, own_cf, other_cf, cols, bh, row, col, dist, appr, ws = refs

    def load(p, side):
        a, o = pa(p), lax.rem(po(p), bd.shape[0])
        dist[side][...] = nn(cols[a], bd[o])
        appr[side][...] = nn(cols[a], bs[o])

    def work(p, side, rows):
        a = pa(p)
        side_row = row[po(p)]

        def grads(c):
            return slope_weights(
                dist[side][c : c + CHUNK, :],
                appr[side][c : c + CHUNK, :],
                two_wide(bh[a, c : c + CHUNK, :], side_row[0:1]),
            )

        fluid_work(ws[side], col, side_row, a, rows, grads)

    def combine(p, side):
        return force_combine(own_cf[pa(p)], other_cf[po(p)], ws[side])

    pipeline(first, count, lambda p: counts[pa(p)], prepare, load, combine, store, work)


def geometry_prepare(o, rows, bd, bs):
    full, norm, cross = basis(rows)
    put_right(bd, o, 0, right_distance(full, norm))
    put_right(bs, o, 48, full)
    return full


def fluid_prepare(o, rows, full, fluid, cf, row):
    cf[o] = stack16(list(split3(rows[7:8] * full)))
    pressure, sound, rho4 = force_fluid(fluid)
    row[o] = jnp.concatenate(
        [rows[6:7], sound, pressure, rho4, jnp.zeros((4, PART), f32)], axis=0
    )


def own_fluid_columns(c, row, col, matrix):
    wide = nn(columns(list(split3(row[c]))).astype(bf16), matrix)
    for k in range(3):
        col[c, k] = wide[:, 128 * k : 128 * (k + 1)]


def sums_kernel(acc1, out):
    def total(c, _):
        out[c] = column_sums(acc1[c])
        return 0

    lax.fori_loop(0, CELLS, total, 0, unroll=4)


def force_sums(rows, sums):
    full, _, cross = basis(rows)
    count = sums[7:8]
    accel = (-0.5 * K_SCALE) * (full[0:3] * count - sums[0:3])
    mixed = jnp.sum(full[3:6] * sums[0:3] + full[0:3] * sums[3:6], axis=0, keepdims=True)
    heat = (0.25 * K_SCALE) * (cross * count - mixed + sums[6:7])
    return jnp.concatenate([accel, heat], axis=0)


def fluid_kernel(state, fluid, cols, own_cf, own_row, col, bh):
    matrix = spreader((1, 2, 3))
    expand(cols, bh)

    def mine(c, _):
        rows = state[c]
        fluid_prepare(c, rows, basis(rows)[0], fluid[c], own_cf, own_row)
        own_fluid_columns(c, own_row, col, matrix)
        return 0

    lax.fori_loop(0, CELLS, mine, 0, unroll=4)


def own_force_kernel(
    after, state, counts, pair_first, pair_offset, cols, cf, row, col, bh, total,
    acc1, acc2, bd, bs, dist0, dist1, appr0, appr1, ws0, ws1, pa, po, ps,
):
    del after
    bd[...] = jnp.zeros_like(bd)
    bs[...] = jnp.zeros_like(bs)

    def mine(c, _):
        geometry_prepare(c, state[c], bd, bs)
        return 0

    lax.fori_loop(0, CELLS, mine, 0, unroll=4)
    own_lists(pair_first, pair_offset, pa, po, ps, CELLS)
    acc1[...] = jnp.zeros_like(acc1)
    acc2[...] = jnp.zeros_like(acc2)
    ws0[...] = jnp.zeros_like(ws0)
    ws1[...] = jnp.zeros_like(ws1)
    refs = (bd, bs, cf, cf, cols, bh, row, col, (dist0, dist1), (appr0, appr1), (ws0, ws1))
    full_force(
        0, CELLS + PAIRS, counts, lambda p: pa[p], lambda p: po[p], refs, lambda p: None,
        lambda p, sums, valid: keep_sums(acc1, acc2, pa[p], ps[p], sums, valid),
    )
    total[...] = acc1[...] + acc2[0:CELLS]


def far_force_kernel(
    blocks, far_fluid, counts, slot, offset, block_own, live, size, cols, own_cf, col, bh,
    acc1, ret,
    acc2, fluids, bd, bs, cf, row, dist0, dist1, appr0, appr1, ws0, ws1,
):
    total = size[0]
    bd[...] = jnp.zeros_like(bd)
    bs[...] = jnp.zeros_like(bs)
    fluids[...] = jnp.ones_like(fluids)

    def fill(e, _):
        pack(fluids, far_fluid[slot[e]], offset[e], live[e])
        return 0

    lax.fori_loop(0, SEND, fill, 0, unroll=8)
    acc1[...] = jnp.zeros_like(acc1)
    ws0[...] = jnp.zeros_like(ws0)
    ws1[...] = jnp.zeros_like(ws1)

    def prepare(p):
        rows = blocks[p]
        fluid_prepare(p, rows, geometry_prepare(p, rows, bd, bs), fluids[p], cf, row)

    def store(p, sums, valid):
        first, second = sums
        if valid is not True:
            first = first * jnp.where(valid, 1.0, 0.0)
        acc1[block_own[p]] += first
        acc2[p] = force_sums(blocks[p], second)

    refs = (
        bd, bs, own_cf, cf, cols, bh, row, col, (dist0, dist1), (appr0, appr1), (ws0, ws1),
    )
    same = lambda p: p
    full_force(0, total, counts, lambda p: block_own[p], same, refs, prepare, store)

    def back(e, _):
        ret[slot[e]] = unpack(acc2, offset[e])
        return 0

    lax.fori_loop(0, SEND, back, 0, unroll=8)


def finish_kernel(
    back, goals, near, far, state, energy, counts, mig_cell, mig_dest, accel, leave, moved, used, *sums
):
    add_by_goal(back, goals, sums)
    lane = lax.broadcasted_iota(i32, (1, PART), 1)

    def cell(c, _):
        rows = state[c]
        here = lane < counts[c]
        total = jnp.where(
            here, force_sums(rows, near[c] + far[c]) + sum(part[c] for part in sums), 0.0
        )
        accel[c] = total
        new_vel = rows[3:6] + STEP * total[0:3]
        new_pos = rows[0:3] + STEP * new_vel
        new_energy = energy[pl.ds(c, 1), :] + STEP * total[3:4]
        kicked = jnp.concatenate(
            [new_pos, new_vel, rows[7:8], rows[6:7], new_energy], axis=0
        )
        moved[c] = jnp.where(here, kicked, 0.0)
        return 0

    lax.fori_loop(0, CELLS, cell, 0)
    leave[...] = jnp.zeros_like(leave)

    def clear(d, _):
        used[d] = 0
        return 0

    lax.fori_loop(0, leave.shape[0], clear, 0)

    def entry(e, _):
        d = mig_dest[e]
        k = used[d]
        used[d] = k + 1
        full = moved[mig_cell[e]]
        for r in range(9):
            leave[d, r, pl.ds(k, 1), :] = full[r : r + 1]
        return 0

    lax.fori_loop(0, mig_cell.shape[0], entry, 0)


def inbox_kernel(came, out):
    for d in range(came.shape[0]):
        for r in range(came.shape[1]):
            out[r, d * CAPM : (d + 1) * CAPM, :] = came[d, r]


def vmem(*dims, dtype=f32):
    return pltpu.VMEM(dims, dtype)


def smem(*dims):
    return pltpu.SMEM(dims, i32)


WS = [vmem(2 * PART, PART, dtype=bf16)] * 2
SQUARE = [vmem(PART, PART)] * 2


def cell_state(position, velocity, mass, smoothing, counts):
    return kernel_call(
        state_kernel,
        (shape(CELLS, 8, PART), shape(CELLS, PART, 128, dtype=bf16)),
        [VMEM] * 4 + [SMEM],
        (VMEM, VMEM),
        flops=2**20,
        moved=2**22,
    )(position, velocity, mass, smoothing, counts)


def own_density(after, state, cols, counts, pair_first, pair_offset):
    return kernel_call(
        own_density_kernel,
        shape(CELLS, 1, PART),
        [ANY] + [VMEM] * 2 + [SMEM] * 3,
        VMEM,
        [
            vmem(CELLS, PART, 128),
            vmem(CELLS + 1, 1, PART),
            vmem(CELLS, PART, 128),
            vmem(CELLS, PART, 128),
            vmem(CELLS, 128, PART, dtype=bf16),
            vmem(CELLS, 1, PART),
            vmem(CELLS, 1, PART),
        ]
        + SQUARE
        + [smem(CELLS + PAIRS)] * 3,
        flops=32 * PART * PART * 300,
        moved=2**20,
    )(after, state, cols, counts, pair_first, pair_offset)


def far_density(near, far, counts, slot, proxy_cell, cols):
    return kernel_call(
        far_density_kernel,
        (
            shape(CELLS, PART, 128),
            shape(far.shape[0], 1, PART),
            shape(BLOCKS + 1, 8, PART),
            shape(SEND, dtype=i32),
            shape(BLOCKS, dtype=i32),
            shape(SEND, dtype=i32),
            shape(1, dtype=i32),
        ),
        [ANY, VMEM] + [SMEM] * 3 + [VMEM],
        (VMEM,) * 3 + (SMEM,) * 4,
        [
            vmem(BLOCKS + 1, 1, PART),
            vmem(CELLS, PART, 128),
            vmem(CELLS, PART, 128),
            vmem(RING, 128, PART, dtype=bf16),
            vmem(BLOCKS, 1, PART),
            vmem(BLOCKS, 1, PART),
        ]
        + SQUARE
        + [smem(CELLS)],
        flops=128 * PART * PART * 300,
        moved=2**20,
    )(near, far, counts, slot, proxy_cell, cols)


def own_fluid(state, fluid, cols):
    return kernel_call(
        fluid_kernel,
        (
            shape(CELLS, 24, PART, dtype=bf16),
            shape(CELLS, 8, PART),
            shape(CELLS, 3, PART, 128),
            shape(CELLS, PART, 128),
        ),
        [VMEM] * 3,
        (VMEM,) * 4,
        flops=2**22,
        moved=2**24,
    )(state, fluid, cols)


def far_force(
    far_fluid, counts, slot, blocks, offset, block_own, live, size, cols, own_cf, col, bh
):
    return kernel_call(
        far_force_kernel,
        (shape(CELLS, 8, PART), shape(far_fluid.shape[0], 4, PART)),
        [VMEM] * 2 + [SMEM] * 6 + [VMEM] * 4,
        (VMEM, VMEM),
        [
            vmem(BLOCKS + 1, 4, PART),
            vmem(BLOCKS + 1, 2, PART),
            vmem(RING, 128, PART, dtype=bf16),
            vmem(RING, 128, PART, dtype=bf16),
            vmem(BLOCKS, 24, PART, dtype=bf16),
            vmem(BLOCKS, 8, PART),
        ]
        + SQUARE * 2
        + WS,
        flops=128 * PART * PART * 600,
        moved=2**20,
    )(blocks, far_fluid, counts, slot, offset, block_own, live, size, cols, own_cf, col, bh)


def own_force(after, state, counts, pair_first, pair_offset, cols, cf, row, col, bh):
    return kernel_call(
        own_force_kernel,
        shape(CELLS, 8, PART),
        [ANY, VMEM] + [SMEM] * 3 + [VMEM] * 5,
        VMEM,
        [
            vmem(CELLS, 8, PART),
            vmem(CELLS + 1, 8, PART),
            vmem(CELLS, 128, PART, dtype=bf16),
            vmem(CELLS, 128, PART, dtype=bf16),
        ]
        + SQUARE * 2
        + WS
        + [smem(CELLS + PAIRS)] * 3,
        flops=32 * PART * PART * 600,
        moved=2**20,
    )(after, state, counts, pair_first, pair_offset, cols, cf, row, col, bh)


def exchange(x, axes):
    return lax.all_to_all(x, axes, split_axis=0, concat_axis=0, tiled=True)


def local(
    position, velocity, mass, smoothing, energy, counts, proxy_cell, proxy_dest,
    proxy_target, pair_first, pair_offset, mig_cell, mig_dest,
):
    devices = lax.axis_size(("rows", "cols"))
    col_count = lax.axis_size("cols")
    slots = devices * CAP
    both = ("rows", "cols")
    req, slot = kernel_call(
        request_kernel,
        (shape(devices, 1, 128, dtype=i32), shape(SEND, dtype=i32)),
        [SMEM] * 2,
        (VMEM, SMEM),
        [smem(devices)],
        moved=2**20,
    )(proxy_dest[:, 0], proxy_target)
    goals = exchange(req, both)[:, 0, 0:CAP].reshape(slots)
    state, cols = cell_state(
        position.transpose(1, 0, 2), velocity.transpose(1, 0, 2), mass, smoothing, counts
    )
    answer = kernel_call(
        respond_kernel, shape(slots, 8, PART), [VMEM, SMEM], VMEM, moved=4 * 2**20
    )(state, goals)
    far = exchange(answer, both)
    near = own_density(answer, state, cols, counts, pair_first, pair_offset)
    acc1, ret, *plan = far_density(near, far, counts, slot, proxy_cell, cols)
    far_sums = kernel_call(
        sums_kernel, shape(CELLS, 1, PART), [VMEM], VMEM, flops=2**20, moved=2**21
    )(acc1)
    back = exchange(ret, both)
    density, fluid, answer2 = kernel_call(
        combine_density_kernel,
        (shape(CELLS, PART), shape(CELLS, 2, PART), shape(slots, 2, PART)),
        [VMEM, SMEM] + [VMEM] * 3 + [SMEM],
        (VMEM, VMEM, VMEM),
        [vmem(CELLS + 1, 1, PART)] * 4,
        moved=2**20,
    )(back, goals, near, far_sums, energy, counts)
    far_fluid = exchange(answer2, both)
    own_cf, own_row, col, bh = own_fluid(state, fluid, cols)
    far_force_sums, ret4 = far_force(far_fluid, counts, slot, *plan, cols, own_cf, col, bh)
    near_force = own_force(
        far_force_sums, state, counts, pair_first, pair_offset, cols, own_cf, own_row, col, bh
    )
    back4 = exchange(ret4, both)
    accel, leave = kernel_call(
        finish_kernel,
        (shape(CELLS, 4, PART), shape(col_count, 9, CAPM, PART)),
        [VMEM, SMEM] + [VMEM] * 4 + [SMEM] * 3,
        (VMEM, VMEM),
        [vmem(CELLS, 9, PART), smem(col_count)] + [vmem(CELLS + 1, 4, PART)] * 4,
        moved=2**20,
    )(
        back4, goals, near_force, far_force_sums, state, energy, counts, mig_cell,
        mig_dest[:, 0],
    )
    arrived = kernel_call(
        inbox_kernel, shape(9, col_count * CAPM, PART), [VMEM], VMEM, moved=2**20
    )(exchange(leave, "cols"))
    return (density, accel, arrived.transpose(1, 0, 2))


def solution(mesh):
    lead = ("rows", "cols")
    one, two, three = P(lead), P(lead, None), P(lead, None, None)
    return jax.shard_map(
        local,
        mesh=mesh,
        in_specs=(three, three, two, two, two, one, one, two, one, one, one, one, two),
        out_specs=(two, three, three),
        check_vma=False,
    )
```

```python
import jax
import jax.numpy as jnp
from jax import lax
from jax.experimental import pallas as pl
from jax.experimental.pallas import tpu as pltpu
from jax.sharding import PartitionSpec as P

CAP = 2
CAPM = 2
CELLS = 16
SEND = 128
PAIRS = 16
PART = 256

GAMMA = 5.0 / 3.0
STEP = 0.02
PI = 3.141592653589793
W_SCALE = 2.0 / PI
K_SCALE = -24.0 / PI
TINY = 1e-12
CHUNK = 32
ROWS = (128, 160, 192, 224, 256)
BLOCKS = SEND + CELLS
WIDE = 4
RING = 4 * WIDE

f32, bf16, i32 = jnp.float32, jnp.bfloat16, jnp.int32
VMEM = pl.BlockSpec(memory_space=pltpu.VMEM)
ANY = pl.BlockSpec(memory_space=pl.ANY)
SMEM = pl.BlockSpec(memory_space=pltpu.SMEM)
LIMIT = 56 * 2**20


def shape(*dims, dtype=f32):
    return jax.ShapeDtypeStruct(dims, dtype)


def kernel_call(body, out_shape, in_specs, out_specs, scratch=(), flops=0, moved=0):
    return pl.pallas_call(
        body,
        out_shape=out_shape,
        in_specs=in_specs,
        out_specs=out_specs,
        scratch_shapes=list(scratch),
        compiler_params=pltpu.CompilerParams(vmem_limit_bytes=LIMIT),
        cost_estimate=pl.CostEstimate(flops=flops, bytes_accessed=moved, transcendentals=0),
    )


def sublane():
    return lax.broadcasted_iota(i32, (8, PART), 0)


def split3(x):
    a = x.astype(bf16).astype(f32)
    b = (x - a).astype(bf16).astype(f32)
    return a, b, x - a - b


def left_parts(x):
    a, b, c = split3(x)
    return [a, a, b, b, a, c]


def right_parts(x):
    a, b, c = split3(x)
    return [a, b, a, b, c, a]


def stack16(parts):
    return jnp.concatenate(parts, axis=0).astype(bf16)


def basis(rows):
    row = sublane()
    place = jnp.where(row < 3, 2.0 * rows - 1.0, rows)
    first = place[0:3]
    norm = jnp.sum(first * first, axis=0, keepdims=True)
    cross = jnp.sum(first * place[3:6], axis=0, keepdims=True)
    full = jnp.where(row < 6, place, jnp.where(row == 6, cross, 1.0))
    return full, norm, cross


def right_distance(full, norm):
    row = sublane()
    return jnp.where(
        row < 3, full, jnp.where(row == 3, norm, jnp.where(row == 4, 1.0, 0.0))
    )


def left_distance(full, norm):
    row = sublane()
    return jnp.where(
        row < 3, -2.0 * full, jnp.where(row == 3, 1.0, jnp.where(row == 4, norm, 0.0))
    )


def left_approach(full, cross):
    return 4.0 * jnp.concatenate(
        [-full[3:6], -full[0:3], jnp.ones((1, PART), f32), cross], axis=0
    )


def columns(parts):
    fill = 128 - 8 * len(parts)
    return jnp.concatenate(parts + [jnp.zeros((fill, PART), f32)], axis=0).T


def halves(w):
    hi = w.astype(bf16)
    return hi, (w - hi.astype(f32)).astype(bf16)


def request_kernel(dest, target, req, slot, used):
    req[...] = jnp.full_like(req, -1)

    def clear(d, _):
        used[d] = 0
        return 0

    lax.fori_loop(0, req.shape[0], clear, 0, unroll=8)
    short = lax.broadcasted_iota(i32, (1, 128), 1)

    def entry(e, _):
        d = dest[e]
        k = used[d]
        used[d] = k + 1
        slot[e] = d * CAP + k
        req[d] = jnp.where(short == k, target[e], req[d])
        return 0

    lax.fori_loop(0, SEND, entry, 0, unroll=4)


def respond_kernel(state, goals, out):
    def one(s, _):
        goal = jnp.maximum(goals[s], 0)
        out[s] = state[goal]
        return 0

    lax.fori_loop(0, out.shape[0], one, 0, unroll=4)


def by_rows(need, step):
    low = 0
    for rows in ROWS:
        pl.when((need > low) & (need <= rows))(lambda rows=rows: step(rows))
        low = rows


def pipeline(count, rows_of, prepare, load, work, combine=None, store=None):
    last = count - 1

    def clamp(p):
        return jnp.minimum(p, last)

    for k in range(2 * WIDE):
        prepare(clamp(k))
    for k in range(WIDE):
        load(clamp(k), k)

    def body(t, _):
        p = WIDE * t
        need = rows_of(p)
        for k in range(1, WIDE):
            need = jnp.maximum(need, rows_of(p + k))

        def step(rows):
            before = jnp.maximum(p - 1, 0)
            done = []
            if combine is not None:
                done.append((before, combine(before, WIDE - 1), t > 0))
            for k in range(WIDE):
                work(p + k, k, rows)
                load(clamp(p + WIDE + k), k)
                if combine is not None and k < WIDE - 1:
                    done.append((p + k, combine(p + k, k), True))
            for item in done:
                store(*item)
            for k in range(WIDE):
                prepare(clamp(p + 2 * WIDE + k))

        by_rows(need, step)
        return 0

    lax.fori_loop(0, count // WIDE, body, 0)
    if combine is not None:
        store(last, combine(last, WIDE - 1), True)


def keep_sums(acc1, acc2, a, s, sums, valid):
    if valid is not True:
        keep = jnp.where(valid, 1.0, 0.0)
        sums = (sums[0] * keep, sums[1] * keep)
    acc1[a] += sums[0]
    acc2[s] += sums[1]


def pack_plan(far, slot, proxy_cell, offset, block_own, live, filled):
    def clear(c, _):
        filled[c] = 0
        return 0

    lax.fori_loop(0, CELLS, clear, 0)

    def measure(e, _):
        mass = far[slot[e]][7:8]
        n = jnp.sum(jnp.where(mass > 0.0, 1.0, 0.0)).astype(i32)
        live[e] = n
        a = proxy_cell[e]
        offset[e] = filled[a]
        filled[a] = filled[a] + n
        return 0

    lax.fori_loop(0, SEND, measure, 0, unroll=16)

    def place(c, total):
        blocks = (filled[c] + PART - 1) // PART
        filled[c] = total * PART

        def name(t, _):
            block_own[total + t] = c
            return 0

        lax.fori_loop(0, blocks, name, 0)
        return total + blocks

    total = lax.fori_loop(0, CELLS, place, 0)

    def shift(e, _):
        offset[e] = offset[e] + filled[proxy_cell[e]]
        return 0

    lax.fori_loop(0, SEND, shift, 0, unroll=8)
    for k in range(WIDE - 1):
        block_own[jnp.minimum(total + k, BLOCKS - 1)] = block_own[total - 1]
    return (total + WIDE - 1) // WIDE * WIDE


def pack(target, rows, offset, n):
    t = offset // PART
    lane0 = offset - t * PART
    lane = lax.broadcasted_iota(i32, rows.shape, 1)
    turned = pltpu.roll(rows, lane0, 1)
    pltpu.store(target.at[t], turned, mask=(lane >= lane0) & (lane < lane0 + n))
    pltpu.store(target.at[t + 1], turned, mask=lane < lane0 + n - PART)


def unpack(source, offset):
    t = offset // PART
    lane0 = offset - t * PART
    first, second = source[t], source[t + 1]
    lane = lax.broadcasted_iota(i32, first.shape, 1)
    return pltpu.roll(jnp.where(lane >= lane0, first, second), lax.rem(PART - lane0, PART), 1)


def own_lists(pair_first, pair_offset, pa, po, ps, dummy):
    def one(e, _):
        pa[e] = e
        po[e] = e
        ps[e] = dummy
        a = pair_first[e]
        b = lax.rem(a + pair_offset[e], CELLS)
        pa[CELLS + e] = a
        po[CELLS + e] = b
        ps[CELLS + e] = b
        return 0

    lax.fori_loop(0, CELLS, one, 0)


def nn(a, b):
    return jnp.dot(a, b, preferred_element_type=f32)


def nt(a, b):
    return lax.dot_general(a, b, (((1,), (1,)), ((), ())), preferred_element_type=f32)


def density_weights(r2, total_h):
    inv = pltpu.reciprocal(total_h, approx=True)
    inv2 = inv * inv
    q2 = jnp.maximum(r2, TINY) * inv2
    q = q2 * lax.rsqrt(q2)
    u = 2.0 - q
    t = jnp.maximum(u, 0.0)
    return jnp.minimum(t * t * t, 4.0 - 3.0 * (q2 * u)) * (inv2 * inv)


def two_wide(col, row):
    return jnp.concatenate([col, col], axis=1) + row


def density_pairs(count, counts, pa, po, ps, refs, prepare, acc1, acc2):
    bf, hj, mj, cols, bh, bm, dist = refs

    def load(p, side):
        dist[side][...] = nn(cols[pa(p)], bf[lax.rem(po(p), bf.shape[0])])

    def work(p, side, rows):
        a, o = pa(p), po(p)
        h_j, m_j = hj[o], mj[o]
        second = jnp.zeros((8, PART), f32)
        for c in range(0, rows, CHUNK):
            w = density_weights(
                dist[side][c : c + CHUNK, :], two_wide(bh[a, c : c + CHUNK, :], h_j)
            )
            first = w * m_j
            acc1[a, c : c + CHUNK, :] += first[:, 0:128] + first[:, 128:256]
            m_i = bm[a, c : c + CHUNK, :]
            other = w * jnp.concatenate([m_i, m_i], axis=1)
            second += jnp.sum(other.reshape(CHUNK // 8, 8, PART), axis=0)
        acc2[ps(p)] += jnp.sum(second, axis=0, keepdims=True)

    pipeline(count, lambda p: counts[pa(p)], prepare, load, work)


def column_sums(x):
    return jnp.sum(x.T, axis=0, keepdims=True)


def spreader(lanes):
    row = lax.broadcasted_iota(i32, (128, 128 * len(lanes)), 0)
    block = lax.broadcasted_iota(i32, (128, 128 * len(lanes)), 1) // 128
    hit = row < 0
    for n, k in enumerate(lanes):
        hit |= (block == n) & ((row == k) | (row == k + 8) | (row == k + 16))
    return jnp.where(hit, 1.0, 0.0).astype(bf16)


def expand(cols, bh, bm=None):
    matrix = spreader((102,) if bm is None else (102, 103))

    def one(c, _):
        wide = nn(cols[c], matrix)
        bh[c] = wide[:, 0:128]
        if bm is not None:
            bm[c] = wide[:, 128:256]
        return 0

    lax.fori_loop(0, CELLS, one, 0, unroll=4)


def put_right(ref, o, start, parts):
    ref[lax.rem(o, ref.shape[0]), start : start + 48, :] = stack16(right_parts(parts))


def density_prepare(o, rows, bf, hj, mj):
    full, norm, cross = basis(rows)
    put_right(bf, o, 0, right_distance(full, norm))
    hj[o] = rows[6:7]
    mj[o] = rows[7:8]
    return full, norm, cross


def state_kernel(pos, vel, mass, smooth, counts, state, cols):
    lane = lax.broadcasted_iota(i32, (1, PART), 1)

    def mine(c, _):
        one = pl.ds(c, 1)
        live = jnp.where(lane < counts[c], mass[one, :], 0.0)
        rows = jnp.concatenate(
            [pos[k, one, :] for k in range(3)]
            + [vel[k, one, :] for k in range(3)]
            + [smooth[one, :], live],
            axis=0,
        )
        state[c] = rows
        full, norm, cross = basis(rows)
        cols[c] = columns(
            left_parts(left_distance(full, norm))
            + left_parts(left_approach(full, cross))
            + list(split3(rows))
        ).astype(bf16)
        return 0

    lax.fori_loop(0, CELLS, mine, 0, unroll=4)


def own_density_kernel(
    after, state, cols, counts, pair_first, pair_offset, near,
    acc1, acc2, bh, bm, bf, hj, mj, pa, po, ps, *dist,
):
    del after
    expand(cols, bh, bm)
    bf[...] = jnp.zeros_like(bf)

    def mine(c, _):
        density_prepare(c, state[c], bf, hj, mj)
        return 0

    lax.fori_loop(0, CELLS, mine, 0, unroll=2)
    own_lists(pair_first, pair_offset, pa, po, ps, CELLS)
    acc1[...] = jnp.zeros_like(acc1)
    acc2[...] = jnp.zeros_like(acc2)
    refs = (bf, hj, mj, cols, bh, bm, dist)
    density_pairs(
        CELLS + PAIRS, counts, lambda p: pa[p], lambda p: po[p], lambda p: ps[p], refs,
        lambda p: None, acc1, acc2,
    )

    def total(c, _):
        near[c] = column_sums(acc1[c]) + acc2[c]
        return 0

    lax.fori_loop(0, CELLS, total, 0, unroll=2)


def far_density_kernel(
    near, far, counts, slot, proxy_cell, cols,
    acc1, ret, blocks, offset, block_own, live, size,
    acc2, bh, bm, bf, hj, mj, filled, *dist,
):
    del near
    total = pack_plan(far, slot, proxy_cell, offset, block_own, live, filled)
    size[0] = total
    expand(cols, bh, bm)
    bf[...] = jnp.zeros_like(bf)
    blocks[...] = jnp.zeros_like(blocks)

    def fill(e, _):
        pack(blocks, far[slot[e]], offset[e], live[e])
        return 0

    lax.fori_loop(0, SEND, fill, 0, unroll=8)
    acc2[...] = jnp.zeros_like(acc2)
    acc1[...] = jnp.zeros_like(acc1)
    refs = (bf, hj, mj, cols, bh, bm, dist)
    same = lambda p: p
    density_pairs(
        total, counts, lambda p: block_own[p], same, same, refs,
        lambda p: density_prepare(p, blocks[p], bf, hj, mj), acc1, acc2,
    )

    def back(e, _):
        ret[slot[e]] = unpack(acc2, offset[e])
        return 0

    lax.fori_loop(0, SEND, back, 0, unroll=8)


def add_by_goal(back, goals, sums):
    for part in sums:
        part[...] = jnp.zeros_like(part)

    def one(t, _):
        for k, part in enumerate(sums):
            s = t * len(sums) + k
            goal = goals[s]
            part[jnp.where(goal < 0, CELLS, goal)] += back[s]
        return 0

    lax.fori_loop(0, back.shape[0] // len(sums), one, 0, unroll=2)


def combine_density_kernel(
    back, goals, near, far, energy, counts, density, fluid, answer, *sums
):
    add_by_goal(back, goals, sums)
    lane = lax.broadcasted_iota(i32, (1, PART), 1)

    def cell(c, _):
        raw = W_SCALE * (near[c] + far[c] + sum(part[c] for part in sums))
        here = lane < counts[c]
        density[pl.ds(c, 1), :] = jnp.where(here, raw, 0.0)
        fluid[c] = jnp.concatenate(
            [jnp.where(here, raw, 1.0), energy[pl.ds(c, 1), :]], axis=0
        )
        return 0

    lax.fori_loop(0, CELLS, cell, 0, unroll=4)

    def send(s, _):
        answer[s] = fluid[jnp.maximum(goals[s], 0)]
        return 0

    lax.fori_loop(0, answer.shape[0], send, 0, unroll=8)


def slope_weights(r2, s, total_h):
    inv = pltpu.reciprocal(total_h, approx=True)
    inv2 = inv * inv
    q2 = jnp.maximum(r2, TINY) * inv2
    rs = lax.rsqrt(q2)
    q = q2 * rs
    u = 2.0 - q
    t = jnp.maximum(u, 0.0)
    grad = jnp.where(q < 1.0, 3.0 * u - 2.0, t * t * rs)
    m = jnp.minimum(s, 0.0) * (inv * pltpu.reciprocal(q2 + 0.01, approx=True))
    return grad * (inv2 * inv2 * inv), m


def fluid_weights(grad, m, total_c, total_p, total_r):
    return (total_p + m * (m - total_c) * pltpu.reciprocal(total_r, approx=True)) * grad


def force_fluid(fluid):
    rho, u = fluid[0:1], fluid[1:2]
    pressure = (GAMMA - 1.0) * u / rho
    sound = jnp.sqrt(GAMMA * (GAMMA - 1.0) * u)
    return pressure, sound, 4.0 * rho


def put_halves(ws, c, w):
    hi, lo = halves(w)
    ws[c : c + CHUNK, :] = hi
    ws[PART + c : PART + c + CHUNK, :] = lo


def fluid_work(ws, col, side_row, a, rows, grads):
    for c in range(0, rows, CHUNK):
        grad, m = grads(c)
        total = [
            two_wide(col[a, k, c : c + CHUNK, :], side_row[k + 1 : k + 2]) for k in range(3)
        ]
        put_halves(ws, c, fluid_weights(grad, m, *total))


def fold(x):
    return x[0:8] + x[8:16] + x[16:24]


def force_combine(own, other, ws):
    second = fold(nn(jnp.concatenate([own, own], axis=1), ws[...]))
    first = fold(nt(other, ws[...]))
    return first[:, 0:PART] + first[:, PART:], second


def full_force(count, counts, pa, po, refs, prepare, store):
    bd, bs, own_cf, other_cf, cols, bh, row, col, dist, appr, ws = refs

    def load(p, side):
        a, o = pa(p), lax.rem(po(p), bd.shape[0])
        dist[side][...] = nn(cols[a], bd[o])
        appr[side][...] = nn(cols[a], bs[o])

    def work(p, side, rows):
        a = pa(p)
        side_row = row[po(p)]

        def grads(c):
            return slope_weights(
                dist[side][c : c + CHUNK, :],
                appr[side][c : c + CHUNK, :],
                two_wide(bh[a, c : c + CHUNK, :], side_row[0:1]),
            )

        fluid_work(ws[side], col, side_row, a, rows, grads)

    def combine(p, side):
        return force_combine(own_cf[pa(p)], other_cf[po(p)], ws[side])

    pipeline(count, lambda p: counts[pa(p)], prepare, load, work, combine, store)


def geometry_prepare(o, rows, bd, bs):
    full, norm, cross = basis(rows)
    put_right(bd, o, 0, right_distance(full, norm))
    put_right(bs, o, 48, full)
    return full


def fluid_prepare(o, rows, full, fluid, cf, row):
    cf[o] = stack16(list(split3(rows[7:8] * full)))
    pressure, sound, rho4 = force_fluid(fluid)
    row[o] = jnp.concatenate(
        [rows[6:7], sound, pressure, rho4, jnp.zeros((4, PART), f32)], axis=0
    )


def own_fluid_columns(c, row, col, matrix):
    wide = nn(columns(list(split3(row[c]))).astype(bf16), matrix)
    for k in range(3):
        col[c, k] = wide[:, 128 * k : 128 * (k + 1)]


def sums_kernel(acc1, out):
    def total(c, _):
        out[c] = column_sums(acc1[c])
        return 0

    lax.fori_loop(0, CELLS, total, 0, unroll=4)


def force_sums(rows, sums):
    full, _, cross = basis(rows)
    count = sums[7:8]
    accel = (-0.5 * K_SCALE) * (full[0:3] * count - sums[0:3])
    mixed = jnp.sum(full[3:6] * sums[0:3] + full[0:3] * sums[3:6], axis=0, keepdims=True)
    heat = (0.25 * K_SCALE) * (cross * count - mixed + sums[6:7])
    return jnp.concatenate([accel, heat], axis=0)


def fluid_kernel(state, fluid, cols, own_cf, own_row, col, bh):
    matrix = spreader((1, 2, 3))
    expand(cols, bh)

    def mine(c, _):
        rows = state[c]
        fluid_prepare(c, rows, basis(rows)[0], fluid[c], own_cf, own_row)
        own_fluid_columns(c, own_row, col, matrix)
        return 0

    lax.fori_loop(0, CELLS, mine, 0, unroll=4)


def own_force_kernel(
    after, state, counts, pair_first, pair_offset, cols, cf, row, col, bh, total,
    acc1, acc2, bd, bs, pa, po, ps, *wide,
):
    del after
    bd[...] = jnp.zeros_like(bd)
    bs[...] = jnp.zeros_like(bs)

    def mine(c, _):
        geometry_prepare(c, state[c], bd, bs)
        return 0

    lax.fori_loop(0, CELLS, mine, 0, unroll=4)
    own_lists(pair_first, pair_offset, pa, po, ps, CELLS)
    acc1[...] = jnp.zeros_like(acc1)
    acc2[...] = jnp.zeros_like(acc2)
    dist, appr, ws = wide[:WIDE], wide[WIDE : 2 * WIDE], wide[2 * WIDE :]
    for part in ws:
        part[...] = jnp.zeros_like(part)
    refs = (bd, bs, cf, cf, cols, bh, row, col, dist, appr, ws)
    full_force(
        CELLS + PAIRS, counts, lambda p: pa[p], lambda p: po[p], refs, lambda p: None,
        lambda p, sums, valid: keep_sums(acc1, acc2, pa[p], ps[p], sums, valid),
    )
    total[...] = acc1[...] + acc2[0:CELLS]


def far_force_kernel(
    blocks, far_fluid, counts, slot, offset, block_own, live, size, cols, own_cf, col_far, bh_far,
    acc1, ret,
    acc2, fluids, bd, bs, cf, row, col, bh, sems, *wide,
):
    total = size[0]
    copies = [
        pltpu.make_async_copy(col_far, col, sems.at[0]),
        pltpu.make_async_copy(bh_far, bh, sems.at[1]),
    ]
    for copy in copies:
        copy.start()
    bd[...] = jnp.zeros_like(bd)
    bs[...] = jnp.zeros_like(bs)
    fluids[...] = jnp.ones_like(fluids)

    def fill(e, _):
        pack(fluids, far_fluid[slot[e]], offset[e], live[e])
        return 0

    lax.fori_loop(0, SEND, fill, 0, unroll=8)
    acc1[...] = jnp.zeros_like(acc1)
    dist, appr, ws = wide[:WIDE], wide[WIDE : 2 * WIDE], wide[2 * WIDE :]
    for part in ws:
        part[...] = jnp.zeros_like(part)

    def prepare(p):
        rows = blocks[p]
        fluid_prepare(p, rows, geometry_prepare(p, rows, bd, bs), fluids[p], cf, row)

    def store(p, sums, valid):
        first, second = sums
        if valid is not True:
            first = first * jnp.where(valid, 1.0, 0.0)
        acc1[block_own[p]] += first
        acc2[p] = force_sums(blocks[p], second)

    refs = (
        bd, bs, own_cf, cf, cols, bh, row, col, dist, appr, ws,
    )
    for copy in copies:
        copy.wait()
    same = lambda p: p
    full_force(total, counts, lambda p: block_own[p], same, refs, prepare, store)

    def back(e, _):
        ret[slot[e]] = unpack(acc2, offset[e])
        return 0

    lax.fori_loop(0, SEND, back, 0, unroll=8)


def finish_kernel(
    back, goals, near, far, state, energy, counts, mig_cell, mig_dest, accel, leave, moved, used, *sums
):
    add_by_goal(back, goals, sums)
    lane = lax.broadcasted_iota(i32, (1, PART), 1)

    def cell(c, _):
        rows = state[c]
        here = lane < counts[c]
        total = jnp.where(
            here, force_sums(rows, near[c] + far[c]) + sum(part[c] for part in sums), 0.0
        )
        accel[c] = total
        new_vel = rows[3:6] + STEP * total[0:3]
        new_pos = rows[0:3] + STEP * new_vel
        new_energy = energy[pl.ds(c, 1), :] + STEP * total[3:4]
        kicked = jnp.concatenate(
            [new_pos, new_vel, rows[7:8], rows[6:7], new_energy], axis=0
        )
        moved[c] = jnp.where(here, kicked, 0.0)
        return 0

    lax.fori_loop(0, CELLS, cell, 0)
    leave[...] = jnp.zeros_like(leave)

    def clear(d, _):
        used[d] = 0
        return 0

    lax.fori_loop(0, leave.shape[0], clear, 0)

    def entry(e, _):
        d = mig_dest[e]
        k = used[d]
        used[d] = k + 1
        full = moved[mig_cell[e]]
        for r in range(9):
            leave[d, r, pl.ds(k, 1), :] = full[r : r + 1]
        return 0

    lax.fori_loop(0, mig_cell.shape[0], entry, 0)


def inbox_kernel(came, out):
    for d in range(came.shape[0]):
        for r in range(came.shape[1]):
            out[r, d * CAPM : (d + 1) * CAPM, :] = came[d, r]


def vmem(*dims, dtype=f32):
    return pltpu.VMEM(dims, dtype)


def smem(*dims):
    return pltpu.SMEM(dims, i32)


WS = [vmem(2 * PART, PART, dtype=bf16)] * WIDE
SQUARE = [vmem(PART, PART)] * WIDE


def cell_state(position, velocity, mass, smoothing, counts):
    return kernel_call(
        state_kernel,
        (shape(CELLS, 8, PART), shape(CELLS, PART, 128, dtype=bf16)),
        [VMEM] * 4 + [SMEM],
        (VMEM, VMEM),
        flops=2**20,
        moved=2**22,
    )(position, velocity, mass, smoothing, counts)


def own_density(after, state, cols, counts, pair_first, pair_offset):
    return kernel_call(
        own_density_kernel,
        shape(CELLS, 1, PART),
        [ANY] + [VMEM] * 2 + [SMEM] * 3,
        VMEM,
        [
            vmem(CELLS, PART, 128),
            vmem(CELLS + 1, 1, PART),
            vmem(CELLS, PART, 128),
            vmem(CELLS, PART, 128),
            vmem(CELLS, 128, PART, dtype=bf16),
            vmem(CELLS, 1, PART),
            vmem(CELLS, 1, PART),
        ]
        + [smem(CELLS + PAIRS)] * 3
        + SQUARE,
        flops=32 * PART * PART * 300,
        moved=2**20,
    )(after, state, cols, counts, pair_first, pair_offset)


def far_density(near, far, counts, slot, proxy_cell, cols):
    return kernel_call(
        far_density_kernel,
        (
            shape(CELLS, PART, 128),
            shape(far.shape[0], 1, PART),
            shape(BLOCKS + 1, 8, PART),
            shape(SEND, dtype=i32),
            shape(BLOCKS, dtype=i32),
            shape(SEND, dtype=i32),
            shape(1, dtype=i32),
        ),
        [ANY, VMEM] + [SMEM] * 3 + [VMEM],
        (VMEM,) * 3 + (SMEM,) * 4,
        [
            vmem(BLOCKS + 1, 1, PART),
            vmem(CELLS, PART, 128),
            vmem(CELLS, PART, 128),
            vmem(RING, 128, PART, dtype=bf16),
            vmem(BLOCKS, 1, PART),
            vmem(BLOCKS, 1, PART),
        ]
        + [smem(CELLS)]
        + SQUARE,
        flops=128 * PART * PART * 300,
        moved=2**20,
    )(near, far, counts, slot, proxy_cell, cols)


def own_fluid(state, fluid, cols):
    return kernel_call(
        fluid_kernel,
        (
            shape(CELLS, 24, PART, dtype=bf16),
            shape(CELLS, 8, PART),
            shape(CELLS, 3, PART, 128),
            shape(CELLS, PART, 128),
        ),
        [VMEM] * 3,
        (VMEM,) * 4,
        flops=2**22,
        moved=2**24,
    )(state, fluid, cols)


def far_force(
    far_fluid, counts, slot, blocks, offset, block_own, live, size, cols, own_cf, col, bh
):
    return kernel_call(
        far_force_kernel,
        (shape(CELLS, 8, PART), shape(far_fluid.shape[0], 4, PART)),
        [VMEM] * 2 + [SMEM] * 6 + [VMEM] * 2 + [ANY] * 2,
        (VMEM, VMEM),
        [
            vmem(BLOCKS + 1, 4, PART),
            vmem(BLOCKS + 1, 2, PART),
            vmem(RING, 128, PART, dtype=bf16),
            vmem(RING, 128, PART, dtype=bf16),
            vmem(BLOCKS, 24, PART, dtype=bf16),
            vmem(BLOCKS, 8, PART),
            vmem(CELLS, 3, PART, 128),
            vmem(CELLS, PART, 128),
            pltpu.SemaphoreType.DMA((2,)),
        ]
        + SQUARE * 2
        + WS,
        flops=128 * PART * PART * 600,
        moved=2**20,
    )(blocks, far_fluid, counts, slot, offset, block_own, live, size, cols, own_cf, col, bh)


def own_force(after, state, counts, pair_first, pair_offset, cols, cf, row, col, bh):
    return kernel_call(
        own_force_kernel,
        shape(CELLS, 8, PART),
        [ANY, VMEM] + [SMEM] * 3 + [VMEM] * 5,
        VMEM,
        [
            vmem(CELLS, 8, PART),
            vmem(CELLS + 1, 8, PART),
            vmem(CELLS, 128, PART, dtype=bf16),
            vmem(CELLS, 128, PART, dtype=bf16),
        ]
        + [smem(CELLS + PAIRS)] * 3
        + SQUARE * 2
        + WS,
        flops=32 * PART * PART * 600,
        moved=2**20,
    )(after, state, counts, pair_first, pair_offset, cols, cf, row, col, bh)


def exchange(x, axes):
    return lax.all_to_all(x, axes, split_axis=0, concat_axis=0, tiled=True)


def local(
    position, velocity, mass, smoothing, energy, counts, proxy_cell, proxy_dest,
    proxy_target, pair_first, pair_offset, mig_cell, mig_dest,
):
    devices = lax.axis_size(("rows", "cols"))
    col_count = lax.axis_size("cols")
    slots = devices * CAP
    both = ("rows", "cols")
    req, slot = kernel_call(
        request_kernel,
        (shape(devices, 1, 128, dtype=i32), shape(SEND, dtype=i32)),
        [SMEM] * 2,
        (VMEM, SMEM),
        [smem(devices)],
        moved=2**20,
    )(proxy_dest[:, 0], proxy_target)
    goals = exchange(req, both)[:, 0, 0:CAP].reshape(slots)
    state, cols = cell_state(
        position.transpose(1, 0, 2), velocity.transpose(1, 0, 2), mass, smoothing, counts
    )
    answer = kernel_call(
        respond_kernel, shape(slots, 8, PART), [VMEM, SMEM], VMEM, moved=4 * 2**20
    )(state, goals)
    far = exchange(answer, both)
    near = own_density(answer, state, cols, counts, pair_first, pair_offset)
    acc1, ret, *plan = far_density(near, far, counts, slot, proxy_cell, cols)
    far_sums = kernel_call(
        sums_kernel, shape(CELLS, 1, PART), [VMEM], VMEM, flops=2**20, moved=2**21
    )(acc1)
    back = exchange(ret, both)
    density, fluid, answer2 = kernel_call(
        combine_density_kernel,
        (shape(CELLS, PART), shape(CELLS, 2, PART), shape(slots, 2, PART)),
        [VMEM, SMEM] + [VMEM] * 3 + [SMEM],
        (VMEM, VMEM, VMEM),
        [vmem(CELLS + 1, 1, PART)] * 4,
        moved=2**20,
    )(back, goals, near, far_sums, energy, counts)
    far_fluid = exchange(answer2, both)
    own_cf, own_row, col, bh = own_fluid(state, fluid, cols)
    far_force_sums, ret4 = far_force(far_fluid, counts, slot, *plan, cols, own_cf, col, bh)
    near_force = own_force(
        far_force_sums, state, counts, pair_first, pair_offset, cols, own_cf, own_row, col, bh
    )
    back4 = exchange(ret4, both)
    accel, leave = kernel_call(
        finish_kernel,
        (shape(CELLS, 4, PART), shape(col_count, 9, CAPM, PART)),
        [VMEM, SMEM] + [VMEM] * 4 + [SMEM] * 3,
        (VMEM, VMEM),
        [vmem(CELLS, 9, PART), smem(col_count)] + [vmem(CELLS + 1, 4, PART)] * 4,
        moved=2**20,
    )(
        back4, goals, near_force, far_force_sums, state, energy, counts, mig_cell,
        mig_dest[:, 0],
    )
    arrived = kernel_call(
        inbox_kernel, shape(9, col_count * CAPM, PART), [VMEM], VMEM, moved=2**20
    )(exchange(leave, "cols"))
    return (density, accel, arrived.transpose(1, 0, 2))


def solution(mesh):
    lead = ("rows", "cols")
    one, two, three = P(lead), P(lead, None), P(lead, None, None)
    return jax.shard_map(
        local,
        mesh=mesh,
        in_specs=(three, three, two, two, two, one, one, two, one, one, one, one, two),
        out_specs=(two, three, three),
        check_vma=False,
    )
```

```python
import jax
import jax.numpy as jnp
from jax import lax
from jax.experimental import pallas as pl
from jax.experimental.pallas import tpu as pltpu
from jax.sharding import PartitionSpec as P

CAP = 2
CAPM = 2
CELLS = 16
SEND = 128
PAIRS = 16
PART = 256

GAMMA = 5.0 / 3.0
STEP = 0.02
PI = 3.141592653589793
W_SCALE = 2.0 / PI
K_SCALE = -24.0 / PI
TINY = 1e-12
CHUNK = 32
ROWS = (128, 160, 192, 224, 256)
BLOCKS = SEND + CELLS
WIDE = 4
RING = 4 * WIDE

f32, bf16, i32 = jnp.float32, jnp.bfloat16, jnp.int32
VMEM = pl.BlockSpec(memory_space=pltpu.VMEM)
ANY = pl.BlockSpec(memory_space=pl.ANY)
SMEM = pl.BlockSpec(memory_space=pltpu.SMEM)
LIMIT = 56 * 2**20


def shape(*dims, dtype=f32):
    return jax.ShapeDtypeStruct(dims, dtype)


def kernel_call(body, out_shape, in_specs, out_specs, scratch=(), flops=0, moved=0):
    return pl.pallas_call(
        body,
        out_shape=out_shape,
        in_specs=in_specs,
        out_specs=out_specs,
        scratch_shapes=list(scratch),
        compiler_params=pltpu.CompilerParams(vmem_limit_bytes=LIMIT),
        cost_estimate=pl.CostEstimate(flops=flops, bytes_accessed=moved, transcendentals=0),
    )


def sublane():
    return lax.broadcasted_iota(i32, (8, PART), 0)


def split3(x):
    a = x.astype(bf16).astype(f32)
    b = (x - a).astype(bf16).astype(f32)
    return a, b, x - a - b


def left_parts(x):
    a, b, c = split3(x)
    return [a, a, b, b, a, c]


def right_parts(x):
    a, b, c = split3(x)
    return [a, b, a, b, c, a]


def stack16(parts):
    return jnp.concatenate(parts, axis=0).astype(bf16)


def basis(rows):
    row = sublane()
    place = jnp.where(row < 3, 2.0 * rows - 1.0, rows)
    first = place[0:3]
    norm = jnp.sum(first * first, axis=0, keepdims=True)
    cross = jnp.sum(first * place[3:6], axis=0, keepdims=True)
    full = jnp.where(row < 6, place, jnp.where(row == 6, cross, 1.0))
    return full, norm, cross


def right_distance(full, norm):
    row = sublane()
    return jnp.where(
        row < 3, full, jnp.where(row == 3, norm, jnp.where(row == 4, 1.0, 0.0))
    )


def left_distance(full, norm):
    row = sublane()
    return jnp.where(
        row < 3, -2.0 * full, jnp.where(row == 3, 1.0, jnp.where(row == 4, norm, 0.0))
    )


def left_approach(full, cross):
    return 4.0 * jnp.concatenate(
        [-full[3:6], -full[0:3], jnp.ones((1, PART), f32), cross], axis=0
    )


def columns(parts):
    fill = 128 - 8 * len(parts)
    return jnp.concatenate(parts + [jnp.zeros((fill, PART), f32)], axis=0).T


def halves(w):
    hi = w.astype(bf16)
    return hi, (w - hi.astype(f32)).astype(bf16)


def request_kernel(dest, target, req, slot, used):
    req[...] = jnp.full_like(req, -1)

    def clear(d, _):
        used[d] = 0
        return 0

    lax.fori_loop(0, req.shape[0], clear, 0, unroll=8)
    short = lax.broadcasted_iota(i32, (1, 128), 1)

    def entry(e, _):
        d = dest[e]
        k = used[d]
        used[d] = k + 1
        slot[e] = d * CAP + k
        req[d] = jnp.where(short == k, target[e], req[d])
        return 0

    lax.fori_loop(0, SEND, entry, 0, unroll=4)


def respond_kernel(state, goals, out):
    def one(s, _):
        goal = jnp.maximum(goals[s], 0)
        out[s] = state[goal]
        return 0

    lax.fori_loop(0, out.shape[0], one, 0, unroll=16)


def by_rows(need, step):
    low = 0
    for rows in ROWS:
        pl.when((need > low) & (need <= rows))(lambda rows=rows: step(rows))
        low = rows


def pipeline(count, rows_of, prepare, load, work, combine=None, store=None):
    last = count - 1

    def clamp(p):
        return jnp.minimum(p, last)

    for k in range(2 * WIDE):
        prepare(clamp(k))
    for k in range(WIDE):
        load(clamp(k), k)

    def body(t, _):
        p = WIDE * t
        need = rows_of(p)
        for k in range(1, WIDE):
            need = jnp.maximum(need, rows_of(p + k))

        def step(rows):
            before = jnp.maximum(p - 1, 0)
            done = []
            if combine is not None:
                done.append((before, combine(before, WIDE - 1), t > 0))
            for k in range(WIDE):
                work(p + k, k, rows)
                load(clamp(p + WIDE + k), k)
                if combine is not None and k < WIDE - 1:
                    done.append((p + k, combine(p + k, k), True))
            for item in done:
                store(*item)
            for k in range(WIDE):
                prepare(clamp(p + 2 * WIDE + k))

        by_rows(need, step)
        return 0

    lax.fori_loop(0, count // WIDE, body, 0)
    if combine is not None:
        store(last, combine(last, WIDE - 1), True)


def keep_sums(acc1, acc2, a, s, sums, valid):
    if valid is not True:
        keep = jnp.where(valid, 1.0, 0.0)
        sums = (sums[0] * keep, sums[1] * keep)
    acc1[a] += sums[0]
    acc2[s] += sums[1]


def pack_plan(far, slot, proxy_cell, order, offset, block_own, live, filled):
    def clear(c, _):
        filled[c] = 0
        return 0

    lax.fori_loop(0, CELLS, clear, 0)

    def measure(e, _):
        mass = far[slot[e]][7:8]
        n = jnp.sum(jnp.where(mass > 0.0, 1.0, 0.0)).astype(i32)
        live[e] = n
        a = proxy_cell[e]
        offset[e] = filled[a]
        filled[a] = filled[a] + n
        return 0

    lax.fori_loop(0, SEND, measure, 0, unroll=16)

    def place(k, total):
        c = order[k]
        blocks = (filled[c] + PART - 1) // PART
        filled[c] = total * PART

        def name(t, _):
            block_own[total + t] = c
            return 0

        lax.fori_loop(0, blocks, name, 0)
        return total + blocks

    total = lax.fori_loop(0, CELLS, place, 0)

    def shift(e, _):
        offset[e] = offset[e] + filled[proxy_cell[e]]
        return 0

    lax.fori_loop(0, SEND, shift, 0, unroll=8)
    for k in range(WIDE - 1):
        block_own[jnp.minimum(total + k, BLOCKS - 1)] = block_own[total - 1]
    return (total + WIDE - 1) // WIDE * WIDE


def pack(target, rows, offset, n):
    t = offset // PART
    lane0 = offset - t * PART
    lane = lax.broadcasted_iota(i32, rows.shape, 1)
    turned = pltpu.roll(rows, lane0, 1)
    pltpu.store(target.at[t], turned, mask=(lane >= lane0) & (lane < lane0 + n))
    pltpu.store(target.at[t + 1], turned, mask=lane < lane0 + n - PART)


def unpack(source, offset):
    t = offset // PART
    lane0 = offset - t * PART
    first, second = source[t], source[t + 1]
    lane = lax.broadcasted_iota(i32, first.shape, 1)
    return pltpu.roll(jnp.where(lane >= lane0, first, second), lax.rem(PART - lane0, PART), 1)


def own_lists(pair_first, pair_offset, pa, po, ps, dummy):
    def one(e, _):
        pa[e] = e
        po[e] = e
        ps[e] = dummy
        a = pair_first[e]
        b = lax.rem(a + pair_offset[e], CELLS)
        pa[CELLS + e] = a
        po[CELLS + e] = b
        ps[CELLS + e] = b
        return 0

    lax.fori_loop(0, CELLS, one, 0)


def nn(a, b):
    return jnp.dot(a, b, preferred_element_type=f32)


def nt(a, b):
    return lax.dot_general(a, b, (((1,), (1,)), ((), ())), preferred_element_type=f32)


def density_weights(r2, total_h):
    inv = pltpu.reciprocal(total_h, approx=True)
    inv2 = inv * inv
    q2 = jnp.maximum(r2, TINY) * inv2
    q = q2 * lax.rsqrt(q2)
    u = 2.0 - q
    t = jnp.maximum(u, 0.0)
    return jnp.minimum(t * t * t, 4.0 - 3.0 * (q2 * u)) * (inv2 * inv)


def two_wide(col, row):
    return jnp.concatenate([col, col], axis=1) + row


def density_pairs(count, counts, pa, po, ps, refs, prepare, acc1, acc2):
    bf, hj, mj, cols, bh, bm, dist = refs

    def load(p, side):
        dist[side][...] = nn(cols[pa(p)], bf[lax.rem(po(p), bf.shape[0])])

    def work(p, side, rows):
        a, o = pa(p), po(p)
        h_j, m_j = hj[o], mj[o]
        second = jnp.zeros((8, PART), f32)
        for c in range(0, rows, CHUNK):
            w = density_weights(
                dist[side][c : c + CHUNK, :], two_wide(bh[a, c : c + CHUNK, :], h_j)
            )
            first = w * m_j
            acc1[a, c : c + CHUNK, :] += first[:, 0:128] + first[:, 128:256]
            m_i = bm[a, c : c + CHUNK, :]
            other = w * jnp.concatenate([m_i, m_i], axis=1)
            second += jnp.sum(other.reshape(CHUNK // 8, 8, PART), axis=0)
        acc2[ps(p)] += jnp.sum(second, axis=0, keepdims=True)

    pipeline(count, lambda p: counts[pa(p)], prepare, load, work)


def column_sums(x):
    return jnp.sum(x.T, axis=0, keepdims=True)


def spreader(lanes):
    row = lax.broadcasted_iota(i32, (128, 128 * len(lanes)), 0)
    block = lax.broadcasted_iota(i32, (128, 128 * len(lanes)), 1) // 128
    hit = row < 0
    for n, k in enumerate(lanes):
        hit |= (block == n) & ((row == k) | (row == k + 8) | (row == k + 16))
    return jnp.where(hit, 1.0, 0.0).astype(bf16)


def expand(cols, bh, bm=None):
    matrix = spreader((102,) if bm is None else (102, 103))

    def one(c, _):
        wide = nn(cols[c], matrix)
        bh[c] = wide[:, 0:128]
        if bm is not None:
            bm[c] = wide[:, 128:256]
        return 0

    lax.fori_loop(0, CELLS, one, 0, unroll=4)


def put_right(ref, o, start, parts):
    ref[lax.rem(o, ref.shape[0]), start : start + 48, :] = stack16(right_parts(parts))


def density_prepare(o, rows, bf, hj, mj):
    full, norm, cross = basis(rows)
    put_right(bf, o, 0, right_distance(full, norm))
    hj[o] = rows[6:7]
    mj[o] = rows[7:8]
    return full, norm, cross


def state_kernel(pos, vel, mass, smooth, counts, state, cols):
    lane = lax.broadcasted_iota(i32, (1, PART), 1)

    def mine(c, _):
        one = pl.ds(c, 1)
        live = jnp.where(lane < counts[c], mass[one, :], 0.0)
        rows = jnp.concatenate(
            [pos[k, one, :] for k in range(3)]
            + [vel[k, one, :] for k in range(3)]
            + [smooth[one, :], live],
            axis=0,
        )
        state[c] = rows
        full, norm, cross = basis(rows)
        cols[c] = columns(
            left_parts(left_distance(full, norm))
            + left_parts(left_approach(full, cross))
            + list(split3(rows))
        ).astype(bf16)
        return 0

    lax.fori_loop(0, CELLS, mine, 0, unroll=4)


def own_density_kernel(
    after, state, cols, counts, pair_first, pair_offset, near, order,
    acc1, acc2, bh, bm, bf, hj, mj, pa, po, ps, *dist,
):
    del after

    def rank(c, _):
        mine = counts[c]

        def ahead(d, n):
            other = counts[d]
            return n + jnp.where((other > mine) | ((other == mine) & (d < c)), 1, 0)

        order[lax.fori_loop(0, CELLS, ahead, 0, unroll=8)] = c
        return 0

    lax.fori_loop(0, CELLS, rank, 0)
    expand(cols, bh, bm)
    bf[...] = jnp.zeros_like(bf)

    def mine(c, _):
        density_prepare(c, state[c], bf, hj, mj)
        return 0

    lax.fori_loop(0, CELLS, mine, 0, unroll=2)
    own_lists(pair_first, pair_offset, pa, po, ps, CELLS)
    acc1[...] = jnp.zeros_like(acc1)
    acc2[...] = jnp.zeros_like(acc2)
    refs = (bf, hj, mj, cols, bh, bm, dist)
    density_pairs(
        CELLS + PAIRS, counts, lambda p: pa[p], lambda p: po[p], lambda p: ps[p], refs,
        lambda p: None, acc1, acc2,
    )

    def total(c, _):
        near[c] = column_sums(acc1[c]) + acc2[c]
        return 0

    lax.fori_loop(0, CELLS, total, 0, unroll=2)


def far_density_kernel(
    near, far, counts, slot, proxy_cell, order, cols,
    acc1, ret, blocks, offset, block_own, live, size,
    acc2, bh, bm, bf, hj, mj, filled, *dist,
):
    del near
    total = pack_plan(far, slot, proxy_cell, order, offset, block_own, live, filled)
    size[0] = total
    expand(cols, bh, bm)
    bf[...] = jnp.zeros_like(bf)
    blocks[...] = jnp.zeros_like(blocks)

    def fill(e, _):
        pack(blocks, far[slot[e]], offset[e], live[e])
        return 0

    lax.fori_loop(0, SEND, fill, 0, unroll=8)
    acc2[...] = jnp.zeros_like(acc2)
    acc1[...] = jnp.zeros_like(acc1)
    refs = (bf, hj, mj, cols, bh, bm, dist)
    same = lambda p: p
    density_pairs(
        total, counts, lambda p: block_own[p], same, same, refs,
        lambda p: density_prepare(p, blocks[p], bf, hj, mj), acc1, acc2,
    )

    def back(e, _):
        ret[slot[e]] = unpack(acc2, offset[e])
        return 0

    lax.fori_loop(0, SEND, back, 0, unroll=8)


def add_by_goal(back, goals, sums):
    for part in sums:
        part[...] = jnp.zeros_like(part)

    def one(t, _):
        for k, part in enumerate(sums):
            s = t * len(sums) + k
            goal = goals[s]
            part[jnp.where(goal < 0, CELLS, goal)] += back[s]
        return 0

    lax.fori_loop(0, back.shape[0] // len(sums), one, 0, unroll=8)


def combine_density_kernel(
    back, goals, near, far, energy, counts, density, fluid, answer, *sums
):
    add_by_goal(back, goals, sums)
    lane = lax.broadcasted_iota(i32, (1, PART), 1)

    def cell(c, _):
        raw = W_SCALE * (near[c] + far[c] + sum(part[c] for part in sums))
        here = lane < counts[c]
        density[pl.ds(c, 1), :] = jnp.where(here, raw, 0.0)
        fluid[c] = jnp.concatenate(
            [jnp.where(here, raw, 1.0), energy[pl.ds(c, 1), :]], axis=0
        )
        return 0

    lax.fori_loop(0, CELLS, cell, 0, unroll=4)

    def send(s, _):
        answer[s] = fluid[jnp.maximum(goals[s], 0)]
        return 0

    lax.fori_loop(0, answer.shape[0], send, 0, unroll=8)


def slope_weights(r2, s, total_h):
    inv = pltpu.reciprocal(total_h, approx=True)
    inv2 = inv * inv
    q2 = jnp.maximum(r2, TINY) * inv2
    rs = lax.rsqrt(q2)
    q = q2 * rs
    u = 2.0 - q
    t = jnp.maximum(u, 0.0)
    grad = jnp.where(q < 1.0, 3.0 * u - 2.0, t * t * rs)
    m = jnp.minimum(s, 0.0) * (inv * pltpu.reciprocal(q2 + 0.01, approx=True))
    return grad * (inv2 * inv2 * inv), m


def fluid_weights(grad, m, total_c, total_p, total_r):
    return (total_p + m * (m - total_c) * pltpu.reciprocal(total_r, approx=True)) * grad


def force_fluid(fluid):
    rho, u = fluid[0:1], fluid[1:2]
    pressure = (GAMMA - 1.0) * u / rho
    sound = jnp.sqrt(GAMMA * (GAMMA - 1.0) * u)
    return pressure, sound, 4.0 * rho


def put_halves(ws, c, w):
    hi, lo = halves(w)
    ws[c : c + CHUNK, :] = hi
    ws[PART + c : PART + c + CHUNK, :] = lo


def fluid_work(ws, col, side_row, a, rows, grads):
    for c in range(0, rows, CHUNK):
        grad, m = grads(c)
        total = [
            two_wide(col[a, k, c : c + CHUNK, :], side_row[k + 1 : k + 2]) for k in range(3)
        ]
        put_halves(ws, c, fluid_weights(grad, m, *total))


def fold(x):
    return x[0:8] + x[8:16] + x[16:24]


def force_combine(own, other, ws):
    second = fold(nn(jnp.concatenate([own, own], axis=1), ws[...]))
    first = fold(nt(other, ws[...]))
    return first[:, 0:PART] + first[:, PART:], second


def full_force(count, counts, pa, po, refs, prepare, store):
    bd, bs, own_cf, other_cf, cols, bh, row, col, dist, appr, ws = refs

    def load(p, side):
        a, o = pa(p), lax.rem(po(p), bd.shape[0])
        dist[side][...] = nn(cols[a], bd[o])
        appr[side][...] = nn(cols[a], bs[o])

    def work(p, side, rows):
        a = pa(p)
        side_row = row[po(p)]

        def grads(c):
            return slope_weights(
                dist[side][c : c + CHUNK, :],
                appr[side][c : c + CHUNK, :],
                two_wide(bh[a, c : c + CHUNK, :], side_row[0:1]),
            )

        fluid_work(ws[side], col, side_row, a, rows, grads)

    def combine(p, side):
        return force_combine(own_cf[pa(p)], other_cf[po(p)], ws[side])

    pipeline(count, lambda p: counts[pa(p)], prepare, load, work, combine, store)


def geometry_prepare(o, rows, bd, bs):
    full, norm, cross = basis(rows)
    put_right(bd, o, 0, right_distance(full, norm))
    put_right(bs, o, 48, full)
    return full


def fluid_prepare(o, rows, full, fluid, cf, row):
    cf[o] = stack16(list(split3(rows[7:8] * full)))
    pressure, sound, rho4 = force_fluid(fluid)
    row[o] = jnp.concatenate(
        [rows[6:7], sound, pressure, rho4, jnp.zeros((4, PART), f32)], axis=0
    )


def own_fluid_columns(c, row, col, matrix):
    wide = nn(columns(list(split3(row[c]))).astype(bf16), matrix)
    for k in range(3):
        col[c, k] = wide[:, 128 * k : 128 * (k + 1)]


def sums_kernel(acc1, out):
    def total(c, _):
        out[c] = column_sums(acc1[c])
        return 0

    lax.fori_loop(0, CELLS, total, 0, unroll=4)


def force_sums(rows, sums):
    full, _, cross = basis(rows)
    count = sums[7:8]
    accel = (-0.5 * K_SCALE) * (full[0:3] * count - sums[0:3])
    mixed = jnp.sum(full[3:6] * sums[0:3] + full[0:3] * sums[3:6], axis=0, keepdims=True)
    heat = (0.25 * K_SCALE) * (cross * count - mixed + sums[6:7])
    return jnp.concatenate([accel, heat], axis=0)


def fluid_kernel(state, fluid, cols, own_cf, own_row, col, bh):
    matrix = spreader((1, 2, 3))
    expand(cols, bh)

    def mine(c, _):
        rows = state[c]
        fluid_prepare(c, rows, basis(rows)[0], fluid[c], own_cf, own_row)
        own_fluid_columns(c, own_row, col, matrix)
        return 0

    lax.fori_loop(0, CELLS, mine, 0, unroll=4)


def own_force_kernel(
    after, state, counts, pair_first, pair_offset, cols, cf, row, col, bh, total,
    acc1, acc2, bd, bs, pa, po, ps, *wide,
):
    del after
    bd[...] = jnp.zeros_like(bd)
    bs[...] = jnp.zeros_like(bs)

    def mine(c, _):
        geometry_prepare(c, state[c], bd, bs)
        return 0

    lax.fori_loop(0, CELLS, mine, 0, unroll=4)
    own_lists(pair_first, pair_offset, pa, po, ps, CELLS)
    acc1[...] = jnp.zeros_like(acc1)
    acc2[...] = jnp.zeros_like(acc2)
    dist, appr, ws = wide[:WIDE], wide[WIDE : 2 * WIDE], wide[2 * WIDE :]
    for part in ws:
        part[...] = jnp.zeros_like(part)
    refs = (bd, bs, cf, cf, cols, bh, row, col, dist, appr, ws)
    full_force(
        CELLS + PAIRS, counts, lambda p: pa[p], lambda p: po[p], refs, lambda p: None,
        lambda p, sums, valid: keep_sums(acc1, acc2, pa[p], ps[p], sums, valid),
    )
    total[...] = acc1[...] + acc2[0:CELLS]


def far_force_kernel(
    blocks, far_fluid, counts, slot, offset, block_own, live, size, cols, own_cf, col_far, bh_far,
    acc1, ret,
    acc2, fluids, bd, bs, cf, row, col, bh, sems, *wide,
):
    total = size[0]
    copies = [
        pltpu.make_async_copy(col_far, col, sems.at[0]),
        pltpu.make_async_copy(bh_far, bh, sems.at[1]),
    ]
    for copy in copies:
        copy.start()
    bd[...] = jnp.zeros_like(bd)
    bs[...] = jnp.zeros_like(bs)
    fluids[...] = jnp.ones_like(fluids)

    def fill(e, _):
        pack(fluids, far_fluid[slot[e]], offset[e], live[e])
        return 0

    lax.fori_loop(0, SEND, fill, 0, unroll=8)
    acc1[...] = jnp.zeros_like(acc1)
    dist, appr, ws = wide[:WIDE], wide[WIDE : 2 * WIDE], wide[2 * WIDE :]
    for part in ws:
        part[...] = jnp.zeros_like(part)

    def prepare(p):
        rows = blocks[p]
        fluid_prepare(p, rows, geometry_prepare(p, rows, bd, bs), fluids[p], cf, row)

    def store(p, sums, valid):
        first, second = sums
        if valid is not True:
            first = first * jnp.where(valid, 1.0, 0.0)
        acc1[block_own[p]] += first
        acc2[p] = force_sums(blocks[p], second)

    refs = (
        bd, bs, own_cf, cf, cols, bh, row, col, dist, appr, ws,
    )
    for copy in copies:
        copy.wait()
    same = lambda p: p
    full_force(total, counts, lambda p: block_own[p], same, refs, prepare, store)

    def back(e, _):
        ret[slot[e]] = unpack(acc2, offset[e])
        return 0

    lax.fori_loop(0, SEND, back, 0, unroll=8)


def finish_kernel(
    back, goals, near, far, state, energy, counts, mig_cell, mig_dest, accel, leave, moved, used, *sums
):
    add_by_goal(back, goals, sums)
    lane = lax.broadcasted_iota(i32, (1, PART), 1)

    def cell(c, _):
        rows = state[c]
        here = lane < counts[c]
        total = jnp.where(
            here, force_sums(rows, near[c] + far[c]) + sum(part[c] for part in sums), 0.0
        )
        accel[c] = total
        new_vel = rows[3:6] + STEP * total[0:3]
        new_pos = rows[0:3] + STEP * new_vel
        new_energy = energy[pl.ds(c, 1), :] + STEP * total[3:4]
        kicked = jnp.concatenate(
            [new_pos, new_vel, rows[7:8], rows[6:7], new_energy], axis=0
        )
        moved[c] = jnp.where(here, kicked, 0.0)
        return 0

    lax.fori_loop(0, CELLS, cell, 0)
    leave[...] = jnp.zeros_like(leave)

    def clear(d, _):
        used[d] = 0
        return 0

    lax.fori_loop(0, leave.shape[0], clear, 0)

    def entry(e, _):
        d = mig_dest[e]
        k = used[d]
        used[d] = k + 1
        full = moved[mig_cell[e]]
        for r in range(9):
            leave[d, r, pl.ds(k, 1), :] = full[r : r + 1]
        return 0

    lax.fori_loop(0, mig_cell.shape[0], entry, 0)


def inbox_kernel(came, out):
    for d in range(came.shape[0]):
        for r in range(came.shape[1]):
            out[r, d * CAPM : (d + 1) * CAPM, :] = came[d, r]


def vmem(*dims, dtype=f32):
    return pltpu.VMEM(dims, dtype)


def smem(*dims):
    return pltpu.SMEM(dims, i32)


WS = [vmem(2 * PART, PART, dtype=bf16)] * WIDE
SQUARE = [vmem(PART, PART)] * WIDE


def cell_state(position, velocity, mass, smoothing, counts):
    return kernel_call(
        state_kernel,
        (shape(CELLS, 8, PART), shape(CELLS, PART, 128, dtype=bf16)),
        [VMEM] * 4 + [SMEM],
        (VMEM, VMEM),
        flops=2**20,
        moved=2**22,
    )(position, velocity, mass, smoothing, counts)


def own_density(after, state, cols, counts, pair_first, pair_offset):
    return kernel_call(
        own_density_kernel,
        (shape(CELLS, 1, PART), shape(CELLS, dtype=i32)),
        [ANY] + [VMEM] * 2 + [SMEM] * 3,
        (VMEM, SMEM),
        [
            vmem(CELLS, PART, 128),
            vmem(CELLS + 1, 1, PART),
            vmem(CELLS, PART, 128),
            vmem(CELLS, PART, 128),
            vmem(CELLS, 128, PART, dtype=bf16),
            vmem(CELLS, 1, PART),
            vmem(CELLS, 1, PART),
        ]
        + [smem(CELLS + PAIRS)] * 3
        + SQUARE,
        flops=32 * PART * PART * 300,
        moved=2**20,
    )(after, state, cols, counts, pair_first, pair_offset)


def far_density(near, far, counts, slot, proxy_cell, order, cols):
    return kernel_call(
        far_density_kernel,
        (
            shape(CELLS, PART, 128),
            shape(far.shape[0], 1, PART),
            shape(BLOCKS + 1, 8, PART),
            shape(SEND, dtype=i32),
            shape(BLOCKS, dtype=i32),
            shape(SEND, dtype=i32),
            shape(1, dtype=i32),
        ),
        [ANY, VMEM] + [SMEM] * 4 + [VMEM],
        (VMEM,) * 3 + (SMEM,) * 4,
        [
            vmem(BLOCKS + 1, 1, PART),
            vmem(CELLS, PART, 128),
            vmem(CELLS, PART, 128),
            vmem(RING, 128, PART, dtype=bf16),
            vmem(BLOCKS, 1, PART),
            vmem(BLOCKS, 1, PART),
        ]
        + [smem(CELLS)]
        + SQUARE,
        flops=128 * PART * PART * 300,
        moved=2**20,
    )(near, far, counts, slot, proxy_cell, order, cols)


def own_fluid(state, fluid, cols):
    return kernel_call(
        fluid_kernel,
        (
            shape(CELLS, 24, PART, dtype=bf16),
            shape(CELLS, 8, PART),
            shape(CELLS, 3, PART, 128),
            shape(CELLS, PART, 128),
        ),
        [VMEM] * 3,
        (VMEM,) * 4,
        flops=2**22,
        moved=2**24,
    )(state, fluid, cols)


def far_force(
    far_fluid, counts, slot, blocks, offset, block_own, live, size, cols, own_cf, col, bh
):
    return kernel_call(
        far_force_kernel,
        (shape(CELLS, 8, PART), shape(far_fluid.shape[0], 4, PART)),
        [VMEM] * 2 + [SMEM] * 6 + [VMEM] * 2 + [ANY] * 2,
        (VMEM, VMEM),
        [
            vmem(BLOCKS + 1, 4, PART),
            vmem(BLOCKS + 1, 2, PART),
            vmem(RING, 128, PART, dtype=bf16),
            vmem(RING, 128, PART, dtype=bf16),
            vmem(BLOCKS, 24, PART, dtype=bf16),
            vmem(BLOCKS, 8, PART),
            vmem(CELLS, 3, PART, 128),
            vmem(CELLS, PART, 128),
            pltpu.SemaphoreType.DMA((2,)),
        ]
        + SQUARE * 2
        + WS,
        flops=128 * PART * PART * 600,
        moved=2**20,
    )(blocks, far_fluid, counts, slot, offset, block_own, live, size, cols, own_cf, col, bh)


def own_force(after, state, counts, pair_first, pair_offset, cols, cf, row, col, bh):
    return kernel_call(
        own_force_kernel,
        shape(CELLS, 8, PART),
        [ANY, VMEM] + [SMEM] * 3 + [VMEM] * 5,
        VMEM,
        [
            vmem(CELLS, 8, PART),
            vmem(CELLS + 1, 8, PART),
            vmem(CELLS, 128, PART, dtype=bf16),
            vmem(CELLS, 128, PART, dtype=bf16),
        ]
        + [smem(CELLS + PAIRS)] * 3
        + SQUARE * 2
        + WS,
        flops=32 * PART * PART * 600,
        moved=2**20,
    )(after, state, counts, pair_first, pair_offset, cols, cf, row, col, bh)


def exchange(x, axes):
    return lax.all_to_all(x, axes, split_axis=0, concat_axis=0, tiled=True)


def local(
    position, velocity, mass, smoothing, energy, counts, proxy_cell, proxy_dest,
    proxy_target, pair_first, pair_offset, mig_cell, mig_dest,
):
    devices = lax.axis_size(("rows", "cols"))
    col_count = lax.axis_size("cols")
    slots = devices * CAP
    both = ("rows", "cols")
    req, slot = kernel_call(
        request_kernel,
        (shape(devices, 1, 128, dtype=i32), shape(SEND, dtype=i32)),
        [SMEM] * 2,
        (VMEM, SMEM),
        [smem(devices)],
        moved=2**20,
    )(proxy_dest[:, 0], proxy_target)
    goals = exchange(req, both)[:, 0, 0:CAP].reshape(slots)
    state, cols = cell_state(
        position.transpose(1, 0, 2), velocity.transpose(1, 0, 2), mass, smoothing, counts
    )
    answer = kernel_call(
        respond_kernel, shape(slots, 8, PART), [VMEM, SMEM], VMEM, moved=4 * 2**20
    )(state, goals)
    far = exchange(answer, both)
    near, order = own_density(answer, state, cols, counts, pair_first, pair_offset)
    acc1, ret, *plan = far_density(near, far, counts, slot, proxy_cell, order, cols)
    far_sums = kernel_call(
        sums_kernel, shape(CELLS, 1, PART), [VMEM], VMEM, flops=2**20, moved=2**21
    )(acc1)
    back = exchange(ret, both)
    density, fluid, answer2 = kernel_call(
        combine_density_kernel,
        (shape(CELLS, PART), shape(CELLS, 2, PART), shape(slots, 2, PART)),
        [VMEM, SMEM] + [VMEM] * 3 + [SMEM],
        (VMEM, VMEM, VMEM),
        [vmem(CELLS + 1, 1, PART)] * 4,
        moved=2**20,
    )(back, goals, near, far_sums, energy, counts)
    far_fluid = exchange(answer2, both)
    own_cf, own_row, col, bh = own_fluid(state, fluid, cols)
    far_force_sums, ret4 = far_force(far_fluid, counts, slot, *plan, cols, own_cf, col, bh)
    near_force = own_force(
        far_force_sums, state, counts, pair_first, pair_offset, cols, own_cf, own_row, col, bh
    )
    back4 = exchange(ret4, both)
    accel, leave = kernel_call(
        finish_kernel,
        (shape(CELLS, 4, PART), shape(col_count, 9, CAPM, PART)),
        [VMEM, SMEM] + [VMEM] * 4 + [SMEM] * 3,
        (VMEM, VMEM),
        [vmem(CELLS, 9, PART), smem(col_count)] + [vmem(CELLS + 1, 4, PART)] * 4,
        moved=2**20,
    )(
        back4, goals, near_force, far_force_sums, state, energy, counts, mig_cell,
        mig_dest[:, 0],
    )
    arrived = kernel_call(
        inbox_kernel, shape(9, col_count * CAPM, PART), [VMEM], VMEM, moved=2**20
    )(exchange(leave, "cols"))
    return (density, accel, arrived.transpose(1, 0, 2))


def solution(mesh):
    lead = ("rows", "cols")
    one, two, three = P(lead), P(lead, None), P(lead, None, None)
    return jax.shard_map(
        local,
        mesh=mesh,
        in_specs=(three, three, two, two, two, one, one, two, one, one, one, one, two),
        out_specs=(two, three, three),
        check_vma=False,
    )
```
